32 devices in a mesh: seq: 8 (over z, y), fsdp: 4 (over x, core).
Axes of the slice: x: 2, y: 2, z: 4, core: 2. Of those that a mesh axis runs over, the one named last changes fastest.
Arguments:
- tokens: bfloat16 [4, 2048, 1024], P('fsdp', 'seq'), may hold values from -6 to 6
- cotangent: bfloat16 [4, 2048, 1024], P('fsdp', 'seq'), may hold values from -6 to 6
- lengths: int32 [4, 3], P('fsdp'), may hold values from 300 to 1024, as said below
- block_perm: int32 [4, 16], P('fsdp'), may hold values from 0 to 15, as said below
- attn_gain: bfloat16 [2, 1024], P(None, 'fsdp'), may hold values from 0.5 to 1.5
- qkv_weight: bfloat16 [2, 1024, 3072], P(None, 'fsdp'), may hold values from -0.1875 to 0.1875
- proj_weight: bfloat16 [2, 1024, 1024], P(None, 'fsdp'), may hold values from -1.5 to 1.5
- mlp_gain: bfloat16 [2, 1024], P(None, 'fsdp'), may hold values from 0.5 to 1.5
- wide_weight: bfloat16 [2, 1024, 5248], P(None, 'fsdp'), may hold values from -0.1875 to 0.1875
- narrow_weight: bfloat16 [2, 1024, 2624], P(None, 'fsdp'), may hold values from -0.125 to 0.125
Outputs:
- block_out: bfloat16 [4, 2048, 1024], P('fsdp', 'seq')
- token_grad: bfloat16 [4, 2048, 1024], P('fsdp', 'seq')
- attn_gain_grad: float32 [2, 1024], P(None, ('seq', 'fsdp'))
- qkv_grad: float32 [2, 1024, 3072], P(None, ('seq', 'fsdp'))
- proj_grad: float32 [2, 1024, 1024], P(None, ('seq', 'fsdp'))
- mlp_gain_grad: float32 [2, 1024], P(None, ('seq', 'fsdp'))
- wide_grad: float32 [2, 1024, 5248], P(None, ('seq', 'fsdp'))
- narrow_grad: float32 [2, 1024, 2624], P(None, ('seq', 'fsdp'))
The draws below stay inside these ranges and needn't reach their ends.
Inputs may be any that keep to these rules, and one draw needn't show every extreme that they name: Sequence s of a batch takes ceil(lengths / 128) blocks, and the blocks of a batch add up to 16; every sequence but the last ends inside the 2 blocks of one index of seq, never at their end. `block_perm`: each row is a permutation. The 2 blocks that one index of seq holds in the given order go together to one index of seq; that map of indices is a composition, for bit = 0, 1, 2 and so on in turn, of swaps of some pairs of indices that differ in that bit only.
All inputs are finite; a program needn't handle non-finite values.
Results may differ from the reference program's by a relative error of at most 0.028.
Values may be sent and summed in bfloat16 or wider, within the bound.
No kernel may reach another device: no remote copies, remote signals or barrier semaphores. Data moves between devices by JAX's collectives and lax.ppermute only.
A program may use at most 448 MiB of HBM per device.

```python
import math
import jax
import jax.numpy as jnp
from jax import lax

D = 1024
HEADS = 16
HEAD_DIM = 64
FF = 2624
WINDOW = 128
BLOCK = 128
BLK_DEV = 2
LAYERS = 2
GROUPS = 4
NBLK = 16
GROUP_TOK = 2048
NSEQ = 3


def sequence_lengths(key):
    seq_count = NBLK // BLK_DEV
    most = min(16, seq_count - 2 * NSEQ + 2)
    pick_key, fill_key, tail_key = jax.random.split(key, 3)
    chosen = jax.random.randint(pick_key, (), 1, NSEQ - 1)
    slots = jnp.arange(NSEQ, dtype=jnp.int32)
    counts = jnp.where(slots == chosen, most, 2).astype(jnp.int32)
    extra = seq_count - 2 * (NSEQ - 1) - most

    def add_one(step, current):
        score = jax.random.randint(jax.random.fold_in(fill_key, step), (NSEQ,), 0, 1 << 20)
        open_slot = (slots != 0) & (slots != chosen) & (current < 15)
        picked = jnp.argmax(jnp.where(open_slot, score, -1))
        return current + (slots == picked).astype(jnp.int32)
    counts = lax.fori_loop(0, extra, add_one, counts)
    blocks = 2 * counts + jnp.where(slots == 0, -1, 0) + jnp.where(slots == NSEQ - 1, 1, 0)
    tails = jax.random.randint(tail_key, (NSEQ,), 1, BLOCK + 1)
    tails = jnp.where(slots == chosen, BLOCK, jnp.where(slots == 0, 11 * BLOCK // 32, tails))
    return ((blocks - 1) * BLOCK + tails).astype(jnp.int32)


def draw_lengths(key, part):
    key = jax.random.fold_in(key, 5)
    return jax.vmap(sequence_lengths)(jax.random.split(key, GROUPS))


def block_order(key):
    seq_count = NBLK // BLK_DEV
    levels = seq_count.bit_length() - 1
    switch_key, flip_key = jax.random.split(key)
    switches = jax.random.randint(switch_key, (levels, seq_count // 2), 0, 2)
    place = jnp.arange(seq_count, dtype=jnp.int32)
    for bit_level in range(levels):
        lower = jnp.bitwise_and(place, (1 << bit_level) - 1)
        pair = jnp.right_shift(place, bit_level + 1) * (1 << bit_level) + lower
        place = jnp.bitwise_xor(place, switches[bit_level][pair] * (1 << bit_level))
    flips = jax.random.randint(flip_key, (seq_count,), 0, 2)
    owner = jnp.arange(NBLK, dtype=jnp.int32) // 2
    within = jnp.arange(NBLK, dtype=jnp.int32) % 2
    return (2 * place[owner] + jnp.bitwise_xor(within, flips[owner])).astype(jnp.int32)


def draw_block_perm(key, part):
    key = jax.random.fold_in(key, 23)
    return jax.vmap(block_order)(jax.random.split(key, GROUPS))


def spiked(drawn, stream_key, source, target, blocks, factor):
    def block_of(dim):
        return (jnp.arange(drawn.shape[dim]) // (drawn.shape[dim] // blocks)).reshape((-1,) + (1,) * (drawn.ndim - 1 - dim))

    first = jax.random.permutation(stream_key, blocks)[block_of(target)]
    far = (block_of(target) + blocks // 2) % blocks
    return jnp.where((block_of(source) == first) | (block_of(source) == far), factor * drawn, drawn)


def block_levels(own_key, dims, cuts, low, high):
    loudness = 1.0
    for dim, parts in cuts:
        draws = jax.random.uniform(jax.random.fold_in(jax.random.fold_in(own_key, 6), dim), (parts,), jnp.float32, low / len(cuts), high / len(cuts))
        loudness = loudness * jnp.repeat(jnp.exp(draws), dims[dim] // parts).reshape((-1,) + (1,) * (len(dims) - 1 - dim))
    return loudness


def normal_values(rng, shape, scale, most, cuts=(), kind=jnp.bfloat16):
    values = scale * jax.random.normal(rng, shape, jnp.float32)
    if cuts:
        values = values * block_levels(rng, shape, cuts, -0.22, 0.18)
    return jnp.clip(values, -most, most).astype(kind)


def gaussian_with(stream_key, extent, deviation, reach, cuts, heavy, kind=jnp.bfloat16):
    array = deviation * jax.random.normal(stream_key, extent, jnp.float32)
    if cuts:
        array = array * block_levels(stream_key, extent, cuts, -0.22, 0.18)
    return jnp.clip(spiked(array, jax.random.fold_in(stream_key, 3), *heavy), -reach, reach).astype(kind)


def setup_inputs(seed: int = 0) -> dict:
    arg_keys = jax.random.split(jax.random.key(seed), 11)
    return {
        "tokens": normal_values(arg_keys[0], (GROUPS, GROUP_TOK, D), 1.0, 6.0, ((0, 4), (1, 8))),
        "cotangent": gaussian_with(arg_keys[1], (GROUPS, GROUP_TOK, D), 1.0, 6.0, ((0, 4), (1, 8)), (1, 2, 8, 2.0)),
        "lengths": draw_lengths(jax.random.fold_in(arg_keys[10], 71), 0),
        "block_perm": draw_block_perm(jax.random.fold_in(arg_keys[10], 71), 0),
        "attn_gain": jnp.clip(1.0 + 0.1 * jax.random.normal(arg_keys[4], (LAYERS, D), jnp.float32), 0.5, 1.5).astype(jnp.bfloat16),
        "qkv_weight": normal_values(arg_keys[5], (LAYERS, D, 3 * D), D ** -0.5, 0.1875, ((1, 4),)),
        "proj_weight": normal_values(arg_keys[6], (LAYERS, D, D), (D * 2 // WINDOW) ** -0.5, 1.5, ((1, 4),)),
        "mlp_gain": jnp.clip(1.0 + 0.1 * jax.random.normal(arg_keys[7], (LAYERS, D), jnp.float32), 0.5, 1.5).astype(jnp.bfloat16),
        "wide_weight": normal_values(arg_keys[8], (LAYERS, D, 2 * FF), D ** -0.5, 0.1875, ((1, 4),)),
        "narrow_weight": normal_values(arg_keys[9], (LAYERS, D, FF), FF ** -0.5, 0.125, ((1, 4),)),
    }


HIGH = lax.Precision.HIGHEST
NEG = -1e+30
EPS = 1e-05
THETA = 10000.0

@jax.custom_vjp
def low(v):
    return lax.optimization_barrier(v.astype(jnp.bfloat16)).astype(jnp.float32)

@jax.custom_vjp
def low_back(v):
    return v

def low_keep(v):
    return (low(v), None)

def low_pass(kept, grad):
    return (grad,)

def back_keep(v):
    return (v, None)

def back_low(kept, grad):
    return (low(grad),)
low.defvjp(low_keep, low_pass)
low_back.defvjp(back_keep, back_low)

def normalize(values, gain):
    average = lax.optimization_barrier(jnp.mean(values, axis=-1, keepdims=True))
    centred = values - average
    spread = lax.optimization_barrier(jnp.mean(centred * centred, axis=-1, keepdims=True))
    return centred * lax.rsqrt(spread + EPS) * gain

def rope_tables(position):
    inverse = jnp.power(THETA, -jnp.arange(0, HEAD_DIM, 2, dtype=jnp.float32) / HEAD_DIM)
    angles = position[:, None] * inverse[None, :]
    angles = jnp.concatenate([angles, angles], axis=-1)
    return (jnp.cos(angles)[:, None, :], jnp.sin(angles)[:, None, :])

def rotate(values, cosine, sine_tab):
    half = values.shape[-1] // 2
    turned = jnp.concatenate([-values[..., half:], values[..., :half]], axis=-1)
    return values * cosine + turned * sine_tab

def layout(positions, lengths, total):
    count = lengths.shape[0]
    blocks = (lengths + BLOCK - 1) // BLOCK
    first = ((jnp.cumsum(blocks) - blocks) * BLOCK).astype(jnp.int32)
    owner = (lax.optimization_barrier(jnp.sum((positions[:, None] >= first[None, :]).astype(jnp.int32), axis=1)) - 1).astype(jnp.int32)
    table = owner[:, None] == jnp.arange(count, dtype=jnp.int32)[None, :]
    start = lax.optimization_barrier(jnp.sum(jnp.where(table, first[None, :], 0), axis=1)).astype(jnp.int32)
    span = lax.optimization_barrier(jnp.sum(jnp.where(table, lengths[None, :], 0), axis=1)).astype(jnp.int32)
    local = positions - start
    inside = (positions >= 0) & (positions < total)
    valid = inside & (local < span)
    segment = jnp.where(inside, jnp.where(valid, owner, owner + count), -1).astype(jnp.int32)
    return (segment, local, valid)

def attend(queries, key_rows, value_rows, segment):
    total = queries.shape[0]
    halo_rows = WINDOW // 2
    q_block = min(512, total)
    span = q_block + 2 * halo_rows
    scale = 1.0 / math.sqrt(HEAD_DIM)
    key_pad = jnp.pad(key_rows, ((halo_rows, halo_rows), (0, 0), (0, 0)))
    value_pad = jnp.pad(value_rows, ((halo_rows, halo_rows), (0, 0), (0, 0)))
    seg_pad = jnp.pad(segment, (halo_rows, halo_rows), constant_values=-1)
    offset = jnp.arange(q_block, dtype=jnp.int32)[:, None] + halo_rows - jnp.arange(span, dtype=jnp.int32)[None, :]
    near = jnp.abs(offset) <= halo_rows

    def one_block(start):
        q_rows = lax.dynamic_slice_in_dim(queries, start, q_block, 0)
        k_rows = lax.dynamic_slice_in_dim(key_pad, start, span, 0)
        v_rows = lax.dynamic_slice_in_dim(value_pad, start, span, 0)
        seg_q = lax.dynamic_slice_in_dim(segment, start, q_block, 0)
        seg_k = lax.dynamic_slice_in_dim(seg_pad, start, span, 0)
        raw_scores = low_back(jnp.einsum('qhd,khd->hqk', q_rows, k_rows, precision=HIGH))
        allowed = near & (seg_q[:, None] == seg_k[None, :])
        scores = jnp.where(allowed[None], raw_scores * scale, NEG)
        top = lax.optimization_barrier(jnp.max(scores, axis=-1, keepdims=True))
        expo = jnp.exp(scores - top)
        probs = expo / lax.optimization_barrier(jnp.sum(expo, axis=-1, keepdims=True))
        return jnp.einsum('hqk,khd->qhd', low(probs), v_rows, precision=HIGH)
    starts = jnp.arange(total // q_block, dtype=jnp.int32) * q_block
    blocks = lax.map(jax.checkpoint(one_block), starts)
    return blocks.reshape(total, HEADS, HEAD_DIM)

def layer(residual, params, segment, cosine, sine_tab):
    gain_a, w_qkv, w_proj, gain_m, w_wide, w_narrow = params
    normed = low(normalize(residual, gain_a))
    projected = low_back(jnp.dot(normed, w_qkv, precision=HIGH))
    queries = low(rotate(projected[:, :D].reshape(-1, HEADS, HEAD_DIM), cosine, sine_tab))
    key_rows = low(rotate(projected[:, D:2 * D].reshape(-1, HEADS, HEAD_DIM), cosine, sine_tab))
    value_rows = low(projected[:, 2 * D:].reshape(-1, HEADS, HEAD_DIM))
    attended = attend(queries, key_rows, value_rows, segment).reshape(-1, D)
    attended = low(low_back(attended))
    middle = residual + low_back(jnp.dot(attended, w_proj, precision=HIGH))
    second = low(normalize(middle, gain_m))
    hidden = low_back(jnp.dot(second, w_wide, precision=HIGH))
    gated = low(jax.nn.gelu(hidden[:, :FF], approximate=False) * hidden[:, FF:])
    return middle + low_back(jnp.dot(gated, w_narrow.T, precision=HIGH))

def to_packed(rows, order_map):
    blocks = rows.reshape(NBLK, BLOCK, D)
    return jnp.zeros_like(blocks).at[order_map].set(blocks).reshape(NBLK * BLOCK, D)

def from_packed(rows, order_map):
    return rows.reshape(NBLK, BLOCK, D)[order_map].reshape(NBLK * BLOCK, D)

def reference(tokens, cotangent, lengths, block_perm, attn_gain, qkv_weight, proj_weight, mlp_gain, wide_weight, narrow_weight):
    weights = tuple((w.astype(jnp.float32) for w in (attn_gain, qkv_weight, proj_weight, mlp_gain, wide_weight, narrow_weight)))
    total = NBLK * BLOCK
    positions = jnp.arange(total, dtype=jnp.int32)

    def one_group(carry, item):
        tok_rows, cot_rows, lens, order_map = item
        packed_tok = to_packed(tok_rows, order_map)
        packed_cot = to_packed(cot_rows, order_map)
        segment, local, valid = layout(positions, lens, total)
        cosine, sine_tab = rope_tables(local.astype(jnp.float32))

        def run_layer(residual, params):
            return layer(residual, params, segment, cosine, sine_tab)

        def forward(residual, params):
            for layer_index in range(LAYERS):
                residual = jax.checkpoint(run_layer)(residual, tuple((p[layer_index] for p in params)))
            return residual
        result, pull = jax.vjp(forward, packed_tok.astype(jnp.float32), weights)
        seed_grad = packed_cot.astype(jnp.float32) * valid[:, None].astype(jnp.float32)
        input_grad, weight_grads = pull(seed_grad)
        carry = tuple((c + g for c, g in zip(carry, weight_grads)))
        return (carry, (from_packed(result.astype(jnp.bfloat16), order_map), from_packed(input_grad.astype(jnp.bfloat16), order_map)))
    start = tuple((jnp.zeros(w.shape, jnp.float32) for w in weights))
    grads, (block_out, token_grad) = lax.scan(one_group, start, (tokens, cotangent, lengths, block_perm))
    return (block_out, token_grad, grads[0], grads[1], grads[2], grads[3], grads[4], grads[5])
```

```python
import math

import jax
import jax.numpy as jnp
from jax import lax
from jax.sharding import PartitionSpec as P

HEADS = 16
HEAD_DIM = 64
FF = 2624
WINDOW = 128
BLOCK = 128
BLK_DEV = 2
LAYERS = 2


NEG = -1e30
EPS = 1e-05
THETA = 10000.0


def padded(shard, sides, width):
    for axis, dim in sides:
        devices, length = (lax.axis_size(axis), shard.shape[dim])
        up = [(i, (i + 1) % devices) for i in range(devices - 1)]
        down = [(j, i) for i, j in up]
        last = lax.slice_in_dim(shard, length - width, length, axis=dim)
        leading = lax.slice_in_dim(shard, 0, width, axis=dim)
        before = lax.ppermute(last, axis, up)
        after = lax.ppermute(leading, axis, down)
        shard = jnp.concatenate([before, shard, after], axis=dim)
    return shard


def partner(block, axis, bit):
    count = lax.axis_size(axis)
    route = []
    for low in range(count):
        high = low | 1 << bit
        if high != low and high < count:
            route += [(low, high), (high, low)]
    return lax.ppermute(block, axis, route)


AXES = ("seq", "fsdp")


def swap(value, bit):
    count = lax.axis_size("seq") * lax.axis_size("fsdp")
    return lax.ppermute(value, AXES, [(i, i ^ (1 << bit)) for i in range(count)])


def flat_index():
    return lax.axis_index("seq") * lax.axis_size("fsdp") + lax.axis_index("fsdp")


def gather_weight(shard):
    rows, cols = shard.shape
    half = rows // 2
    quarter = lax.axis_index("fsdp")
    side = lax.axis_index("seq") % 2
    sent = lax.dynamic_slice_in_dim(shard, side * half, half, 0)
    own_core = swap(shard, 0)
    far_x = swap(sent, 1)
    far_y = swap(far_x, 2)
    far_x_core = swap(far_x, 0)
    far_y_core = swap(far_y, 0)
    whole = jnp.zeros((4 * rows, cols), shard.dtype)
    whole = lax.dynamic_update_slice(whole, shard, (quarter * rows, 0))
    whole = lax.dynamic_update_slice(whole, own_core, ((quarter ^ 1) * rows, 0))
    whole = lax.dynamic_update_slice(whole, far_x, ((quarter ^ 2) * rows + side * half, 0))
    whole = lax.dynamic_update_slice(whole, far_y, ((quarter ^ 2) * rows + (1 - side) * half, 0))
    whole = lax.dynamic_update_slice(whole, far_x_core, ((quarter ^ 3) * rows + side * half, 0))
    whole = lax.dynamic_update_slice(
        whole, far_y_core, ((quarter ^ 3) * rows + (1 - side) * half, 0)
    )
    return whole


def stage_bits(first_x):
    levels = lax.axis_size("seq").bit_length() - 1
    rest = [2 + level for level in range(1, levels)]
    return ([1, 2] if first_x else [2, 1]) + rest


def row_order(features, bits):
    order = [0] + bits
    per_device = features >> len(order)
    rows = jnp.arange(features, dtype=jnp.int32)
    place = rows // per_device
    owner = flat_index()
    for step, bit in enumerate(order):
        taken = (place >> (len(order) - 1 - step)) & 1
        owner = owner ^ (taken << bit)
    return owner * per_device + rows % per_device


def row_picker(features, bits):
    order = row_order(features, bits)
    grid = jnp.arange(features, dtype=jnp.int32)
    return (grid[:, None] == order[None, :]).astype(jnp.bfloat16)


def outer(left, right):
    return jnp.einsum("tc,tf->cf", left, right, preferred_element_type=jnp.float32)


def scatter_outer(left, right, picker, bits):
    features = left.shape[1]
    picked = jnp.dot(left, picker, preferred_element_type=jnp.float32).astype(jnp.bfloat16)
    half = features // 2
    left = jnp.concatenate([picked[:, :half], swap(picked[:, half:], 0)], axis=0)
    right = jnp.concatenate([right, swap(right, 0)], axis=0)
    part = half // 2
    arrived = swap(outer(left[:, part:], right).astype(jnp.bfloat16), bits[0])
    total = outer(left[:, :part], right) + arrived.astype(jnp.float32)
    for bit in bits[1:]:
        part = part // 2
        rounded = total.astype(jnp.bfloat16)
        arrived = swap(rounded[part:], bit)
        total = total[:part] + arrived.astype(jnp.float32)
    return total


def scatter_vectors(vectors, bits):
    features = vectors.shape[1]
    part = features
    total = jnp.take(vectors, row_order(features, bits), axis=1)
    for bit in [0] + bits:
        part = part // 2
        total = total[:, :part] + swap(total[:, part:], bit)
    return total


def normalize(values, gain):
    average = jnp.mean(values, axis=-1, keepdims=True)
    centred = values - average
    spread = jnp.mean(centred * centred, axis=-1, keepdims=True)
    return centred * lax.rsqrt(spread + EPS) * gain


def rope_tables(position):
    inverse = jnp.power(THETA, -jnp.arange(0, HEAD_DIM, 2, dtype=jnp.float32) / HEAD_DIM)
    angles = position[:, None] * inverse[None, :]
    angles = jnp.concatenate([angles, angles], axis=-1)
    return (jnp.cos(angles)[:, None, :], jnp.sin(angles)[:, None, :])


def rotate(values, cosine, sine_tab):
    half = values.shape[-1] // 2
    turned = jnp.concatenate([-values[..., half:], values[..., :half]], axis=-1)
    return values * cosine + turned * sine_tab


def unrotate(grads, cosine, sine_tab):
    half = grads.shape[-1] // 2
    scaled = grads * sine_tab
    return grads * cosine + jnp.concatenate([scaled[..., half:], -scaled[..., :half]], axis=-1)


def layout(positions, lengths, total):
    count = lengths.shape[0]
    blocks = (lengths + BLOCK - 1) // BLOCK
    first = (jnp.cumsum(blocks) - blocks) * BLOCK
    owner = jnp.sum((positions[:, None] >= first[None, :]).astype(jnp.int32), axis=1) - 1
    table = owner[:, None] == jnp.arange(count, dtype=jnp.int32)[None, :]
    start = jnp.sum(jnp.where(table, first[None, :], 0), axis=1)
    span = jnp.sum(jnp.where(table, lengths[None, :], 0), axis=1)
    local = positions - start
    inside = (positions >= 0) & (positions < total)
    valid = inside & (local < span)
    segment = jnp.where(inside, jnp.where(valid, owner, owner + count), -1)
    return (segment, local, valid)


def gelu_pair(hidden):
    return jax.nn.gelu(hidden[:, :FF], approximate=False) * hidden[:, FF:]


def split_keys(extended):
    features = HEADS * HEAD_DIM
    key_rows = extended[:, :features].reshape(-1, HEADS, HEAD_DIM)
    value_rows = extended[:, features:].reshape(-1, HEADS, HEAD_DIM)
    return (key_rows, value_rows)


def attend_forward(queries, extended, allowed):
    scale = 1.0 / math.sqrt(HEAD_DIM)
    key_rows, value_rows = split_keys(extended)
    raw_scores = jnp.einsum("qhd,khd->hqk", queries, key_rows, preferred_element_type=jnp.float32)
    scores = jnp.where(allowed[None], raw_scores * scale, NEG)
    top = jnp.max(scores, axis=-1, keepdims=True)
    expo = jnp.exp(scores - top)
    summed = jnp.sum(expo, axis=-1, keepdims=True)
    probs = (expo / summed).astype(jnp.bfloat16)
    attended = jnp.einsum("hqk,khd->qhd", probs, value_rows, preferred_element_type=jnp.float32)
    return (attended, top + jnp.log(summed))


def attend_backward(queries, extended, log_total, attended_grad, allowed):
    scale = 1.0 / math.sqrt(HEAD_DIM)
    key_rows, value_rows = split_keys(extended)
    raw_scores = jnp.einsum("qhd,khd->hqk", queries, key_rows, preferred_element_type=jnp.float32)
    scores = jnp.where(allowed[None], raw_scores * scale, NEG)
    probs = jnp.exp(scores - log_total)
    probs_b = probs.astype(jnp.bfloat16)
    prob_grad = jnp.einsum(
        "qhd,khd->hqk", attended_grad, value_rows, preferred_element_type=jnp.float32
    )
    row_dot = jnp.sum(prob_grad * probs, axis=-1, keepdims=True)
    score_grad = (probs * (prob_grad - row_dot) * scale).astype(jnp.bfloat16)
    query_grad = jnp.einsum(
        "hqk,khd->qhd", score_grad, key_rows, preferred_element_type=jnp.float32
    )
    key_grad = jnp.einsum("hqk,qhd->khd", score_grad, queries, preferred_element_type=jnp.float32)
    value_grad = jnp.einsum(
        "hqk,qhd->khd", probs_b, attended_grad, preferred_element_type=jnp.float32
    )
    rows = extended.shape[0]
    return (
        query_grad,
        jnp.concatenate([key_grad.reshape(rows, -1), value_grad.reshape(rows, -1)], axis=1),
    )


def forward_layer(residual, weights, allowed, cosine, sine_tab):
    gain_a, w_qkv, w_proj, gain_m, w_wide, w_narrow = weights
    features = residual.shape[1]
    normed = normalize(residual, gain_a.astype(jnp.float32)).astype(jnp.bfloat16)
    projected = jnp.dot(normed, w_qkv, preferred_element_type=jnp.float32)
    queries = rotate(projected[:, :features].reshape(-1, HEADS, HEAD_DIM), cosine, sine_tab).astype(
        jnp.bfloat16
    )
    key_rows = (
        rotate(projected[:, features : 2 * features].reshape(-1, HEADS, HEAD_DIM), cosine, sine_tab)
        .astype(jnp.bfloat16)
        .reshape(-1, features)
    )
    value_rows = projected[:, 2 * features :].astype(jnp.bfloat16)
    extended = padded(jnp.concatenate([key_rows, value_rows], axis=1), (("seq", 0),), WINDOW // 2)
    attended, log_total = attend_forward(queries, extended, allowed)
    mixed_b = attended.reshape(-1, features).astype(jnp.bfloat16)
    middle = residual + jnp.dot(mixed_b, w_proj, preferred_element_type=jnp.float32)
    second = normalize(middle, gain_m.astype(jnp.float32)).astype(jnp.bfloat16)
    hidden = jnp.dot(second, w_wide, preferred_element_type=jnp.float32)
    gated_b = gelu_pair(hidden).astype(jnp.bfloat16)
    result = middle + jnp.einsum("tf,df->td", gated_b, w_narrow, preferred_element_type=jnp.float32)
    return (
        result,
        (residual, normed, queries, extended, log_total, mixed_b, middle, second, hidden, gated_b),
    )


def backward_layer(upstream, weights, kept, allowed, cosine, sine_tab, paths):
    gain_a, w_qkv, w_proj, gain_m, w_wide, w_narrow = weights
    residual, normed, queries, extended, log_total, mixed_b, middle, second, hidden, gated_b = kept
    features = residual.shape[1]
    halo_rows = WINDOW // 2
    upstream_b = upstream.astype(jnp.bfloat16)
    path_x, path_y = paths
    narrow_term = scatter_outer(upstream_b, gated_b, *path_x)
    gated_grad = jnp.einsum("td,df->tf", upstream_b, w_narrow, preferred_element_type=jnp.float32)
    _, pull_gate = jax.vjp(gelu_pair, hidden)
    hidden_grad = pull_gate(gated_grad)[0].astype(jnp.bfloat16)
    wide_term = jnp.concatenate(
        [
            scatter_outer(second, hidden_grad[:, :FF], *path_y),
            scatter_outer(second, hidden_grad[:, FF:], *path_x),
        ],
        axis=1,
    )
    second_grad = jnp.einsum("tf,cf->tc", hidden_grad, w_wide, preferred_element_type=jnp.float32)
    _, pull_second = jax.vjp(normalize, middle, gain_m.astype(jnp.float32))
    middle_part, mlp_term = pull_second(second_grad)
    middle_grad = upstream + middle_part
    middle_b = middle_grad.astype(jnp.bfloat16)
    proj_term = scatter_outer(mixed_b, middle_b, *path_x)
    attended_grad = (
        jnp.einsum("td,cd->tc", middle_b, w_proj, preferred_element_type=jnp.float32)
        .astype(jnp.bfloat16)
        .reshape(-1, HEADS, HEAD_DIM)
    )
    query_grad, extended_grad = attend_backward(
        queries, extended, log_total, attended_grad, allowed
    )
    rim_rows = jnp.concatenate([extended_grad[:halo_rows], extended_grad[-halo_rows:]], axis=0)
    arrived = padded(rim_rows.astype(jnp.bfloat16), (("seq", 0),), halo_rows).astype(rim_rows.dtype)
    own_rows = extended_grad[halo_rows:-halo_rows]
    own_rows = jnp.concatenate(
        [
            own_rows[:halo_rows] + arrived[:halo_rows],
            own_rows[halo_rows:-halo_rows],
            own_rows[-halo_rows:] + arrived[-halo_rows:],
        ],
        axis=0,
    )
    query_back = unrotate(query_grad, cosine, sine_tab).reshape(-1, features)
    key_back = unrotate(
        own_rows[:, :features].reshape(-1, HEADS, HEAD_DIM), cosine, sine_tab
    ).reshape(-1, features)
    joint_grad = jnp.concatenate([query_back, key_back, own_rows[:, features:]], axis=1).astype(
        jnp.bfloat16
    )
    split = 3 * features // 2
    qkv_term = jnp.concatenate(
        [
            scatter_outer(normed, joint_grad[:, :split], *path_y),
            scatter_outer(normed, joint_grad[:, split:], *path_x),
        ],
        axis=1,
    )
    normed_grad = jnp.einsum("tf,cf->tc", joint_grad, w_qkv, preferred_element_type=jnp.float32)
    _, pull_first = jax.vjp(normalize, residual, gain_a.astype(jnp.float32))
    residual_part, attn_term = pull_first(normed_grad)
    return (
        middle_grad + residual_part,
        (attn_term, qkv_term, proj_term, mlp_term, wide_term, narrow_term),
    )


def body(
    tokens,
    cotangent,
    lengths,
    block_perm,
    attn_gain,
    qkv_weight,
    proj_weight,
    mlp_gain,
    wide_weight,
    narrow_weight,
):
    seq_index = lax.axis_index("seq")
    seq_count = lax.axis_size("seq")
    levels = seq_count.bit_length() - 1
    tok_dev = tokens.shape[1]
    features = tokens.shape[2]
    block_rows = tok_dev // BLK_DEV
    halo_rows = WINDOW // 2
    order_map = block_perm[0]
    target = order_map[0::BLK_DEV] // BLK_DEV
    source = jnp.arange(seq_count, dtype=jnp.int32)

    def holder(bit_level):
        low_mask = (1 << bit_level) - 1
        place = jnp.bitwise_or(
            jnp.bitwise_and(target, low_mask), jnp.bitwise_and(source, ~low_mask)
        )
        return jnp.sum(jnp.where(place == seq_index, source, 0))

    moving = (tokens[0], cotangent[0])
    for bit_level in range(levels):
        payload = holder(bit_level)
        goal_index = jnp.sum(jnp.where(source == payload, target, 0))
        flipped = (
            jnp.bitwise_and(jnp.right_shift(jnp.bitwise_xor(seq_index, goal_index), bit_level), 1)
            == 1
        )
        arrived = partner((moving[0], moving[1]), "seq", bit_level)
        moving = (
            jnp.where(flipped, arrived[0], moving[0]),
            jnp.where(flipped, arrived[1], moving[1]),
        )
    home_index = holder(levels)
    slot_of = lax.dynamic_slice_in_dim(order_map, home_index * BLK_DEV, BLK_DEV) % BLK_DEV
    slot_range = jnp.arange(BLK_DEV, dtype=jnp.int32)
    placing = jnp.sum(
        jnp.where(slot_of[None, :] == slot_range[:, None], slot_range[None, :], 0), axis=1
    )
    packed_tok = jnp.take(
        moving[0].reshape(BLK_DEV, block_rows, features), placing, axis=0
    ).reshape(tok_dev, features)
    packed_cot = jnp.take(
        moving[1].reshape(BLK_DEV, block_rows, features), placing, axis=0
    ).reshape(tok_dev, features)
    total = seq_count * tok_dev
    own_place = seq_index * tok_dev + jnp.arange(tok_dev, dtype=jnp.int32)
    key_place = (
        seq_index * tok_dev - halo_rows + jnp.arange(tok_dev + 2 * halo_rows, dtype=jnp.int32)
    )
    seg_query, local_query, valid_query = layout(own_place, lengths[0], total)
    seg_key, _, _ = layout(key_place, lengths[0], total)
    offset = (
        jnp.arange(tok_dev, dtype=jnp.int32)[:, None]
        + halo_rows
        - jnp.arange(tok_dev + 2 * halo_rows, dtype=jnp.int32)[None, :]
    )
    allowed = (jnp.abs(offset) <= halo_rows) & (seg_query[:, None] == seg_key[None, :])
    cosine, sine_tab = rope_tables(local_query.astype(jnp.float32))
    residual = packed_tok.astype(jnp.float32)
    gains = jnp.concatenate([attn_gain, mlp_gain], axis=0)
    gains = lax.all_gather(gains, "fsdp", axis=1, tiled=True)
    gains_a, gains_m = gains[:LAYERS], gains[LAYERS:]
    paths = tuple(
        (row_picker(features, stage_bits(first_x)), stage_bits(first_x)) for first_x in (True, False)
    )
    kept_all = []
    weights_all = []
    for layer_index in range(LAYERS):
        weights = (
            gains_a[layer_index],
            gather_weight(qkv_weight[layer_index]),
            gather_weight(proj_weight[layer_index]),
            gains_m[layer_index],
            gather_weight(wide_weight[layer_index]),
            gather_weight(narrow_weight[layer_index]),
        )
        residual, kept = forward_layer(residual, weights, allowed, cosine, sine_tab)
        weights_all.append(weights)
        kept_all.append(kept)
    block_out = residual.astype(jnp.bfloat16)
    upstream = packed_cot.astype(jnp.float32) * valid_query[:, None].astype(jnp.float32)
    layer_terms = [None] * LAYERS
    for layer_index in reversed(range(LAYERS)):
        upstream, grad_terms = backward_layer(
            upstream,
            weights_all[layer_index],
            kept_all[layer_index],
            allowed,
            cosine,
            sine_tab,
            paths,
        )
        layer_terms[layer_index] = grad_terms
    vectors = jnp.stack(
        [layer_terms[layer_index][0] for layer_index in range(LAYERS)]
        + [layer_terms[layer_index][3] for layer_index in range(LAYERS)]
    )
    gain_sums = scatter_vectors(vectors, stage_bits(True))
    stacked = [
        jnp.stack([layer_terms[layer_index][part_index] for layer_index in range(LAYERS)])
        if part_index not in (0, 3)
        else gain_sums[(0 if part_index == 0 else LAYERS) :][:LAYERS]
        for part_index in range(6)
    ]
    out_blocks = block_out.reshape(BLK_DEV, block_rows, features)
    grad_blocks = upstream.astype(jnp.bfloat16).reshape(BLK_DEV, block_rows, features)
    returning = (
        jnp.take(out_blocks, slot_of, axis=0).reshape(tok_dev, features),
        jnp.take(grad_blocks, slot_of, axis=0).reshape(tok_dev, features),
    )
    for bit_level in reversed(range(levels)):
        payload = holder(bit_level + 1)
        flipped = (
            jnp.bitwise_and(jnp.right_shift(jnp.bitwise_xor(seq_index, payload), bit_level), 1) == 1
        )
        arrived = partner((returning[0], returning[1]), "seq", bit_level)
        returning = (
            jnp.where(flipped, arrived[0], returning[0]),
            jnp.where(flipped, arrived[1], returning[1]),
        )
    return (
        returning[0][None],
        returning[1][None],
        stacked[0],
        stacked[1],
        stacked[2],
        stacked[3],
        stacked[4],
        stacked[5],
    )


def solution(mesh):
    in_specs = (
        P("fsdp", "seq", None),
        P("fsdp", "seq", None),
        P("fsdp", None),
        P("fsdp", None),
        P(None, "fsdp"),
        P(None, "fsdp", None),
        P(None, "fsdp", None),
        P(None, "fsdp"),
        P(None, "fsdp", None),
        P(None, "fsdp", None),
    )
    out_specs = (
        P("fsdp", "seq", None),
        P("fsdp", "seq", None),
        P(None, ("seq", "fsdp")),
        P(None, ("seq", "fsdp"), None),
        P(None, ("seq", "fsdp"), None),
        P(None, ("seq", "fsdp")),
        P(None, ("seq", "fsdp"), None),
        P(None, ("seq", "fsdp"), None),
    )
    return jax.shard_map(body, mesh=mesh, in_specs=in_specs, out_specs=out_specs, check_vma=False)
```

```python
import functools
import math

import jax
import jax.numpy as jnp
from jax import lax
from jax.experimental import pallas as pl
from jax.experimental.pallas import tpu as pltpu
from jax.sharding import PartitionSpec as P

HEADS = 16
HEAD_DIM = 64
FF = 2624
WINDOW = 128
BLOCK = 128
BLK_DEV = 2
LAYERS = 2

NEG = -1e30
EPS = 1e-05
THETA = 10000.0

AXES = ("seq", "fsdp")
LANES = 128
HALO = WINDOW // 2
CHUNKS = 3
FF_PAD = -(-FF // (LANES * CHUNKS)) * LANES * CHUNKS
FF_CHUNK = FF_PAD // CHUNKS
F32 = jnp.float32
BF16 = jnp.bfloat16
VMEM_LIMIT = 48 * 1024 * 1024
NT = (((1,), (1,)), ((), ()))
TN = (((0,), (0,)), ((), ()))


class Links:
    DEPTH = 2

    def __init__(self):
        self.queues = {}

    def tie(self, value, key):
        queue = self.queues.setdefault(key, [])
        if len(queue) >= self.DEPTH:
            value, _ = lax.optimization_barrier((value, queue[-self.DEPTH]))
        return value

    def swap(self, value, bit):
        count = lax.axis_size("seq") * lax.axis_size("fsdp")
        value = self.tie(value, bit)
        result = lax.ppermute(value, AXES, [(i, i ^ (1 << bit)) for i in range(count)])
        self.queues.setdefault(bit, []).append(result)
        return result


def shift(value, up):
    count = lax.axis_size("seq")
    route = [(i, i + 1) for i in range(count - 1)]
    if not up:
        route = [(b, a) for a, b in route]
    return lax.ppermute(value, "seq", route)


def flat_index():
    return lax.axis_index("seq") * lax.axis_size("fsdp") + lax.axis_index("fsdp")


def gather_pieces(links, shard):
    half = shard.shape[0] // 2
    side = lax.axis_index("seq") % 2
    sent = lax.dynamic_slice_in_dim(shard, side * half, half, 0)
    own_core = links.swap(shard, 0)
    far_x = links.swap(sent, 1)
    far_y = links.swap(far_x, 2)
    far_x_core = links.swap(far_x, 0)
    far_y_core = links.swap(far_y, 0)
    return (shard, own_core, far_x, far_y, far_x_core, far_y_core)


def piece_order():
    quarter = lax.axis_index("fsdp")
    side = lax.axis_index("seq") % 2
    one = 1 - side
    order = [quarter * 2, quarter * 2 + 1, (quarter ^ 1) * 2, (quarter ^ 1) * 2 + 1]
    order += [(quarter ^ 2) * 2 + side, (quarter ^ 2) * 2 + one]
    order += [(quarter ^ 3) * 2 + side, (quarter ^ 3) * 2 + one]
    return jnp.stack(order).astype(jnp.int32)


def stage_bits(first_x):
    levels = lax.axis_size("seq").bit_length() - 1
    rest = [2 + level for level in range(1, levels)]
    return ([1, 2] if first_x else [2, 1]) + rest


def row_order(features, bits):
    order = [0] + bits
    per_device = features >> len(order)
    rows = jnp.arange(features, dtype=jnp.int32)
    place = rows // per_device
    owner = flat_index()
    for step, bit in enumerate(order):
        taken = (place >> (len(order) - 1 - step)) & 1
        owner = owner ^ (taken << bit)
    return owner * per_device + rows % per_device


def row_picker(features, bits):
    order = row_order(features, bits)
    grid = jnp.arange(features, dtype=jnp.int32)
    return (order[:, None] == grid[None, :]).astype(BF16)


def pick(links, picker, left):
    half = picker.shape[0] // 2
    rows = lax.dot_general(picker, left, NT, preferred_element_type=F32).astype(BF16)
    return (rows[:half], links.swap(rows[half:], 0))


def scatter_vectors(vectors, bits):
    links = Links()
    features = vectors.shape[1]
    part = features
    total = jnp.take(vectors, row_order(features, bits), axis=1)
    for bit in [0] + bits:
        part = part // 2
        total = total[:, :part] + links.swap(total[:, part:], bit)
    return total


def call(kernel, outs, scratch=(), smem=1, grid=None, in_specs=None, out_specs=None, flops=0):
    params = dict(
        compiler_params=pltpu.CompilerParams(vmem_limit_bytes=VMEM_LIMIT),
        out_shape=outs,
        scratch_shapes=list(scratch),
        cost_estimate=pl.CostEstimate(flops=flops, bytes_accessed=1 << 20, transcendentals=0),
    )
    if grid is not None:
        params["grid"] = grid

    def run(*args):
        specs = in_specs
        if specs is None:
            specs = [pl.BlockSpec(memory_space=pltpu.SMEM)] * smem
            specs += [pl.BlockSpec(memory_space=pltpu.VMEM)] * (len(args) - smem)
        results = out_specs
        if results is None:
            results = jax.tree.map(lambda _: pl.BlockSpec(memory_space=pltpu.VMEM), outs)
        return pl.pallas_call(kernel, in_specs=specs, out_specs=results, **params)(*args)

    return run


def struct(shape, dtype):
    return jax.ShapeDtypeStruct(shape, dtype)


def to_pieces(offs, source, target):
    for k in range(source.shape[1] // LANES):
        start = pl.multiple_of(offs[k] * LANES, LANES)
        target[:, k * LANES : (k + 1) * LANES] = source[:, pl.ds(start, LANES)]


def from_pieces(offs, source, target):
    for k in range(source.shape[1] // LANES):
        start = pl.multiple_of(offs[k] * LANES, LANES)
        target[:, pl.ds(start, LANES)] = source[:, k * LANES : (k + 1) * LANES]


def joined(pieces, columns=slice(None)):
    return jnp.concatenate([piece[:, columns] for piece in pieces], axis=0)


def statistics(values):
    average = jnp.mean(values, axis=-1, keepdims=True)
    centred = values - average
    spread = jnp.mean(centred * centred, axis=-1, keepdims=True)
    rho = lax.rsqrt(spread + EPS)
    return centred, rho


def norm_pull(values, gain, grad):
    centred, rho = statistics(values)
    unit = centred * rho
    scaled = grad * gain
    mean_a = jnp.mean(scaled, axis=-1, keepdims=True)
    mean_b = jnp.mean(scaled * unit, axis=-1, keepdims=True)
    return rho * (scaled - mean_a - unit * mean_b), jnp.sum(grad * unit, axis=0, keepdims=True)


def turn_chunk(values, cosine, sine, sign):
    lane = lax.broadcasted_iota(jnp.int32, values.shape, 1)
    ahead = pltpu.roll(values, LANES - HEAD_DIM // 2, 1)
    behind = pltpu.roll(values, HEAD_DIM // 2, 1)
    turned = jnp.where(lane % HEAD_DIM < HEAD_DIM // 2, ahead, behind)
    if sign > 0:
        return values * cosine + turned * sine
    return values * cosine - turned * sine


def qkv_kernel(offs, x, gain, cosine, sine, p0, p1, p2, p3, p4, p5, out, normed, placed):
    step = pl.program_id(0)

    @pl.when(step == 0)
    def _():
        centred, rho = statistics(x[...])
        normed[...] = (centred * rho * gain[...]).astype(BF16)
        to_pieces(offs, normed, placed)

    product = jnp.dot(
        placed[...], joined((p0, p1, p2, p3, p4, p5)), preferred_element_type=F32
    )

    @pl.when(step < 2)
    def _():
        for k in range(product.shape[1] // LANES):
            part = slice(k * LANES, (k + 1) * LANES)
            out[:, part] = turn_chunk(product[:, part], cosine[...], sine[...], 1).astype(BF16)

    @pl.when(step == 2)
    def _():
        out[...] = product.astype(BF16)


def piece_specs(rows, columns):
    half = rows // 2
    own = pl.BlockSpec((rows, columns), lambda j: (0, j))
    far = pl.BlockSpec((half, columns), lambda j: (0, j))
    return [own, own, far, far, far, far]


def whole_spec(shape):
    return pl.BlockSpec(shape, lambda j: tuple(0 for _ in shape))


def run_qkv(offs, x, gain, cosine, sine, pieces):
    tokens, features = x.shape
    return call(
        qkv_kernel,
        (struct((tokens, 3 * features), BF16), struct((tokens, features), BF16)),
        [pltpu.VMEM((tokens, features), BF16)],
        grid=(3,),
        in_specs=[pl.BlockSpec(memory_space=pltpu.SMEM)]
        + [whole_spec(v.shape) for v in (x, gain, cosine, sine)]
        + piece_specs(pieces[0].shape[0], features),
        out_specs=(
            pl.BlockSpec((tokens, features), lambda j: (0, j)),
            whole_spec((tokens, features)),
        ),
    )(offs, x, gain, cosine, sine, *pieces)


def extend(qkv, before, after, extended):
    tokens, features = qkv.shape[0], qkv.shape[1] // 3
    extended[:HALO, :] = before[...]
    extended[HALO : HALO + tokens, :] = qkv[:, features:]
    extended[HALO + tokens :, :] = after[...]


def attend_kernel(
    offs, qkv, before, after, seg_q, seg_k, x, gain,
    p0, p1, p2, p3, p4, p5, mixed, middle, second, extended, placed,
):
    tokens, features = x.shape
    extend(qkv, before, after, extended)
    scale = 1.0 / math.sqrt(HEAD_DIM)
    span = BLOCK + 2 * HALO
    row = lax.broadcasted_iota(jnp.int32, (BLOCK, span), 0)
    col = lax.broadcasted_iota(jnp.int32, (BLOCK, span), 1)
    near = (col >= row) & (col - row <= 2 * HALO)
    low = lax.broadcasted_iota(jnp.int32, (BLOCK, LANES), 1) < HEAD_DIM
    bias = []
    for block in range(tokens // BLOCK):
        base = block * BLOCK
        same = seg_q[base : base + BLOCK, :] == seg_k[:, base : base + span]
        bias.append(jnp.where(near & same, 0.0, NEG))

    def pair(index, carry):
        lanes = pl.ds(pl.multiple_of(index * LANES, LANES), LANES)
        value_lanes = pl.ds(pl.multiple_of(features + index * LANES, LANES), LANES)
        for block in range(tokens // BLOCK):
            base = block * BLOCK
            queries = qkv[base : base + BLOCK, lanes]
            keys = extended[base : base + span, lanes]
            values = extended[base : base + span, value_lanes]
            parts = []
            for keep in (low, ~low):
                chosen = jnp.where(keep, queries, jnp.zeros_like(queries))
                raw = lax.dot_general(chosen, keys, NT, preferred_element_type=F32)
                scores = raw * scale + bias[block]
                expo = jnp.exp(scores - jnp.max(scores, axis=-1, keepdims=True))
                probs = expo * (1.0 / jnp.sum(expo, axis=-1, keepdims=True))
                parts.append(jnp.dot(probs.astype(BF16), values, preferred_element_type=F32))
            mixed[base : base + BLOCK, lanes] = jnp.where(low, parts[0], parts[1]).astype(BF16)
        return carry

    lax.fori_loop(0, features // LANES, pair, 0)
    to_pieces(offs, mixed, placed)
    total = x[...] + jnp.dot(
        placed[...], joined((p0, p1, p2, p3, p4, p5)), preferred_element_type=F32
    )
    middle[...] = total
    centred, rho = statistics(total)
    second[...] = (centred * rho * gain[...]).astype(BF16)


def run_attend(offs, qkv, before, after, seg_q, seg_k, x, gain, pieces):
    tokens, features = x.shape
    return call(
        attend_kernel,
        (
            struct((tokens, features), BF16),
            struct((tokens, features), F32),
            struct((tokens, features), BF16),
        ),
        [
            pltpu.VMEM((tokens + 2 * HALO, 2 * features), BF16),
            pltpu.VMEM((tokens, features), BF16),
        ],
    )(offs, qkv, before, after, seg_q, seg_k, x, gain, *pieces)


def mlp_kernel(offs, second, carried, p0, p1, p2, p3, p4, p5, total, gated, slope, gate, placed, part):
    pieces = (p0, p1, p2, p3, p4, p5)
    to_pieces(offs, second, placed)
    source = placed[...]
    hidden = jnp.dot(source, joined(pieces, slice(0, FF_CHUNK)), preferred_element_type=F32)
    other = jnp.dot(
        source, joined(pieces, slice(FF_CHUNK, 2 * FF_CHUNK)), preferred_element_type=F32
    )
    normal = 0.5 * (1.0 + lax.erf(hidden * math.sqrt(0.5)))
    density = jnp.exp(-0.5 * hidden * hidden) * (1.0 / math.sqrt(2.0 * math.pi))
    active = hidden * normal
    product = (active * other).astype(BF16)
    gated[...] = product
    slope[...] = ((normal + hidden * density) * other).astype(BF16)
    gate[...] = active.astype(BF16)
    part[...] = lax.dot_general(
        product,
        joined(pieces, slice(2 * FF_CHUNK, 3 * FF_CHUNK)),
        NT,
        preferred_element_type=F32,
    )
    for k in range(part.shape[1] // LANES):
        lanes = pl.ds(pl.multiple_of(offs[k] * LANES, LANES), LANES)
        total[:, lanes] = carried[:, lanes] + part[:, k * LANES : (k + 1) * LANES]


def run_mlp(offs, second, carried, pieces):
    tokens, features = second.shape
    hidden = struct((tokens, FF_CHUNK), BF16)
    return call(
        mlp_kernel,
        (struct((tokens, features), F32), hidden, hidden, hidden),
        [pltpu.VMEM((tokens, features), BF16), pltpu.VMEM((tokens, features), F32)],
    )(offs, second, carried, *pieces)


def mlp_pull(offs, upstream, slope, gate, pieces, input_grad, gate_grad, placed):
    to_pieces(offs, upstream, placed)
    gated_grad = jnp.dot(
        placed[...],
        joined(pieces, slice(2 * FF_CHUNK, 3 * FF_CHUNK)),
        preferred_element_type=F32,
    )
    first = (slope[...].astype(F32) * gated_grad).astype(BF16)
    other = (gate[...].astype(F32) * gated_grad).astype(BF16)
    input_grad[...] = first
    gate_grad[...] = other
    return lax.dot_general(
        first, joined(pieces, slice(0, FF_CHUNK)), NT, preferred_element_type=F32
    ) + lax.dot_general(
        other, joined(pieces, slice(FF_CHUNK, 2 * FF_CHUNK)), NT, preferred_element_type=F32
    )


def mlp_back_kernel(
    first, offs, upstream, slope, gate, carried, p0, p1, p2, p3, p4, p5,
    total, input_grad, gate_grad, placed,
):
    part = mlp_pull(
        offs, upstream, slope, gate, (p0, p1, p2, p3, p4, p5), input_grad, gate_grad, placed
    )
    total[...] = part if first else carried[...] + part


def mlp_back_last_kernel(
    offs, upstream, slope, gate, carried, residual_grad, middle, gain, p0, p1, p2, p3, p4, p5,
    middle_grad, middle_grad_b, gain_grad, input_grad, gate_grad, placed, sums, ordered,
):
    part = mlp_pull(
        offs, upstream, slope, gate, (p0, p1, p2, p3, p4, p5), input_grad, gate_grad, placed
    )
    sums[...] = carried[...] + part
    from_pieces(offs, sums, ordered)
    pulled, gains = norm_pull(middle[...], gain[...], ordered[...])
    result = residual_grad[...] + pulled
    middle_grad[...] = result
    middle_grad_b[...] = result.astype(BF16)
    gain_grad[...] = gains


def run_mlp_back(offs, upstream, slope, gate, carried, pieces):
    tokens, features = upstream.shape
    hidden = struct((tokens, FF_CHUNK), BF16)
    first = carried is None
    if first:
        carried = jnp.zeros((8, LANES), F32)
    return call(
        functools.partial(mlp_back_kernel, first),
        (struct((tokens, features), F32), hidden, hidden),
        [pltpu.VMEM((tokens, features), BF16)],
    )(offs, upstream, slope, gate, carried, *pieces)


def run_mlp_back_last(offs, upstream, slope, gate, carried, residual_grad, middle, gain, pieces):
    tokens, features = upstream.shape
    hidden = struct((tokens, FF_CHUNK), BF16)
    return call(
        mlp_back_last_kernel,
        (
            struct((tokens, features), F32),
            struct((tokens, features), BF16),
            struct((1, features), F32),
            hidden,
            hidden,
        ),
        [
            pltpu.VMEM((tokens, features), BF16),
            pltpu.VMEM((tokens, features), F32),
            pltpu.VMEM((tokens, features), F32),
        ],
    )(offs, upstream, slope, gate, carried, residual_grad, middle, gain, *pieces)


def attend_back_kernel(
    offs, middle_grad, qkv, before, after, seg_q, seg_k, cosine, sine, p0, p1, p2, p3, p4, p5,
    query_grad, own_grad, rim_before, rim_after, extended, mixed_grad, extended_grad,
):
    tokens, features = middle_grad.shape
    extend(qkv, before, after, extended)
    placed = lax.dot_general(
        middle_grad[...], joined((p0, p1, p2, p3, p4, p5)), NT, preferred_element_type=F32
    ).astype(BF16)
    for k in range(features // LANES):
        lanes = pl.ds(pl.multiple_of(offs[k] * LANES, LANES), LANES)
        mixed_grad[:, lanes] = placed[:, k * LANES : (k + 1) * LANES]
    scale = 1.0 / math.sqrt(HEAD_DIM)
    span = BLOCK + 2 * HALO
    row = lax.broadcasted_iota(jnp.int32, (span, BLOCK), 1)
    col = lax.broadcasted_iota(jnp.int32, (span, BLOCK), 0)
    near = (col >= row) & (col - row <= 2 * HALO)
    low = lax.broadcasted_iota(jnp.int32, (BLOCK, LANES), 1) < HEAD_DIM
    bias = []
    for block in range(tokens // BLOCK):
        base = block * BLOCK
        same = seg_q[:, base : base + BLOCK] == seg_k[base : base + span, :]
        bias.append(jnp.where(near & same, 0.0, NEG))

    def pair(index, carry):
        lanes = pl.ds(pl.multiple_of(index * LANES, LANES), LANES)
        value_lanes = pl.ds(pl.multiple_of(features + index * LANES, LANES), LANES)
        key_sums = []
        value_sums = []
        for block in range(tokens // BLOCK):
            base = block * BLOCK
            here = slice(base, base + BLOCK)
            queries = qkv[here, lanes]
            grads = mixed_grad[here, lanes]
            keys = extended[base : base + span, lanes]
            values = extended[base : base + span, value_lanes]
            key_sum = None
            value_sum = None
            query_parts = []
            for keep in (low, ~low):
                chosen = jnp.where(keep, queries, jnp.zeros_like(queries))
                chosen_grad = jnp.where(keep, grads, jnp.zeros_like(grads))
                raw = lax.dot_general(keys, chosen, NT, preferred_element_type=F32)
                scores = raw * scale + bias[block]
                expo = jnp.exp(scores - jnp.max(scores, axis=0, keepdims=True))
                probs = expo * (1.0 / jnp.sum(expo, axis=0, keepdims=True))
                prob_grad = lax.dot_general(values, chosen_grad, NT, preferred_element_type=F32)
                delta = jnp.sum(prob_grad * probs, axis=0, keepdims=True)
                score_grad = (probs * (prob_grad - delta) * scale).astype(BF16)
                query_parts.append(
                    lax.dot_general(score_grad, keys, TN, preferred_element_type=F32)
                )
                to_keys = jnp.dot(score_grad, chosen, preferred_element_type=F32)
                to_values = jnp.dot(
                    probs.astype(BF16), chosen_grad, preferred_element_type=F32
                )
                key_sum = to_keys if key_sum is None else key_sum + to_keys
                value_sum = to_values if value_sum is None else value_sum + to_values
            joint = jnp.where(low, query_parts[0], query_parts[1])
            query_grad[here, lanes] = turn_chunk(
                joint, cosine[here, :], sine[here, :], -1
            ).astype(BF16)
            key_sums.append(key_sum)
            value_sums.append(value_sum)
        for sums, place in ((key_sums, lanes), (value_sums, value_lanes)):
            over = 2 * HALO
            extended_grad[:BLOCK, place] = sums[0][:BLOCK]
            extended_grad[BLOCK : BLOCK + over, place] = sums[0][BLOCK:] + sums[1][:over]
            extended_grad[BLOCK + over :, place] = sums[1][over:]
        return carry

    lax.fori_loop(0, features // LANES, pair, 0)
    rim_before[...] = extended_grad[:HALO, :].astype(BF16)
    own_grad[...] = extended_grad[HALO : HALO + tokens, :]
    rim_after[...] = extended_grad[HALO + tokens :, :].astype(BF16)


def run_attend_back(offs, middle_grad, qkv, before, after, seg_q, seg_k, cosine, sine, pieces):
    tokens, features = middle_grad.shape
    rim = struct((HALO, 2 * features), BF16)
    return call(
        attend_back_kernel,
        (struct((tokens, features), BF16), struct((tokens, 2 * features), F32), rim, rim),
        [
            pltpu.VMEM((tokens + 2 * HALO, 2 * features), BF16),
            pltpu.VMEM((tokens, features), BF16),
            pltpu.VMEM((tokens + 2 * HALO, 2 * features), F32),
        ],
    )(offs, middle_grad, qkv, before, after, seg_q, seg_k, cosine, sine, *pieces)


def qkv_back_kernel(
    offs, query_grad, own_grad, arrived_first, arrived_last, cosine, sine, x, gain, middle_grad,
    p0, p1, p2, p3, p4, p5, joint, upstream, upstream_b, gain_grad, sums, ordered,
):
    step = pl.program_id(0)
    tokens, features = x.shape

    @pl.when(step == 0)
    def _():
        joint[...] = query_grad[...]

    for part in (1, 2):

        @pl.when(step == part)
        def _():
            for k in range(features // LANES):
                here = slice(k * LANES, (k + 1) * LANES)
                there = slice((part - 1) * features + k * LANES, (part - 1) * features + (k + 1) * LANES)
                rows = [
                    own_grad[:HALO, there] + arrived_first[:, there].astype(F32),
                    own_grad[HALO : tokens - HALO, there],
                    own_grad[tokens - HALO :, there] + arrived_last[:, there].astype(F32),
                ]
                grads = jnp.concatenate(rows, axis=0)
                if part == 1:
                    grads = turn_chunk(grads, cosine[...], sine[...], -1)
                joint[:, here] = grads.astype(BF16)

    product = lax.dot_general(
        joint[...], joined((p0, p1, p2, p3, p4, p5)), NT, preferred_element_type=F32
    )

    @pl.when(step == 0)
    def _():
        sums[...] = product

    @pl.when(step > 0)
    def _():
        sums[...] += product

    @pl.when(step == 2)
    def _():
        from_pieces(offs, sums, ordered)
        pulled, gains = norm_pull(x[...], gain[...], ordered[...])
        result = middle_grad[...] + pulled
        upstream[...] = result
        upstream_b[...] = result.astype(BF16)
        gain_grad[...] = gains


def run_qkv_back(
    offs, query_grad, own_grad, arrived_first, arrived_last, cosine, sine, x, gain, middle_grad, pieces
):
    tokens, features = x.shape
    whole = (query_grad, own_grad, arrived_first, arrived_last, cosine, sine, x, gain, middle_grad)
    return call(
        qkv_back_kernel,
        (
            struct((tokens, 3 * features), BF16),
            struct((tokens, features), F32),
            struct((tokens, features), BF16),
            struct((1, features), F32),
        ),
        [pltpu.VMEM((tokens, features), F32), pltpu.VMEM((tokens, features), F32)],
        grid=(3,),
        in_specs=[pl.BlockSpec(memory_space=pltpu.SMEM)]
        + [whole_spec(v.shape) for v in whole]
        + piece_specs(pieces[0].shape[0], features),
        out_specs=(
            pl.BlockSpec((tokens, features), lambda j: (0, j)),
            whole_spec((tokens, features)),
            whole_spec((tokens, features)),
            whole_spec((1, features)),
        ),
    )(offs, *whole, *pieces)


def outer_kernel(count, *refs):
    keep, send = refs[4 * count :]
    half = keep.shape[0]
    column = 0
    for k in range(count):
        left, left_far, right, right_far = refs[4 * k : 4 * k + 4]
        width = right.shape[1]
        for rows, target in ((slice(half, 2 * half), send), (slice(0, half), keep)):
            target[:, column : column + width] = (
                jnp.dot(left[rows, :], right[...], preferred_element_type=F32)
                + jnp.dot(left_far[rows, :], right_far[...], preferred_element_type=F32)
            ).astype(BF16)
        column += width


def run_outer(terms):
    flat = []
    specs = []
    width = 0
    for (left, left_far), (right, right_far, start, columns) in terms:
        flat += [left, left_far, right, right_far]
        specs += [whole_spec(left.shape)] * 2
        specs += [
            pl.BlockSpec((right.shape[0], columns), lambda j, at=start // columns: (0, at))
        ] * 2
        width += columns
    half = terms[0][0][0].shape[0] // 2
    out = struct((half, width), BF16)
    return call(
        functools.partial(outer_kernel, len(terms)),
        (out, out),
        grid=(1,),
        in_specs=specs,
        out_specs=(whole_spec((half, width)),) * 2,
    )(*flat)


class Sum:
    def __init__(self, links, terms, bits):
        self.links = links
        self.bits = list(bits)
        self.keep, send = run_outer(terms)
        self.come = links.swap(send, self.bits.pop(0))

    def step(self, final=False):
        total = self.keep.shape[0]
        if final:
            return self.keep.astype(F32) + self.come.astype(F32)
        half = total // 2
        send = (self.keep[half:].astype(F32) + self.come[half:].astype(F32)).astype(BF16)
        self.keep = (self.keep[:half].astype(F32) + self.come[:half].astype(F32)).astype(BF16)
        self.come = self.links.swap(send, self.bits.pop(0))


class Joint:
    def __init__(self, links, sums):
        self.sums = sums
        self.links = links
        self.bits = list(sums[0].bits)
        self.keep = None

    def advance(self):
        if self.keep is None and len(self.sums[0].bits) > len(self.bits) - 1:
            for part in self.sums:
                part.step()
            self.bits = list(self.sums[0].bits)
            self.keep = False
            return None
        if self.keep is False:
            keeps = [part.keep for part in self.sums]
            comes = [part.come for part in self.sums]
        else:
            keeps, comes = [self.keep], [self.come]
        if not self.bits:
            rows = [k.astype(F32) + c.astype(F32) for k, c in zip(keeps, comes)]
            return jnp.concatenate(rows, axis=1)
        half = keeps[0].shape[0] // 2

        def added(rows):
            parts = [
                (k[rows].astype(F32) + c[rows].astype(F32)).astype(BF16)
                for k, c in zip(keeps, comes)
            ]
            return jnp.concatenate(parts, axis=1)

        send = added(slice(half, None))
        self.keep = added(slice(0, half))
        self.come = self.links.swap(send, self.bits.pop(0))
        return None


class Pipeline:
    def __init__(self):
        self.running = []

    def advance(self):
        for item in list(self.running):
            result = item[0].advance()
            if result is not None:
                item[1](result)
                self.running.remove(item)

    def add(self, joint, deliver):
        self.running.append((joint, deliver))

    def finish(self):
        while self.running:
            self.advance()


def rope_tables(position):
    inverse = jnp.power(THETA, -jnp.arange(0, HEAD_DIM, 2, dtype=F32) / HEAD_DIM)
    angles = position[:, None] * inverse[None, :]
    cosine, sine = jnp.cos(angles), jnp.sin(angles)
    return (
        jnp.concatenate([cosine, cosine, cosine, cosine], axis=-1),
        jnp.concatenate([-sine, sine, -sine, sine], axis=-1),
    )


def layout(positions, lengths, total):
    count = lengths.shape[0]
    blocks = (lengths + BLOCK - 1) // BLOCK
    first = (jnp.cumsum(blocks) - blocks) * BLOCK
    owner = jnp.sum((positions[:, None] >= first[None, :]).astype(jnp.int32), axis=1) - 1
    table = owner[:, None] == jnp.arange(count, dtype=jnp.int32)[None, :]
    start = jnp.sum(jnp.where(table, first[None, :], 0), axis=1)
    span = jnp.sum(jnp.where(table, lengths[None, :], 0), axis=1)
    local = positions - start
    inside = (positions >= 0) & (positions < total)
    valid = inside & (local < span)
    segment = jnp.where(inside, jnp.where(valid, owner, owner + count), -1)
    return (segment, local, valid)


def body(
    tokens,
    cotangent,
    lengths,
    block_perm,
    attn_gain,
    qkv_weight,
    proj_weight,
    mlp_gain,
    wide_weight,
    narrow_weight,
):
    links = Links()
    seq_index = lax.axis_index("seq")
    seq_count = lax.axis_size("seq")
    levels = seq_count.bit_length() - 1
    tok_dev = tokens.shape[1]
    features = tokens.shape[2]
    block_rows = tok_dev // BLK_DEV
    order_map = block_perm[0]
    target = order_map[0::BLK_DEV] // BLK_DEV
    source = jnp.arange(seq_count, dtype=jnp.int32)

    def holder(bit_level):
        low_mask = (1 << bit_level) - 1
        place = jnp.bitwise_or(
            jnp.bitwise_and(target, low_mask), jnp.bitwise_and(source, ~low_mask)
        )
        return jnp.sum(jnp.where(place == seq_index, source, 0))

    home_index = holder(levels)
    slot_of = lax.dynamic_slice_in_dim(order_map, home_index * BLK_DEV, BLK_DEV) % BLK_DEV
    crossed = slot_of[0] == 1

    def crossing(rows):
        turned = jnp.concatenate([rows[block_rows:], rows[:block_rows]], axis=0)
        return jnp.where(crossed, turned, rows)

    def to_packed_step(moving, bit_level):
        payload = holder(bit_level)
        goal_index = jnp.sum(jnp.where(source == payload, target, 0))
        flipped = (
            jnp.bitwise_and(jnp.right_shift(jnp.bitwise_xor(seq_index, goal_index), bit_level), 1)
            == 1
        )
        return jnp.where(flipped, links.swap(moving, 2 + bit_level), moving)

    def to_given_step(moving, bit_level):
        payload = holder(bit_level + 1)
        flipped = (
            jnp.bitwise_and(jnp.right_shift(jnp.bitwise_xor(seq_index, payload), bit_level), 1) == 1
        )
        return jnp.where(flipped, links.swap(moving, 2 + bit_level), moving)

    def to_packed(rows):
        for bit_level in range(levels):
            rows = to_packed_step(rows, bit_level)
        return crossing(rows)

    def to_given(rows):
        rows = crossing(rows)
        for bit_level in reversed(range(levels)):
            rows = to_given_step(rows, bit_level)
        return rows

    total = seq_count * tok_dev
    own_place = seq_index * tok_dev + jnp.arange(tok_dev, dtype=jnp.int32)
    key_place = seq_index * tok_dev - HALO + jnp.arange(tok_dev + 2 * HALO, dtype=jnp.int32)
    seg_query, local_query, valid_query = layout(own_place, lengths[0], total)
    seg_key, _, _ = layout(key_place, lengths[0], total)
    cosine, sine = rope_tables(local_query.astype(F32))
    seg_q_col, seg_q_row = seg_query[:, None], seg_query[None, :]
    seg_k_col, seg_k_row = seg_key[:, None], seg_key[None, :]
    offs = piece_order()
    bits_x, bits_y = stage_bits(True), stage_bits(False)
    picker_x, picker_y = row_picker(features, bits_x), row_picker(features, bits_y)

    gains = jnp.concatenate([attn_gain, mlp_gain], axis=0)
    gains = lax.all_gather(gains, "fsdp", axis=1, tiled=True).astype(F32)
    gains_a = [gains[layer : layer + 1] for layer in range(LAYERS)]
    gains_m = [gains[LAYERS + layer : LAYERS + layer + 1] for layer in range(LAYERS)]

    def mlp_shard(layer, chunk):
        parts = []
        start, stop = chunk * FF_CHUNK, min((chunk + 1) * FF_CHUNK, FF)
        for array, base in ((wide_weight, 0), (wide_weight, FF), (narrow_weight, 0)):
            part = array[layer, :, base + start : base + stop]
            parts.append(jnp.pad(part, ((0, 0), (0, FF_CHUNK - (stop - start)))))
        return jnp.concatenate(parts, axis=1)

    residual = to_packed(tokens[0]).astype(F32)
    w_qkv, w_proj, w_mlp = [], [], []
    for layer in range(LAYERS):
        w_qkv.append(gather_pieces(links, qkv_weight[layer]))
        w_proj.append(gather_pieces(links, proj_weight[layer]))
        w_mlp.append(
            [gather_pieces(links, mlp_shard(layer, chunk)) for chunk in range(CHUNKS)]
        )
    packed_cot = to_packed(cotangent[0])

    kept = []
    for layer in range(LAYERS):
        qkv, normed = run_qkv(offs, residual, gains_a[layer], cosine, sine, w_qkv[layer])
        edges = qkv[:, features:]
        before = shift(edges[tok_dev - HALO :], True)
        after = shift(edges[:HALO], False)
        mixed, middle, second = run_attend(
            offs, qkv, before, after, seg_q_col, seg_k_row, residual, gains_m[layer], w_proj[layer]
        )
        start = residual
        residual = middle
        hidden = []
        for chunk in range(CHUNKS):
            residual, gated, slope, gate = run_mlp(offs, second, residual, w_mlp[layer][chunk])
            hidden.append((gated, links.swap(gated, 0), slope, gate))
        picks = (
            pick(links, picker_x, normed),
            pick(links, picker_y, normed),
            pick(links, picker_y, mixed),
            pick(links, picker_x, second),
            pick(links, picker_y, second),
        )
        kept.append((start, qkv, before, after, middle, hidden, picks))

    block_out = to_given(residual.astype(BF16))

    upstream_b = packed_cot * valid_query[:, None].astype(BF16)
    upstream = upstream_b.astype(F32)
    grads = [None] * LAYERS
    pipeline = Pipeline()
    for layer in reversed(range(LAYERS)):
        start, qkv, before, after, middle, hidden, picks = kept[layer]
        normed_x, normed_y, mixed_y, second_x, second_y = picks
        upstream_x = pick(links, picker_x, upstream_b)
        found = {}
        carried = None
        for chunk in range(CHUNKS):
            gated, gated_far, slope, gate = hidden[chunk]
            if chunk < CHUNKS - 1:
                carried, input_grad, gate_grad = run_mlp_back(
                    offs, upstream_b, slope, gate, carried, w_mlp[layer][chunk]
                )
            else:
                middle_grad, middle_grad_b, mlp_term, input_grad, gate_grad = run_mlp_back_last(
                    offs, upstream_b, slope, gate, carried, upstream, middle, gains_m[layer],
                    w_mlp[layer][chunk],
                )
            input_far = links.swap(input_grad, 0)
            gate_far = links.swap(gate_grad, 0)
            parts = [
                Sum(
                    links,
                    [
                        (upstream_x, (gated, gated_far, 0, FF_CHUNK)),
                        (second_x, (gate_grad, gate_far, 0, FF_CHUNK)),
                    ],
                    bits_x,
                ),
                Sum(links, [(second_y, (input_grad, input_far, 0, FF_CHUNK))], bits_y),
            ]
            pipeline.advance()
            pipeline.add(
                Joint(links, parts), functools.partial(found.__setitem__, ("mlp", chunk))
            )
        middle_far = links.swap(middle_grad_b, 0)
        parts = [Sum(links, [(mixed_y, (middle_grad_b, middle_far, 0, features))], bits_y)]
        pipeline.advance()
        pipeline.add(Joint(links, parts), functools.partial(found.__setitem__, "proj"))
        query_grad, own_grad, rim_before, rim_after = run_attend_back(
            offs, middle_grad_b, qkv, before, after, seg_q_row, seg_k_col, cosine, sine, w_proj[layer]
        )
        arrived_first = shift(rim_after, True)
        arrived_last = shift(rim_before, False)
        joint_grad, upstream, upstream_b, attn_term = run_qkv_back(
            offs, query_grad, own_grad, arrived_first, arrived_last, cosine, sine, start,
            gains_a[layer], middle_grad, w_qkv[layer],
        )
        joint_far = links.swap(joint_grad, 0)
        split = 3 * features // 2
        parts = [
            Sum(links, [(normed_x, (joint_grad, joint_far, split, split))], bits_x),
            Sum(links, [(normed_y, (joint_grad, joint_far, 0, split))], bits_y),
        ]
        pipeline.advance()
        pipeline.add(Joint(links, parts), functools.partial(found.__setitem__, "qkv"))
        grads[layer] = (found, attn_term, mlp_term)
    token_grad = to_given(upstream_b)
    pipeline.finish()
    vectors = [grads[layer][1] for layer in range(LAYERS)]
    vectors += [grads[layer][2] for layer in range(LAYERS)]
    gain_sums = scatter_vectors(jnp.concatenate(vectors, axis=0), bits_x)

    def wide(found):
        parts = [found["mlp", chunk] for chunk in range(CHUNKS)]
        inputs = [part[:, 2 * FF_CHUNK :] for part in parts]
        gates = [part[:, FF_CHUNK : 2 * FF_CHUNK] for part in parts]
        return jnp.concatenate(
            [jnp.concatenate(half, axis=1)[:, :FF] for half in (inputs, gates)], axis=1
        )

    def narrow(found):
        parts = [found["mlp", chunk][:, :FF_CHUNK] for chunk in range(CHUNKS)]
        return jnp.concatenate(parts, axis=1)[:, :FF]

    def qkv_sum(found):
        split = 3 * features // 2
        return jnp.concatenate([found["qkv"][:, split:], found["qkv"][:, :split]], axis=1)

    founds = [grads[layer][0] for layer in range(LAYERS)]
    return (
        block_out[None],
        token_grad[None],
        gain_sums[:LAYERS],
        jnp.stack([qkv_sum(found) for found in founds]),
        jnp.stack([found["proj"] for found in founds]),
        gain_sums[LAYERS:],
        jnp.stack([wide(found) for found in founds]),
        jnp.stack([narrow(found) for found in founds]),
    )


def solution(mesh):
    in_specs = (
        P("fsdp", "seq", None),
        P("fsdp", "seq", None),
        P("fsdp", None),
        P("fsdp", None),
        P(None, "fsdp"),
        P(None, "fsdp", None),
        P(None, "fsdp", None),
        P(None, "fsdp"),
        P(None, "fsdp", None),
        P(None, "fsdp", None),
    )
    out_specs = (
        P("fsdp", "seq", None),
        P("fsdp", "seq", None),
        P(None, ("seq", "fsdp")),
        P(None, ("seq", "fsdp"), None),
        P(None, ("seq", "fsdp"), None),
        P(None, ("seq", "fsdp")),
        P(None, ("seq", "fsdp"), None),
        P(None, ("seq", "fsdp"), None),
    )
    return jax.shard_map(body, mesh=mesh, in_specs=in_specs, out_specs=out_specs, check_vma=False)
```

```python
import functools
import math

import jax
import jax.numpy as jnp
from jax import lax
from jax.experimental import pallas as pl
from jax.experimental.pallas import tpu as pltpu
from jax.sharding import PartitionSpec as P

HEADS = 16
HEAD_DIM = 64
FF = 2624
WINDOW = 128
BLOCK = 128
BLK_DEV = 2
LAYERS = 2

NEG = -1e30
EPS = 1e-05
THETA = 10000.0

AXES = ("seq", "fsdp")
LANES = 128
HALO = WINDOW // 2
SPLIT = (5, 8, 8)
FF_PAD = sum(SPLIT) * LANES
WIDTHS = tuple(blocks * LANES for blocks in SPLIT)
STARTS = tuple(sum(WIDTHS[:k]) for k in range(len(WIDTHS)))
CHUNKS = len(SPLIT)
TILES = 3
F32 = jnp.float32
BF16 = jnp.bfloat16
VMEM_LIMIT = 60 * 1024 * 1024
NT = (((1,), (1,)), ((), ()))
TN = (((0,), (0,)), ((), ()))


class Phases:
    def __init__(self):
        self.gate = ()
        self.made = []

    def next(self):
        self.gate = tuple(self.made)
        self.made = []

    def tie(self, value):
        return lax.optimization_barrier((value,) + self.gate)[0] if self.gate else value

    def keep(self, *values):
        self.made += values

    def route(self, value, axes, pairs):
        result = lax.ppermute(self.tie(value), axes, pairs)
        self.made.append(result)
        return result

    def swap(self, value, bit):
        count = lax.axis_size("seq") * lax.axis_size("fsdp")
        return self.route(value, AXES, [(i, i ^ (1 << bit)) for i in range(count)])

    def shift(self, value, up):
        pairs = [(i, i + 1) for i in range(lax.axis_size("seq") - 1)]
        if not up:
            pairs = [(b, a) for a, b in pairs]
        return self.route(value, "seq", pairs)


def flat_index():
    return lax.axis_index("seq") * lax.axis_size("fsdp") + lax.axis_index("fsdp")


class Weights:
    def __init__(self, flow, shard, sent):
        self.flow = flow
        self.shard = shard
        self.sent = sent

    def own(self):
        self.own_core = self.flow.swap(self.shard, 0)

    def over_x(self):
        self.far_x = self.flow.swap(self.sent, 1)

    def over_y(self):
        self.far_y = self.flow.swap(self.far_x, 2)

    def over_core(self):
        far = jnp.concatenate([self.far_x, self.flow.tie(self.far_y)], axis=0)
        self.pieces = (self.shard, far, self.own_core, self.flow.swap(far, 0))


def piece_order():
    quarter = lax.axis_index("fsdp")
    side = lax.axis_index("seq") % 2
    one = 1 - side
    order = []
    for core in (quarter, quarter ^ 1):
        order += [core * 2, core * 2 + 1, (core ^ 2) * 2 + side, (core ^ 2) * 2 + one]
    return jnp.stack(order).astype(jnp.int32)


def stage_bits(first_x):
    levels = lax.axis_size("seq").bit_length() - 1
    rest = [2 + level for level in range(1, levels)]
    return ([1, 2] if first_x else [2, 1]) + rest


def row_order(features, bits):
    order = [0] + bits
    per_device = features >> len(order)
    rows = jnp.arange(features, dtype=jnp.int32)
    place = rows // per_device
    owner = flat_index()
    for step, bit in enumerate(order):
        taken = (place >> (len(order) - 1 - step)) & 1
        owner = owner ^ (taken << bit)
    return owner * per_device + rows % per_device


def row_picker(features, bits):
    order = row_order(features, bits)
    grid = jnp.arange(features, dtype=jnp.int32)
    return (order[:, None] == grid[None, :]).astype(BF16)


def call(kernel, outs, scratch=(), smem=1, grid=None, in_specs=None, out_specs=None):
    params = dict(
        compiler_params=pltpu.CompilerParams(vmem_limit_bytes=VMEM_LIMIT),
        out_shape=outs,
        scratch_shapes=list(scratch),
        cost_estimate=pl.CostEstimate(
            flops=0, bytes_accessed=0, transcendentals=0
        ),
    )
    if grid is not None:
        params["grid"] = grid

    def run(*args):
        specs = in_specs
        if specs is None:
            specs = [pl.BlockSpec(memory_space=pltpu.SMEM)] * smem
            specs += [pl.BlockSpec(memory_space=pltpu.VMEM)] * (len(args) - smem)
        results = out_specs
        if results is None:
            results = jax.tree.map(lambda _: pl.BlockSpec(memory_space=pltpu.VMEM), outs)
        return pl.pallas_call(kernel, in_specs=specs, out_specs=results, **params)(*args)

    return run


def struct(shape, dtype):
    return jax.ShapeDtypeStruct(shape, dtype)


def to_pieces(offs, source, target):
    for k in range(source.shape[1] // LANES):
        start = pl.multiple_of(offs[k] * LANES, LANES)
        target[:, k * LANES : (k + 1) * LANES] = source[:, pl.ds(start, LANES)]


def from_pieces(offs, source, target):
    for k in range(source.shape[1] // LANES):
        start = pl.multiple_of(offs[k] * LANES, LANES)
        target[:, pl.ds(start, LANES)] = source[:, k * LANES : (k + 1) * LANES]


def joined(pieces, columns=slice(None)):
    return jnp.concatenate([piece[:, columns] for piece in pieces], axis=0)


def statistics(values):
    average = jnp.mean(values, axis=-1, keepdims=True)
    centred = values - average
    spread = jnp.mean(centred * centred, axis=-1, keepdims=True)
    rho = lax.rsqrt(spread + EPS)
    return centred, rho


def norm_pull(values, gain, grad):
    centred, rho = statistics(values)
    unit = centred * rho
    scaled = grad * gain
    mean_a = jnp.mean(scaled, axis=-1, keepdims=True)
    mean_b = jnp.mean(scaled * unit, axis=-1, keepdims=True)
    return rho * (scaled - mean_a - unit * mean_b), jnp.sum(grad * unit, axis=0, keepdims=True)


def turn_chunk(values, cosine, sine, sign):
    lane = lax.broadcasted_iota(jnp.int32, values.shape, 1)
    ahead = pltpu.roll(values, LANES - HEAD_DIM // 2, 1)
    behind = pltpu.roll(values, HEAD_DIM // 2, 1)
    turned = jnp.where(lane % HEAD_DIM < HEAD_DIM // 2, ahead, behind)
    if sign > 0:
        return values * cosine + turned * sine
    return values * cosine - turned * sine


def pack_one_kernel(side, first, own, sent):
    half = first.shape[1] // 2
    own[...] = first[0]
    sent[...] = first[0, pl.ds(pl.multiple_of(side[0] * half, half), half), :]


def pack_kernel(side, second, wide, narrow, *outs):
    half = wide.shape[1] // 2
    features = second.shape[2]
    outs[0][:, :features] = second[0]
    for chunk in range(CHUNKS):
        own = outs[2 * chunk]
        at = features if chunk == 0 else 0
        width = WIDTHS[chunk]
        start, stop = STARTS[chunk], min(STARTS[chunk] + width, FF)
        for array, base in ((narrow, 0), (wide, 0), (wide, FF)):
            if stop - start < width:
                own[:, at + width - LANES : at + width] = jnp.zeros((2 * half, LANES), BF16)
            own[:, at : at + stop - start] = array[0, :, base + start : base + stop]
            at += width
    for k in range(0, len(outs), 2):
        outs[k + 1][...] = outs[k][pl.ds(pl.multiple_of(side[0] * half, half), half), :]


def run_pack(side, arrays, layer):
    rows = arrays[0].shape[1]
    one = len(arrays) == 1
    features = arrays[0].shape[2]
    columns = [features + 3 * WIDTHS[0]] + [3 * width for width in WIDTHS[1:]]
    if one:
        columns = [features]
    outs = tuple(struct((height, width), BF16) for width in columns for height in (rows, rows // 2))
    flat = call(
        pack_one_kernel if one else pack_kernel,
        outs,
        grid=(1,),
        in_specs=[pl.BlockSpec(memory_space=pltpu.SMEM)]
        + [pl.BlockSpec((1,) + v.shape[1:], lambda j: (layer, 0, 0)) for v in arrays],
        out_specs=tuple(whole_spec(out.shape) for out in outs),
    )(side, *arrays)
    return [flat[k : k + 2] for k in range(0, len(flat), 2)]


def qkv_kernel(offs, x, gain, cosine, sine, p0, p1, p2, p3, out, normed, first, last, placed):
    step = pl.program_id(0)
    tokens = x.shape[0]

    @pl.when(step == 0)
    def _():
        centred, rho = statistics(x[...])
        normed[...] = (centred * rho * gain[...]).astype(BF16)
        to_pieces(offs, normed, placed)

    product = jnp.dot(
        placed[...], joined((p0, p1, p2, p3)), preferred_element_type=F32
    )

    @pl.when(step < 2)
    def _():
        for k in range(product.shape[1] // LANES):
            part = slice(k * LANES, (k + 1) * LANES)
            out[:, part] = turn_chunk(product[:, part], cosine[...], sine[...], 1).astype(BF16)

    @pl.when(step == 2)
    def _():
        out[...] = product.astype(BF16)

    first[...] = out[:HALO, :]
    last[...] = out[tokens - HALO :, :]


def piece_specs(rows, columns):
    return [pl.BlockSpec((rows, columns), lambda j: (0, j))] * 4


def proj_specs(rows, columns):
    return [pl.BlockSpec((rows, columns), lambda j: (0, 0))] * 4


def whole_spec(shape):
    return pl.BlockSpec(shape, lambda j: tuple(0 for _ in shape))


def run_qkv(offs, x, gain, cosine, sine, pieces):
    tokens, features = x.shape
    return call(
        qkv_kernel,
        (
            struct((tokens, 3 * features), BF16),
            struct((tokens, features), BF16),
            struct((HALO, 2 * features), BF16),
            struct((HALO, 2 * features), BF16),
        ),
        [pltpu.VMEM((tokens, features), BF16)],
        grid=(3,),
        in_specs=[pl.BlockSpec(memory_space=pltpu.SMEM)]
        + [whole_spec(v.shape) for v in (x, gain, cosine, sine)]
        + piece_specs(pieces[0].shape[0], features),
        out_specs=(
            pl.BlockSpec((tokens, features), lambda j: (0, j)),
            whole_spec((tokens, features)),
            pl.BlockSpec((HALO, features), lambda j: (0, jnp.maximum(j - 1, 0))),
            pl.BlockSpec((HALO, features), lambda j: (0, jnp.maximum(j - 1, 0))),
        ),
    )(offs, x, gain, cosine, sine, *pieces)


def extend(qkv, before, after, extended):
    tokens, features = qkv.shape[0], qkv.shape[1] // 3
    extended[:HALO, :] = before[...]
    extended[HALO : HALO + tokens, :] = qkv[:, features:]
    extended[HALO + tokens :, :] = after[...]


def attend_kernel(
    offs, qkv, before, after, seg_q, seg_k, x, gain,
    p0, p1, p2, p3, mixed, middle, second, extended, placed,
):
    tokens, features = x.shape
    extend(qkv, before, after, extended)
    scale = 1.0 / math.sqrt(HEAD_DIM)
    span = BLOCK + 2 * HALO
    row = lax.broadcasted_iota(jnp.int32, (BLOCK, span), 0)
    col = lax.broadcasted_iota(jnp.int32, (BLOCK, span), 1)
    near = (col >= row) & (col - row <= 2 * HALO)
    low = lax.broadcasted_iota(jnp.int32, (BLOCK, LANES), 1) < HEAD_DIM
    bias = []
    for block in range(tokens // BLOCK):
        base = block * BLOCK
        same = seg_q[base : base + BLOCK, :] == seg_k[:, base : base + span]
        bias.append(jnp.where(near & same, 0.0, NEG))

    def pair(index, carry):
        lanes = pl.ds(pl.multiple_of(index * LANES, LANES), LANES)
        value_lanes = pl.ds(pl.multiple_of(features + index * LANES, LANES), LANES)
        for block in range(tokens // BLOCK):
            base = block * BLOCK
            queries = qkv[base : base + BLOCK, lanes]
            keys = extended[base : base + span, lanes]
            values = extended[base : base + span, value_lanes]
            parts = []
            for keep in (low, ~low):
                chosen = jnp.where(keep, queries, jnp.zeros_like(queries))
                raw = lax.dot_general(chosen, keys, NT, preferred_element_type=F32)
                scores = raw * scale + bias[block]
                expo = jnp.exp(scores - jnp.max(scores, axis=-1, keepdims=True))
                probs = expo * (1.0 / jnp.sum(expo, axis=-1, keepdims=True))
                parts.append(jnp.dot(probs.astype(BF16), values, preferred_element_type=F32))
            mixed[base : base + BLOCK, lanes] = jnp.where(low, parts[0], parts[1]).astype(BF16)
        return carry

    lax.fori_loop(0, features // LANES, pair, 0)
    to_pieces(offs, mixed, placed)
    total = x[...] + jnp.dot(
        placed[...], joined((p0, p1, p2, p3)), preferred_element_type=F32
    )
    middle[...] = total
    centred, rho = statistics(total)
    second[...] = (centred * rho * gain[...]).astype(BF16)


def run_attend(offs, qkv, before, after, seg_q, seg_k, x, gain, pieces):
    tokens, features = x.shape
    return call(
        attend_kernel,
        (
            struct((tokens, features), BF16),
            struct((tokens, features), F32),
            struct((tokens, features), BF16),
        ),
        [
            pltpu.VMEM((tokens + 2 * HALO, 2 * features), BF16),
            pltpu.VMEM((tokens, features), BF16),
        ],
        grid=(1,),
        in_specs=[pl.BlockSpec(memory_space=pltpu.SMEM)]
        + [whole_spec(v.shape) for v in (qkv, before, after, seg_q, seg_k, x, gain)]
        + proj_specs(pieces[0].shape[0], features),
        out_specs=(whole_spec((tokens, features)),) * 3,
    )(offs, qkv, before, after, seg_q, seg_k, x, gain, *pieces)


def chunk_parts(pieces, base, width):
    return [
        joined(pieces, slice(base + k * width, base + (k + 1) * width)) for k in range(3)
    ]


def mlp_kernel(
    base, width, offs, second, carried, p0, p1, p2, p3, total, gated, slope, gate, placed, part
):
    output, first, other = chunk_parts((p0, p1, p2, p3), base, width)
    to_pieces(offs, second, placed)
    source = placed[...]
    hidden = jnp.dot(source, first, preferred_element_type=F32)
    factor = jnp.dot(source, other, preferred_element_type=F32)
    normal = 0.5 * (1.0 + lax.erf(hidden * math.sqrt(0.5)))
    density = jnp.exp(-0.5 * hidden * hidden) * (1.0 / math.sqrt(2.0 * math.pi))
    active = hidden * normal
    product = (active * factor).astype(BF16)
    gated[...] = product
    slope[...] = ((normal + hidden * density) * factor).astype(BF16)
    gate[...] = active.astype(BF16)
    part[...] = lax.dot_general(product, output, NT, preferred_element_type=F32)
    for k in range(part.shape[1] // LANES):
        lanes = pl.ds(pl.multiple_of(offs[k] * LANES, LANES), LANES)
        total[:, lanes] = carried[:, lanes] + part[:, k * LANES : (k + 1) * LANES]


def run_mlp(offs, second, carried, pieces, chunk):
    tokens, features = second.shape
    width = WIDTHS[chunk]
    base = pieces[0].shape[1] - 3 * width
    hidden = struct((tokens, width), BF16)
    return call(
        functools.partial(mlp_kernel, base, width),
        (struct((tokens, features), F32), hidden, hidden, hidden),
        [pltpu.VMEM((tokens, features), BF16), pltpu.VMEM((tokens, features), F32)],
    )(offs, second, carried, *pieces)


def mlp_pull(base, width, offs, upstream, gated, slope, gate, pieces, right, placed):
    output, first, other = chunk_parts(pieces, base, width)
    to_pieces(offs, upstream, placed)
    gated_grad = jnp.dot(placed[...], output, preferred_element_type=F32)
    input_grad = (slope[...].astype(F32) * gated_grad).astype(BF16)
    gate_grad = (gate[...].astype(F32) * gated_grad).astype(BF16)
    store(right, 0, gated[...])
    store(right, width, input_grad)
    store(right, 2 * width, gate_grad)
    return lax.dot_general(input_grad, first, NT, preferred_element_type=F32) + lax.dot_general(
        gate_grad, other, NT, preferred_element_type=F32
    )


def store(target, at, value):
    target[:, at : at + value.shape[1]] = value


def mlp_back_kernel(
    base, width, first, offs, upstream, gated, slope, gate, carried, p0, p1, p2, p3,
    total, right, placed,
):
    part = mlp_pull(
        base, width, offs, upstream, gated, slope, gate, (p0, p1, p2, p3), right, placed
    )
    total[...] = part if first else carried[...] + part


def mlp_back_last_kernel(
    base, width, offs, upstream, gated, slope, gate, carried, residual_grad, middle, gain,
    p0, p1, p2, p3, middle_grad, middle_grad_b, gain_grad, right, placed, sums, ordered,
):
    part = mlp_pull(
        base, width, offs, upstream, gated, slope, gate, (p0, p1, p2, p3), right, placed
    )
    sums[...] = carried[...] + part
    from_pieces(offs, sums, ordered)
    pulled, gains = norm_pull(middle[...], gain[...], ordered[...])
    result = residual_grad[...] + pulled
    middle_grad[...] = result
    middle_grad_b[...] = result.astype(BF16)
    gain_grad[...] = gains
    at = 3 * width
    store(right, at, result.astype(BF16))
    at += result.shape[1]
    rest = right.shape[1] - at
    if rest:
        store(right, at, jnp.zeros((result.shape[0], rest), BF16))


def run_mlp_back(offs, upstream, hidden, carried, pieces, chunk):
    tokens, features = upstream.shape
    width = WIDTHS[chunk]
    base = pieces[0].shape[1] - 3 * width
    right = struct((tokens, 3 * features), BF16)
    first = carried is None
    if first:
        carried = jnp.zeros((8, LANES), F32)
    return call(
        functools.partial(mlp_back_kernel, base, width, first),
        (struct((tokens, features), F32), right),
        [pltpu.VMEM((tokens, features), BF16)],
    )(offs, upstream, *hidden, carried, *pieces)


def run_mlp_back_last(offs, upstream, hidden, carried, residual_grad, middle, gain, pieces, chunk):
    tokens, features = upstream.shape
    width = WIDTHS[chunk]
    base = pieces[0].shape[1] - 3 * width
    right = struct((tokens, 3 * features), BF16)
    return call(
        functools.partial(mlp_back_last_kernel, base, width),
        (
            struct((tokens, features), F32),
            struct((tokens, features), BF16),
            struct((1, features), F32),
            right,
        ),
        [
            pltpu.VMEM((tokens, features), BF16),
            pltpu.VMEM((tokens, features), F32),
            pltpu.VMEM((tokens, features), F32),
        ],
    )(offs, upstream, *hidden, carried, residual_grad, middle, gain, *pieces)


def attend_back_kernel(
    offs, middle_grad, qkv, before, after, seg_q, seg_k, cosine, sine, p0, p1, p2, p3,
    query_grad, own_grad, rim_before, rim_after, extended, mixed_grad, extended_grad,
):
    tokens, features = middle_grad.shape
    extend(qkv, before, after, extended)
    placed = lax.dot_general(
        middle_grad[...], joined((p0, p1, p2, p3)), NT, preferred_element_type=F32
    ).astype(BF16)
    for k in range(features // LANES):
        lanes = pl.ds(pl.multiple_of(offs[k] * LANES, LANES), LANES)
        mixed_grad[:, lanes] = placed[:, k * LANES : (k + 1) * LANES]
    scale = 1.0 / math.sqrt(HEAD_DIM)
    span = BLOCK + 2 * HALO
    row = lax.broadcasted_iota(jnp.int32, (span, BLOCK), 1)
    col = lax.broadcasted_iota(jnp.int32, (span, BLOCK), 0)
    near = (col >= row) & (col - row <= 2 * HALO)
    low = lax.broadcasted_iota(jnp.int32, (BLOCK, LANES), 1) < HEAD_DIM
    bias = []
    for block in range(tokens // BLOCK):
        base = block * BLOCK
        same = seg_q[:, base : base + BLOCK] == seg_k[base : base + span, :]
        bias.append(jnp.where(near & same, 0.0, NEG))

    def pair(index, carry):
        lanes = pl.ds(pl.multiple_of(index * LANES, LANES), LANES)
        value_lanes = pl.ds(pl.multiple_of(features + index * LANES, LANES), LANES)
        key_sums = []
        value_sums = []
        for block in range(tokens // BLOCK):
            base = block * BLOCK
            here = slice(base, base + BLOCK)
            queries = qkv[here, lanes]
            grads = mixed_grad[here, lanes]
            keys = extended[base : base + span, lanes]
            values = extended[base : base + span, value_lanes]
            key_sum = None
            value_sum = None
            query_parts = []
            for keep in (low, ~low):
                chosen = jnp.where(keep, queries, jnp.zeros_like(queries))
                chosen_grad = jnp.where(keep, grads, jnp.zeros_like(grads))
                raw = lax.dot_general(keys, chosen, NT, preferred_element_type=F32)
                scores = raw * scale + bias[block]
                expo = jnp.exp(scores - jnp.max(scores, axis=0, keepdims=True))
                probs = expo * (1.0 / jnp.sum(expo, axis=0, keepdims=True))
                prob_grad = lax.dot_general(values, chosen_grad, NT, preferred_element_type=F32)
                delta = jnp.sum(prob_grad * probs, axis=0, keepdims=True)
                score_grad = (probs * (prob_grad - delta) * scale).astype(BF16)
                query_parts.append(
                    lax.dot_general(score_grad, keys, TN, preferred_element_type=F32)
                )
                to_keys = jnp.dot(score_grad, chosen, preferred_element_type=F32)
                to_values = jnp.dot(
                    probs.astype(BF16), chosen_grad, preferred_element_type=F32
                )
                key_sum = to_keys if key_sum is None else key_sum + to_keys
                value_sum = to_values if value_sum is None else value_sum + to_values
            joint = jnp.where(low, query_parts[0], query_parts[1])
            query_grad[here, lanes] = turn_chunk(
                joint, cosine[here, :], sine[here, :], -1
            ).astype(BF16)
            key_sums.append(key_sum)
            value_sums.append(value_sum)
        for sums, place in ((key_sums, lanes), (value_sums, value_lanes)):
            over = 2 * HALO
            extended_grad[:BLOCK, place] = sums[0][:BLOCK]
            extended_grad[BLOCK : BLOCK + over, place] = sums[0][BLOCK:] + sums[1][:over]
            extended_grad[BLOCK + over :, place] = sums[1][over:]
        return carry

    lax.fori_loop(0, features // LANES, pair, 0)
    rim_before[...] = extended_grad[:HALO, :].astype(BF16)
    own_grad[...] = extended_grad[HALO : HALO + tokens, :]
    rim_after[...] = extended_grad[HALO + tokens :, :].astype(BF16)


def run_attend_back(offs, middle_grad, qkv, before, after, seg_q, seg_k, cosine, sine, pieces):
    tokens, features = middle_grad.shape
    rim = struct((HALO, 2 * features), BF16)
    return call(
        attend_back_kernel,
        (struct((tokens, features), BF16), struct((tokens, 2 * features), F32), rim, rim),
        [
            pltpu.VMEM((tokens + 2 * HALO, 2 * features), BF16),
            pltpu.VMEM((tokens, features), BF16),
            pltpu.VMEM((tokens + 2 * HALO, 2 * features), F32),
        ],
        grid=(1,),
        in_specs=[pl.BlockSpec(memory_space=pltpu.SMEM)]
        + [
            whole_spec(v.shape)
            for v in (middle_grad, qkv, before, after, seg_q, seg_k, cosine, sine)
        ]
        + proj_specs(pieces[0].shape[0], features),
        out_specs=(
            whole_spec((tokens, features)),
            whole_spec((tokens, 2 * features)),
            whole_spec((HALO, 2 * features)),
            whole_spec((HALO, 2 * features)),
        ),
    )(offs, middle_grad, qkv, before, after, seg_q, seg_k, cosine, sine, *pieces)


def qkv_back_kernel(
    offs, query_grad, own_grad, arrived_first, arrived_last, cosine, sine, x, gain, middle_grad,
    p0, p1, p2, p3, right, upstream, upstream_b, gain_grad, sums, ordered,
):
    step = pl.program_id(0)
    tokens, features = x.shape
    for part in range(3):

        @pl.when(step == part)
        def _():
            if part == 0:
                joint = query_grad[...]
            else:
                chunks = []
                for k in range(features // LANES):
                    at = (part - 1) * features + k * LANES
                    there = slice(at, at + LANES)
                    rows = [
                        own_grad[:HALO, there] + arrived_first[:, there].astype(F32),
                        own_grad[HALO : tokens - HALO, there],
                        own_grad[tokens - HALO :, there] + arrived_last[:, there].astype(F32),
                    ]
                    grads = jnp.concatenate(rows, axis=0)
                    if part == 1:
                        grads = turn_chunk(grads, cosine[...], sine[...], -1)
                    chunks.append(grads.astype(BF16))
                joint = jnp.concatenate(chunks, axis=1)
            store(right, part * features, joint)
            product = lax.dot_general(
                joint, joined((p0, p1, p2, p3)), NT, preferred_element_type=F32
            )
            sums[...] = product if part == 0 else sums[...] + product

    @pl.when(step == 2)
    def _():
        from_pieces(offs, sums, ordered)
        pulled, gains = norm_pull(x[...], gain[...], ordered[...])
        result = middle_grad[...] + pulled
        upstream[...] = result
        upstream_b[...] = result.astype(BF16)
        gain_grad[...] = gains


def run_qkv_back(
    offs, query_grad, own_grad, arrived_first, arrived_last, cosine, sine, x, gain, middle_grad, pieces
):
    tokens, features = x.shape
    whole = (query_grad, own_grad, arrived_first, arrived_last, cosine, sine, x, gain, middle_grad)
    outs = (
        struct((tokens, 3 * features), BF16),
        struct((tokens, features), F32),
        struct((tokens, features), BF16),
        struct((1, features), F32),
    )
    return call(
        qkv_back_kernel,
        outs,
        [pltpu.VMEM((tokens, features), F32), pltpu.VMEM((tokens, features), F32)],
        grid=(3,),
        in_specs=[pl.BlockSpec(memory_space=pltpu.SMEM)]
        + [whole_spec(v.shape) for v in whole]
        + piece_specs(pieces[0].shape[0], features),
        out_specs=tuple(whole_spec(out.shape) for out in outs),
    )(offs, *whole, *pieces)


def pick_kernel(which, *refs):
    pickers, lefts, (mine, theirs) = refs[:2], refs[2:-2], refs[-2:]
    half = pickers[0].shape[0] // 2
    for k, (picker, left) in enumerate(which):
        rows = lax.dot_general(
            pickers[picker][...], lefts[left][...], NT, preferred_element_type=F32
        ).astype(BF16)
        mine[k * half : (k + 1) * half, :] = rows[:half]
        theirs[k * half : (k + 1) * half, :] = rows[half:]


def run_pick(pickers, lefts, which):
    rows = len(which) * pickers[0].shape[0] // 2
    out = struct((rows, lefts[0].shape[0]), BF16)
    return call(functools.partial(pick_kernel, which), (out, out), smem=0)(*pickers, *lefts)


def exchange_kernel(plan, *refs):
    segments, stages = plan
    refs = list(refs)
    take = lambda count: [refs.pop(0) for _ in range(count)]
    adding, ending, far_ending, finishing = stages
    if segments:
        rights, rights_far = take(2), take(2)
        lefts = [take(2) for _ in segments]
    kept = take(2) if adding else None
    last = take(2) if ending else None
    come = take(2) if adding or ending else None
    near_pair = take(2) if far_ending else None
    far_pair = take(2) if finishing else None
    keep = take(2) if segments else None
    stay = take(2) if adding else None
    send = take(2) if segments or adding else None
    near_out = take(2) if ending else None
    far_out = take(2) if far_ending else None
    result = take(1)[0] if finishing else None

    def added(pair, rows, columns):
        return pair[0][rows, columns].astype(F32) + pair[1][rows, columns].astype(F32)

    def body(step):
        everything = slice(None)
        top = 0
        if segments:
            half, tile = keep[0].shape
            for (path, start, stop), (left, left_far) in zip(segments, lefts):
                low, high = max(start - step * tile, 0), min(stop - step * tile, tile)
                if low >= high:
                    continue
                columns = slice(low, high)
                total = jnp.dot(
                    jnp.concatenate([left[...], left_far[...]], axis=1),
                    jnp.concatenate(
                        [rights[path][:, columns], rights_far[path][:, columns]], axis=0
                    ),
                    preferred_element_type=F32,
                ).astype(BF16)
                keep[path][:, columns] = total[:half]
                send[path][:half, columns] = total[half:]
            top = half
        came = 0
        if adding:
            rows, tile = kept[0].shape
            half = rows // 2
            for path in range(2):
                total = kept[path][...].astype(F32) + come[path][:rows, :].astype(F32)
                stay[path][...] = total[:half].astype(BF16)
                send[1 - path][top : top + half, :] = total[half:].astype(BF16)
            came = rows
        if ending:
            rows, tile = last[0].shape
            half = rows // 2
            for path in range(2):
                at = (path * TILES + step) * tile
                total = last[path][...].astype(F32) + come[1 - path][
                    came : came + rows, :
                ].astype(F32)
                near_out[0][:, at : at + tile] = total[:half].astype(BF16)
                near_out[1][:, at : at + tile] = total[half:].astype(BF16)
        if step == 0 and far_ending:
            half = near_pair[0].shape[0] // 2
            far_out[0][...] = added(near_pair, slice(0, half), everything).astype(BF16)
            far_out[1][...] = added(near_pair, slice(half, 2 * half), everything).astype(BF16)
        if step == 0 and finishing:
            result[...] = added(far_pair, everything, everything).astype(result.dtype)

    for step in range(TILES):
        pl.when(pl.program_id(0) == step)(functools.partial(body, step))


class Exchange:
    def __init__(self, flow, rows, width, bits):
        self.flow = flow
        self.rows = rows
        self.width = width
        self.near, self.far = bits[:2]
        self.dtype = F32 if len(bits) == 2 else BF16
        self.kept = self.last = self.come = self.near_pair = self.far_pair = None

    def busy(self):
        return any((self.kept, self.last, self.near_pair, self.far_pair))

    def step(self, rights=None, segments=()):
        flow, rows, width = self.flow, self.rows, self.width
        tile = width // TILES
        args, specs, outs, out_specs = [], [], [], []

        def tiled(shape):
            return pl.BlockSpec((shape[0], tile), lambda j: (0, j))

        def give(pair, spec):
            if pair:
                args.extend(pair)
                specs.extend(spec(value.shape) for value in pair)

        def want(height, columns, spec, count=2, dtype=BF16):
            outs.extend([struct((height, columns), dtype)] * count)
            out_specs.extend([spec((height, columns))] * count)

        for right in rights or ():
            args += [right, right]
            block = (right.shape[0], tile)
            specs += [pl.BlockSpec(block, lambda j: (0, j))]
            specs += [pl.BlockSpec(block, lambda j: (0, TILES + j))]
        for _, _, _, left, place in segments:
            args += left
            specs += [pl.BlockSpec((rows, left[0].shape[1]), lambda j, at=place: (at, 0))] * 2
        give(self.kept, tiled)
        give(self.last, tiled)
        give(self.come if self.kept or self.last else None, tiled)
        give(self.near_pair, whole_spec)
        give(self.far_pair, whole_spec)
        height = 0
        if segments:
            want(rows // 2, width, tiled)
            height += rows // 2
        if self.kept:
            want(rows // 4, width, tiled)
            height += rows // 4
        if height:
            want(height, width, tiled)
        if self.last:
            want(rows // 8, 2 * width, whole_spec)
        if self.near_pair:
            want(rows // 16, 2 * width, whole_spec)
        if self.far_pair:
            want(rows // 16, 2 * width, whole_spec, 1, self.dtype)
        stages = tuple(map(bool, (self.kept, self.last, self.near_pair, self.far_pair)))
        plan = (
            tuple((path, start - path * width, stop - path * width) for path, start, stop, _, _ in segments),
            stages,
        )
        args[0] = flow.tie(args[0])
        results = list(
            call(
                functools.partial(exchange_kernel, plan),
                tuple(outs),
                grid=(TILES,),
                in_specs=specs,
                out_specs=tuple(out_specs),
            )(*args)
        )

        def got(wanted):
            return [results.pop(0), results.pop(0)] if wanted else None

        keep, stay, send = got(segments), got(self.kept), got(height)
        near, far = got(self.last), got(self.near_pair)
        result = results.pop(0) if self.far_pair else None
        self.kept, self.last = keep, stay
        self.come = send and [flow.swap(value, 1 + path) for path, value in enumerate(send)]
        self.near_pair = near and [near[0], flow.swap(near[1], self.near)]
        self.far_pair = far and [far[0], flow.swap(far[1], self.far)]
        return result


class Ending:
    def __init__(self, flow, value, bits, deliver):
        self.flow = flow
        self.bits = list(bits)
        self.deliver = deliver
        self.keep = value
        self.come = None

    def step(self):
        if self.come is not None:
            self.keep = self.keep.astype(F32) + self.flow.tie(self.come).astype(F32)
        if not self.bits:
            self.deliver(self.keep)
            return False
        half = self.keep.shape[0] // 2
        send = self.keep[half:].astype(BF16)
        self.keep = self.keep[:half].astype(BF16)
        self.come = self.flow.swap(send, self.bits.pop(0))
        return True


def rope_tables(position):
    inverse = jnp.power(THETA, -jnp.arange(0, HEAD_DIM, 2, dtype=F32) / HEAD_DIM)
    angles = position[:, None] * inverse[None, :]
    cosine, sine = jnp.cos(angles), jnp.sin(angles)
    return (
        jnp.concatenate([cosine, cosine, cosine, cosine], axis=-1),
        jnp.concatenate([-sine, sine, -sine, sine], axis=-1),
    )


def layout(positions, lengths, total):
    count = lengths.shape[0]
    blocks = (lengths + BLOCK - 1) // BLOCK
    first = (jnp.cumsum(blocks) - blocks) * BLOCK
    owner = jnp.sum((positions[:, None] >= first[None, :]).astype(jnp.int32), axis=1) - 1
    table = owner[:, None] == jnp.arange(count, dtype=jnp.int32)[None, :]
    start = jnp.sum(jnp.where(table, first[None, :], 0), axis=1)
    span = jnp.sum(jnp.where(table, lengths[None, :], 0), axis=1)
    local = positions - start
    inside = (positions >= 0) & (positions < total)
    valid = inside & (local < span)
    segment = jnp.where(inside, jnp.where(valid, owner, owner + count), -1)
    return (segment, local, valid)


def body(
    tokens,
    cotangent,
    lengths,
    block_perm,
    attn_gain,
    qkv_weight,
    proj_weight,
    mlp_gain,
    wide_weight,
    narrow_weight,
):
    flow = Phases()
    seq_index = lax.axis_index("seq")
    seq_count = lax.axis_size("seq")
    levels = seq_count.bit_length() - 1
    tok_dev = tokens.shape[1]
    features = tokens.shape[2]
    block_rows = tok_dev // BLK_DEV
    order_map = block_perm[0]
    target = order_map[0::BLK_DEV] // BLK_DEV
    source = jnp.arange(seq_count, dtype=jnp.int32)

    def holder(bit_level):
        low_mask = (1 << bit_level) - 1
        place = jnp.bitwise_or(
            jnp.bitwise_and(target, low_mask), jnp.bitwise_and(source, ~low_mask)
        )
        return jnp.sum(jnp.where(place == seq_index, source, 0))

    home_index = holder(levels)
    slot_of = lax.dynamic_slice_in_dim(order_map, home_index * BLK_DEV, BLK_DEV) % BLK_DEV
    crossed = slot_of[0] == 1

    def crossing(rows):
        turned = jnp.concatenate([rows[block_rows:], rows[:block_rows]], axis=0)
        return jnp.where(crossed, turned, rows)

    def crossed_over(bit_level, given):
        payload = holder(bit_level + 1 if given else bit_level)
        if not given:
            payload = jnp.sum(jnp.where(source == payload, target, 0))
        flips = jnp.right_shift(jnp.bitwise_xor(seq_index, payload), bit_level)
        return jnp.bitwise_and(flips, 1) == 1

    class Route:
        def __init__(self, rows, given):
            self.rows = crossing(rows) if given else rows
            self.given = given
            self.levels = list(range(levels))
            if given:
                self.levels.reverse()
            self.arrived = None
            self.settled = False

        def step(self):
            if self.arrived is not None:
                self.rows = jnp.where(
                    crossed_over(self.level, self.given), flow.tie(self.arrived), self.rows
                )
                self.arrived = None
            if self.levels:
                self.level = self.levels.pop(0)
                self.arrived = flow.swap(self.rows, 2 + self.level)
                return True
            if not self.given and not self.settled:
                self.rows = crossing(self.rows)
            self.settled = True
            return False

        def finish(self):
            while self.step():
                flow.next()
            return self.rows

    total = seq_count * tok_dev
    own_place = seq_index * tok_dev + jnp.arange(tok_dev, dtype=jnp.int32)
    key_place = seq_index * tok_dev - HALO + jnp.arange(tok_dev + 2 * HALO, dtype=jnp.int32)
    seg_query, local_query, valid_query = layout(own_place, lengths[0], total)
    seg_key, _, _ = layout(key_place, lengths[0], total)
    cosine, sine = rope_tables(local_query.astype(F32))
    seg_q_col, seg_q_row = seg_query[:, None], seg_query[None, :]
    seg_k_col, seg_k_row = seg_key[:, None], seg_key[None, :]
    offs = piece_order()
    bits_x, bits_y = stage_bits(True), stage_bits(False)
    picker_x, picker_y = row_picker(features, bits_x), row_picker(features, bits_y)

    gains = jnp.concatenate([attn_gain, mlp_gain], axis=0)
    gains = lax.all_gather(gains, "fsdp", axis=1, tiled=True).astype(F32)
    gains_a = [gains[layer : layer + 1] for layer in range(LAYERS)]
    gains_m = [gains[LAYERS + layer : LAYERS + layer + 1] for layer in range(LAYERS)]

    side = (seq_index % 2).astype(jnp.int32).reshape(1)
    arrays = (proj_weight, wide_weight, narrow_weight)
    items = []
    for layer in range(LAYERS):
        packs = run_pack(side, (qkv_weight,), layer) + run_pack(side, arrays, layer)
        items += [Weights(flow, *pack) for pack in packs]
    per_layer = len(items) // LAYERS
    tok_route, cot_route = Route(tokens[0], False), Route(cotangent[0], False)

    first_use = 3
    owns = {0: (0,), 1: (1, 2), 2: (3,), 4: (4, 5), 5: (6,), 6: (7,)}
    phase = 0

    def transfers():
        if phase < len(items):
            items[phase].over_x()
        if 0 <= phase - 1 < len(items):
            items[phase - 1].over_y()
        if 0 <= phase - 2 < len(items):
            items[phase - 2].over_core()
        for place in owns.get(phase, ()):
            items[place].own()

    flow.keep(gains)
    while phase < first_use or tok_route.levels:
        transfers()
        tok_route.step()
        if phase < 2:
            cot_route.step()
        if phase == 0:
            flow.keep(*(item.shard for item in items[1:]))
        phase += 1
        flow.next()
    tok_route.step()
    residual = tok_route.rows.astype(F32)
    kept = []
    for layer in range(LAYERS):
        base = layer * per_layer
        transfers()
        qkv, normed, edge_first, edge_last = run_qkv(
            offs, flow.tie(residual), gains_a[layer], cosine, sine, items[base].pieces
        )
        flow.keep(normed)
        before = flow.shift(edge_last, True)
        after = flow.shift(edge_first, False)
        phase += 1
        flow.next()
        transfers()
        if layer and kept[-1][-1] is None:
            kept[-1][-1] = (mine, flow.swap(theirs, 0))
        start = residual
        mixed, middle, second = run_attend(
            offs, flow.tie(qkv), before, after, seg_q_col, seg_k_row, residual, gains_m[layer],
            items[base + 1].pieces,
        )
        residual = middle
        hidden = []
        for chunk in range(CHUNKS):
            if chunk:
                phase += 1
                flow.next()
                transfers()
                if chunk == 1 and layer == 0:
                    cot_route.step()
            residual, gated, slope, gate = run_mlp(
                offs, second, flow.tie(residual), items[base + 1 + chunk].pieces, chunk
            )
            flow.keep(residual, gated)
            hidden.append((gated, slope, gate))
            if chunk == 1:
                lefts = (normed, mixed, second)
                which = ((0, 0), (1, 0), (1, 1), (0, 2), (1, 2))
                mine, theirs = run_pick((picker_x, picker_y), lefts, which)
                flow.keep(theirs)
        picks = None
        if layer == LAYERS - 1:
            flow.next()
            picks = (mine, flow.swap(theirs, 0))
        kept.append([start, qkv, before, after, middle, hidden, picks])
        phase += 1
        flow.next()

    upstream_b = cot_route.finish() * valid_query[:, None].astype(BF16)
    upstream = upstream_b.astype(F32)
    out_route = Route(residual.astype(BF16), True)

    late = bits_x[2:]
    exchange = Exchange(flow, features // 2, 3 * features // 2, late)
    endings = []
    sums = {}
    count = 0
    width = 3 * features // 2

    def settle(done):
        nonlocal count
        if done is None:
            return
        deliver = functools.partial(sums.__setitem__, count)
        count += 1
        if len(late) > 2:
            endings.append(Ending(flow, done, late[2:], deliver))
        else:
            deliver(done)

    def step_endings():
        for item in list(endings):
            if not item.step():
                endings.remove(item)

    def group(right, parts):
        segments = []
        at = 0
        for columns, lefts in parts:
            for path in range(2):
                low = max(at, path * width)
                high = min(at + columns, (path + 1) * width)
                if low < high:
                    segments.append((path, low, high, lefts[path][:2], lefts[path][2]))
            at += columns
        return list(right), tuple(segments)

    terms = [None] * LAYERS
    made, ready = None, None

    def backward_phase():
        nonlocal made, ready
        flow.next()
        moving = bool(made or ready or exchange.busy())
        if ready or exchange.busy():
            settle(exchange.step(*(group(*ready) if ready else ())))
        ready = None
        if made:
            right, parts = made
            ready = ((right, flow.swap(right, 0)), parts)
        made = None
        step_endings()
        return moving

    for layer in reversed(range(LAYERS)):
        start, qkv, before, after, middle, hidden, picks = kept[layer]
        base = layer * per_layer
        normed_x, normed_y, mixed_y, second_x, second_y = (picks + (row,) for row in range(5))
        carried = None
        upstream_left = None
        for chunk in reversed(range(CHUNKS)):
            if layer < LAYERS - 1 or chunk < CHUNKS - 1:
                backward_phase()
            pieces = items[base + 1 + chunk].pieces
            if upstream_left is None:
                mine, theirs = run_pick(
                    (picker_x, picker_y), (flow.tie(upstream_b),), ((0, 0), (1, 0))
                )
                flow.keep(theirs)
                upstream_left = []
            elif not upstream_left:
                far = flow.swap(theirs, 0)
                upstream_left += [(mine, far, path) for path in range(2)]
            if layer == LAYERS - 1 and chunk < CHUNKS - 1:
                out_route.step()
            args = (offs, flow.tie(upstream_b), hidden[chunk], carried)
            columns = WIDTHS[chunk]
            parts = [
                (columns, upstream_left),
                (2 * columns, (second_x, second_y)),
            ]
            if chunk:
                carried, right = run_mlp_back(*args, pieces, chunk)
                flow.keep(carried)
            else:
                middle_grad, middle_grad_b, mlp_term, right = run_mlp_back_last(
                    *args, upstream, middle, gains_m[layer], pieces, chunk
                )
                parts.append((2 * width - 3 * columns, (None, mixed_y)))
                query_grad, own_grad, rim_before, rim_after = run_attend_back(
                    offs, middle_grad_b, qkv, before, after, seg_q_row, seg_k_col, cosine, sine, pieces
                )
                flow.keep(query_grad, own_grad)
                arrived_first = flow.shift(rim_after, True)
                arrived_last = flow.shift(rim_before, False)
            flow.keep(right)
            made = (right, parts)
        backward_phase()
        right, upstream, upstream_b, attn_term = run_qkv_back(
            offs, flow.tie(query_grad), own_grad, arrived_first, arrived_last, cosine, sine, start,
            gains_a[layer], middle_grad, items[base].pieces,
        )
        flow.keep(upstream_b, right)
        made = (right, [(2 * width, (normed_x, normed_y))])
        terms[layer] = (attn_term, mlp_term)
    grad_route = Route(upstream_b, True)
    vectors = [terms[layer][0] for layer in range(LAYERS)]
    vectors += [terms[layer][1] for layer in range(LAYERS)]
    backward_phase()
    grad_route.step()
    gain_sums = lax.dot_general(
        flow.tie(jnp.concatenate(vectors, axis=0)), picker_x.astype(F32), NT, precision=lax.Precision.HIGHEST
    )
    gain_bits = [0] + list(bits_x)
    while backward_phase() or endings or gain_bits:
        if not grad_route.step():
            out_route.step()
        for bit in gain_bits[: 1 if len(gain_bits) > 2 else 2]:
            half = gain_sums.shape[1] // 2
            gain_sums = gain_sums[:, :half] + flow.swap(gain_sums[:, half:], bit)
        gain_bits = gain_bits[1 if len(gain_bits) > 2 else 2 :]
    block_out, token_grad = out_route.finish(), grad_route.finish()

    def pieces_of(layer):
        at = per_layer * (LAYERS - 1 - layer)
        parts = {chunk: sums[at + CHUNKS - 1 - chunk] for chunk in range(CHUNKS)}
        return parts, sums[at + CHUNKS]

    def hidden_sum(parts, role):
        columns = [
            parts[chunk][:, role * WIDTHS[chunk] : (role + 1) * WIDTHS[chunk]]
            for chunk in range(CHUNKS)
        ]
        return jnp.concatenate(columns, axis=1)[:, :FF]

    wide, narrow, proj, qkv_sum = [], [], [], []
    for layer in range(LAYERS):
        parts, attend = pieces_of(layer)
        narrow.append(hidden_sum(parts, 0))
        wide.append(jnp.concatenate([hidden_sum(parts, 1), hidden_sum(parts, 2)], axis=1))
        proj.append(parts[0][:, 3 * WIDTHS[0] : 3 * WIDTHS[0] + features])
        qkv_sum.append(attend)
    return (
        block_out[None],
        token_grad[None],
        gain_sums[:LAYERS],
        jnp.stack(qkv_sum),
        jnp.stack(proj),
        gain_sums[LAYERS:],
        jnp.stack(wide),
        jnp.stack(narrow),
    )


def solution(mesh):
    in_specs = (
        P("fsdp", "seq", None),
        P("fsdp", "seq", None),
        P("fsdp", None),
        P("fsdp", None),
        P(None, "fsdp"),
        P(None, "fsdp", None),
        P(None, "fsdp", None),
        P(None, "fsdp"),
        P(None, "fsdp", None),
        P(None, "fsdp", None),
    )
    out_specs = (
        P("fsdp", "seq", None),
        P("fsdp", "seq", None),
        P(None, ("seq", "fsdp")),
        P(None, ("seq", "fsdp"), None),
        P(None, ("seq", "fsdp"), None),
        P(None, ("seq", "fsdp")),
        P(None, ("seq", "fsdp"), None),
        P(None, ("seq", "fsdp"), None),
    )
    return jax.shard_map(body, mesh=mesh, in_specs=in_specs, out_specs=out_specs, check_vma=False)
```

```python
import functools
import math

import jax
import jax.numpy as jnp
from jax import lax
from jax.experimental import pallas as pl
from jax.experimental.pallas import tpu as pltpu
from jax.sharding import PartitionSpec as P

HEADS = 16
HEAD_DIM = 64
FF = 2624
WINDOW = 128
BLOCK = 128
BLK_DEV = 2
LAYERS = 2

NEG = -1e30
EPS = 1e-05
THETA = 10000.0

AXES = ("seq", "fsdp")
LANES = 128
HALO = WINDOW // 2
SPLIT = (5, 8, 8)
FF_PAD = sum(SPLIT) * LANES
WIDTHS = tuple(blocks * LANES for blocks in SPLIT)
STARTS = tuple(sum(WIDTHS[:k]) for k in range(len(WIDTHS)))
CHUNKS = len(SPLIT)
TILES = 3
F32 = jnp.float32
BF16 = jnp.bfloat16
VMEM_LIMIT = 20 * 1024 * 1024
NT = (((1,), (1,)), ((), ()))
TN = (((0,), (0,)), ((), ()))


class Phases:
    def __init__(self):
        self.gate = ()
        self.made = []

    def next(self):
        self.gate = tuple(self.made)
        self.made = []

    def tie(self, value):
        return lax.optimization_barrier((value,) + self.gate)[0] if self.gate else value

    def keep(self, *values):
        self.made += values

    def route(self, value, axes, pairs):
        result = lax.ppermute(self.tie(value), axes, pairs)
        self.made.append(result)
        return result

    def swap(self, value, bit):
        count = lax.axis_size("seq") * lax.axis_size("fsdp")
        return self.route(value, AXES, [(i, i ^ (1 << bit)) for i in range(count)])

    def shift(self, value, up):
        pairs = [(i, i + 1) for i in range(lax.axis_size("seq") - 1)]
        if not up:
            pairs = [(b, a) for a, b in pairs]
        return self.route(value, "seq", pairs)


def flat_index():
    return lax.axis_index("seq") * lax.axis_size("fsdp") + lax.axis_index("fsdp")


class Weights:
    def __init__(self, flow, shard, sent):
        self.flow = flow
        self.shard = shard
        self.sent = sent

    def own(self):
        self.own_core = self.flow.swap(self.shard, 0)

    def over_x(self):
        self.far_x = self.flow.swap(self.sent, 1)

    def over_y(self):
        self.far_y = self.flow.swap(self.far_x, 2)

    def over_core(self):
        far = jnp.concatenate([self.far_x, self.flow.tie(self.far_y)], axis=0)
        self.pieces = (self.shard, far, self.own_core, self.flow.swap(far, 0))


def piece_order():
    quarter = lax.axis_index("fsdp")
    side = lax.axis_index("seq") % 2
    one = 1 - side
    order = []
    for core in (quarter, quarter ^ 1):
        order += [core * 2, core * 2 + 1, (core ^ 2) * 2 + side, (core ^ 2) * 2 + one]
    return jnp.stack(order).astype(jnp.int32)


def stage_bits(first_x):
    levels = lax.axis_size("seq").bit_length() - 1
    rest = [2 + level for level in range(1, levels)]
    return ([1, 2] if first_x else [2, 1]) + rest


def row_order(features, bits):
    order = [0] + bits
    per_device = features >> len(order)
    rows = jnp.arange(features, dtype=jnp.int32)
    place = rows // per_device
    owner = flat_index()
    for step, bit in enumerate(order):
        taken = (place >> (len(order) - 1 - step)) & 1
        owner = owner ^ (taken << bit)
    return owner * per_device + rows % per_device


def row_picker(features, bits):
    order = row_order(features, bits)
    grid = jnp.arange(features, dtype=jnp.int32)
    return (order[:, None] == grid[None, :]).astype(BF16)


def call(kernel, outs, scratch=(), smem=1, grid=None, in_specs=None, out_specs=None, limit=VMEM_LIMIT):
    params = dict(
        compiler_params=pltpu.CompilerParams(vmem_limit_bytes=limit),
        out_shape=outs,
        scratch_shapes=list(scratch),
        cost_estimate=pl.CostEstimate(
            flops=0, bytes_accessed=0, transcendentals=0
        ),
    )
    if grid is not None:
        params["grid"] = grid

    def run(*args):
        specs = in_specs
        if specs is None:
            specs = [pl.BlockSpec(memory_space=pltpu.SMEM)] * smem
            specs += [pl.BlockSpec(memory_space=pltpu.VMEM)] * (len(args) - smem)
        results = out_specs
        if results is None:
            results = jax.tree.map(lambda _: pl.BlockSpec(memory_space=pltpu.VMEM), outs)
        return pl.pallas_call(kernel, in_specs=specs, out_specs=results, **params)(*args)

    return run


def struct(shape, dtype):
    return jax.ShapeDtypeStruct(shape, dtype)


def to_pieces(offs, source, target):
    for k in range(source.shape[1] // LANES):
        start = pl.multiple_of(offs[k] * LANES, LANES)
        target[:, k * LANES : (k + 1) * LANES] = source[:, pl.ds(start, LANES)]


def from_pieces(offs, source, target):
    for k in range(source.shape[1] // LANES):
        start = pl.multiple_of(offs[k] * LANES, LANES)
        target[:, pl.ds(start, LANES)] = source[:, k * LANES : (k + 1) * LANES]


def joined(pieces, columns=slice(None)):
    return jnp.concatenate([piece[:, columns] for piece in pieces], axis=0)


def statistics(values):
    average = jnp.mean(values, axis=-1, keepdims=True)
    centred = values - average
    spread = jnp.mean(centred * centred, axis=-1, keepdims=True)
    rho = lax.rsqrt(spread + EPS)
    return centred, rho


def norm_pull(values, gain, grad):
    centred, rho = statistics(values)
    unit = centred * rho
    scaled = grad * gain
    mean_a = jnp.mean(scaled, axis=-1, keepdims=True)
    mean_b = jnp.mean(scaled * unit, axis=-1, keepdims=True)
    return rho * (scaled - mean_a - unit * mean_b), jnp.sum(grad * unit, axis=0, keepdims=True)


def turn_chunk(values, cosine, sine, sign):
    lane = lax.broadcasted_iota(jnp.int32, values.shape, 1)
    ahead = pltpu.roll(values, LANES - HEAD_DIM // 2, 1)
    behind = pltpu.roll(values, HEAD_DIM // 2, 1)
    turned = jnp.where(lane % HEAD_DIM < HEAD_DIM // 2, ahead, behind)
    if sign > 0:
        return values * cosine + turned * sine
    return values * cosine - turned * sine


def pack_one_kernel(side, first, own, sent):
    half = first.shape[1] // 2
    own[...] = first[0]
    sent[...] = first[0, pl.ds(pl.multiple_of(side[0] * half, half), half), :]


def pack_kernel(side, second, wide, narrow, *outs):
    half = wide.shape[1] // 2
    features = second.shape[2]
    outs[0][:, :features] = second[0]
    for chunk in range(CHUNKS):
        own = outs[2 * chunk]
        at = features if chunk == 0 else 0
        width = WIDTHS[chunk]
        start, stop = STARTS[chunk], min(STARTS[chunk] + width, FF)
        for array, base in ((narrow, 0), (wide, 0), (wide, FF)):
            if stop - start < width:
                own[:, at + width - LANES : at + width] = jnp.zeros((2 * half, LANES), BF16)
            own[:, at : at + stop - start] = array[0, :, base + start : base + stop]
            at += width
    for k in range(0, len(outs), 2):
        outs[k + 1][...] = outs[k][pl.ds(pl.multiple_of(side[0] * half, half), half), :]


def run_pack(side, arrays, layer):
    rows = arrays[0].shape[1]
    one = len(arrays) == 1
    features = arrays[0].shape[2]
    columns = [features + 3 * WIDTHS[0]] + [3 * width for width in WIDTHS[1:]]
    if one:
        columns = [features]
    outs = tuple(struct((height, width), BF16) for width in columns for height in (rows, rows // 2))
    flat = call(
        pack_one_kernel if one else pack_kernel,
        outs,
        grid=(1,),
        in_specs=[pl.BlockSpec(memory_space=pltpu.SMEM)]
        + [pl.BlockSpec((1,) + v.shape[1:], lambda j: (layer, 0, 0)) for v in arrays],
        out_specs=tuple(whole_spec(out.shape) for out in outs),
    )(side, *arrays)
    return [flat[k : k + 2] for k in range(0, len(flat), 2)]


def qkv_kernel(offs, x, gain, cosine, sine, p0, p1, p2, p3, out, normed, first, last, placed):
    step = pl.program_id(0)
    tokens = x.shape[0]

    @pl.when(step == 0)
    def _():
        centred, rho = statistics(x[...])
        normed[...] = (centred * rho * gain[...]).astype(BF16)
        to_pieces(offs, normed, placed)

    product = jnp.dot(
        placed[...], joined((p0, p1, p2, p3)), preferred_element_type=F32
    )

    @pl.when(step < 2)
    def _():
        for k in range(product.shape[1] // LANES):
            part = slice(k * LANES, (k + 1) * LANES)
            out[:, part] = turn_chunk(product[:, part], cosine[...], sine[...], 1).astype(BF16)

    @pl.when(step == 2)
    def _():
        out[...] = product.astype(BF16)

    first[...] = out[:HALO, :]
    last[...] = out[tokens - HALO :, :]


def piece_specs(rows, columns):
    return [pl.BlockSpec((rows, columns), lambda j: (0, j))] * 4


def proj_specs(rows, columns):
    return [pl.BlockSpec((rows, columns), lambda j: (0, 0))] * 4


def whole_spec(shape):
    return pl.BlockSpec(shape, lambda j: tuple(0 for _ in shape))


def run_qkv(offs, x, gain, cosine, sine, pieces):
    tokens, features = x.shape
    return call(
        qkv_kernel,
        (
            struct((tokens, 3 * features), BF16),
            struct((tokens, features), BF16),
            struct((HALO, 2 * features), BF16),
            struct((HALO, 2 * features), BF16),
        ),
        [pltpu.VMEM((tokens, features), BF16)],
        grid=(3,),
        in_specs=[pl.BlockSpec(memory_space=pltpu.SMEM)]
        + [whole_spec(v.shape) for v in (x, gain, cosine, sine)]
        + piece_specs(pieces[0].shape[0], features),
        out_specs=(
            pl.BlockSpec((tokens, features), lambda j: (0, j)),
            whole_spec((tokens, features)),
            pl.BlockSpec((HALO, features), lambda j: (0, jnp.maximum(j - 1, 0))),
            pl.BlockSpec((HALO, features), lambda j: (0, jnp.maximum(j - 1, 0))),
        ),
    )(offs, x, gain, cosine, sine, *pieces)


def extend(qkv, before, after, extended):
    tokens, features = qkv.shape[0], qkv.shape[1] // 3
    extended[:HALO, :] = before[...]
    extended[HALO : HALO + tokens, :] = qkv[:, features:]
    extended[HALO + tokens :, :] = after[...]


def attend_kernel(
    offs, qkv, before, after, seg_q, seg_k, x, gain,
    p0, p1, p2, p3, mixed, middle, second, extended, placed,
):
    tokens, features = x.shape
    extend(qkv, before, after, extended)
    scale = 1.0 / math.sqrt(HEAD_DIM)
    span = BLOCK + 2 * HALO
    row = lax.broadcasted_iota(jnp.int32, (BLOCK, span), 0)
    col = lax.broadcasted_iota(jnp.int32, (BLOCK, span), 1)
    near = (col >= row) & (col - row <= 2 * HALO)
    low = lax.broadcasted_iota(jnp.int32, (BLOCK, LANES), 1) < HEAD_DIM
    bias = []
    for block in range(tokens // BLOCK):
        base = block * BLOCK
        same = seg_q[base : base + BLOCK, :] == seg_k[:, base : base + span]
        bias.append(jnp.where(near & same, 0.0, NEG))

    def pair(index, carry):
        lanes = pl.ds(pl.multiple_of(index * LANES, LANES), LANES)
        value_lanes = pl.ds(pl.multiple_of(features + index * LANES, LANES), LANES)
        for block in range(tokens // BLOCK):
            base = block * BLOCK
            queries = qkv[base : base + BLOCK, lanes]
            keys = extended[base : base + span, lanes]
            values = extended[base : base + span, value_lanes]
            parts = []
            for keep in (low, ~low):
                chosen = jnp.where(keep, queries, jnp.zeros_like(queries))
                raw = lax.dot_general(chosen, keys, NT, preferred_element_type=F32)
                scores = raw * scale + bias[block]
                expo = jnp.exp(scores - jnp.max(scores, axis=-1, keepdims=True))
                probs = expo * (1.0 / jnp.sum(expo, axis=-1, keepdims=True))
                parts.append(jnp.dot(probs.astype(BF16), values, preferred_element_type=F32))
            mixed[base : base + BLOCK, lanes] = jnp.where(low, parts[0], parts[1]).astype(BF16)
        return carry

    lax.fori_loop(0, features // LANES, pair, 0)
    to_pieces(offs, mixed, placed)
    total = x[...] + jnp.dot(
        placed[...], joined((p0, p1, p2, p3)), preferred_element_type=F32
    )
    middle[...] = total
    centred, rho = statistics(total)
    second[...] = (centred * rho * gain[...]).astype(BF16)


def run_attend(offs, qkv, before, after, seg_q, seg_k, x, gain, pieces):
    tokens, features = x.shape
    return call(
        attend_kernel,
        (
            struct((tokens, features), BF16),
            struct((tokens, features), F32),
            struct((tokens, features), BF16),
        ),
        [
            pltpu.VMEM((tokens + 2 * HALO, 2 * features), BF16),
            pltpu.VMEM((tokens, features), BF16),
        ],
        grid=(1,),
        in_specs=[pl.BlockSpec(memory_space=pltpu.SMEM)]
        + [whole_spec(v.shape) for v in (qkv, before, after, seg_q, seg_k, x, gain)]
        + proj_specs(pieces[0].shape[0], features),
        out_specs=(whole_spec((tokens, features)),) * 3,
    )(offs, qkv, before, after, seg_q, seg_k, x, gain, *pieces)


def chunk_parts(pieces, base, width):
    return [
        joined(pieces, slice(base + k * width, base + (k + 1) * width)) for k in range(3)
    ]


def mlp_kernel(
    base, width, offs, second, carried, p0, p1, p2, p3, total, gated, slope, gate, placed, part
):
    output, first, other = chunk_parts((p0, p1, p2, p3), base, width)
    to_pieces(offs, second, placed)
    source = placed[...]
    hidden = jnp.dot(source, first, preferred_element_type=F32)
    factor = jnp.dot(source, other, preferred_element_type=F32)
    normal = 0.5 * (1.0 + lax.erf(hidden * math.sqrt(0.5)))
    density = jnp.exp(-0.5 * hidden * hidden) * (1.0 / math.sqrt(2.0 * math.pi))
    active = hidden * normal
    product = (active * factor).astype(BF16)
    gated[...] = product
    slope[...] = ((normal + hidden * density) * factor).astype(BF16)
    gate[...] = active.astype(BF16)
    part[...] = lax.dot_general(product, output, NT, preferred_element_type=F32)
    for k in range(part.shape[1] // LANES):
        lanes = pl.ds(pl.multiple_of(offs[k] * LANES, LANES), LANES)
        total[:, lanes] = carried[:, lanes] + part[:, k * LANES : (k + 1) * LANES]


def run_mlp(offs, second, carried, pieces, chunk):
    tokens, features = second.shape
    width = WIDTHS[chunk]
    base = pieces[0].shape[1] - 3 * width
    hidden = struct((tokens, width), BF16)
    return call(
        functools.partial(mlp_kernel, base, width),
        (struct((tokens, features), F32), hidden, hidden, hidden),
        [pltpu.VMEM((tokens, features), BF16), pltpu.VMEM((tokens, features), F32)],
    )(offs, second, carried, *pieces)


def mlp_pull(base, width, offs, upstream, gated, slope, gate, pieces, right, placed):
    output, first, other = chunk_parts(pieces, base, width)
    to_pieces(offs, upstream, placed)
    gated_grad = jnp.dot(placed[...], output, preferred_element_type=F32)
    input_grad = (slope[...].astype(F32) * gated_grad).astype(BF16)
    gate_grad = (gate[...].astype(F32) * gated_grad).astype(BF16)
    store(right, 0, gated[...])
    store(right, width, input_grad)
    store(right, 2 * width, gate_grad)
    return lax.dot_general(input_grad, first, NT, preferred_element_type=F32) + lax.dot_general(
        gate_grad, other, NT, preferred_element_type=F32
    )


def store(target, at, value):
    target[:, at : at + value.shape[1]] = value


def mlp_back_kernel(
    base, width, first, offs, upstream, gated, slope, gate, carried, p0, p1, p2, p3,
    total, right, placed,
):
    part = mlp_pull(
        base, width, offs, upstream, gated, slope, gate, (p0, p1, p2, p3), right, placed
    )
    total[...] = part if first else carried[...] + part


def mlp_back_last_kernel(
    base, width, offs, upstream, gated, slope, gate, carried, residual_grad, middle, gain,
    p0, p1, p2, p3, middle_grad, middle_grad_b, gain_grad, right, placed, sums, ordered,
):
    part = mlp_pull(
        base, width, offs, upstream, gated, slope, gate, (p0, p1, p2, p3), right, placed
    )
    sums[...] = carried[...] + part
    from_pieces(offs, sums, ordered)
    pulled, gains = norm_pull(middle[...], gain[...], ordered[...])
    result = residual_grad[...] + pulled
    middle_grad[...] = result
    middle_grad_b[...] = result.astype(BF16)
    gain_grad[...] = gains
    at = 3 * width
    store(right, at, result.astype(BF16))
    at += result.shape[1]
    rest = right.shape[1] - at
    if rest:
        store(right, at, jnp.zeros((result.shape[0], rest), BF16))


def run_mlp_back(offs, upstream, hidden, carried, pieces, chunk):
    tokens, features = upstream.shape
    width = WIDTHS[chunk]
    base = pieces[0].shape[1] - 3 * width
    right = struct((tokens, 3 * features), BF16)
    first = carried is None
    if first:
        carried = jnp.zeros((8, LANES), F32)
    return call(
        functools.partial(mlp_back_kernel, base, width, first),
        (struct((tokens, features), F32), right),
        [pltpu.VMEM((tokens, features), BF16)],
    )(offs, upstream, *hidden, carried, *pieces)


def run_mlp_back_last(offs, upstream, hidden, carried, residual_grad, middle, gain, pieces, chunk):
    tokens, features = upstream.shape
    width = WIDTHS[chunk]
    base = pieces[0].shape[1] - 3 * width
    right = struct((tokens, 3 * features), BF16)
    return call(
        functools.partial(mlp_back_last_kernel, base, width),
        (
            struct((tokens, features), F32),
            struct((tokens, features), BF16),
            struct((1, features), F32),
            right,
        ),
        [
            pltpu.VMEM((tokens, features), BF16),
            pltpu.VMEM((tokens, features), F32),
            pltpu.VMEM((tokens, features), F32),
        ],
    )(offs, upstream, *hidden, carried, residual_grad, middle, gain, *pieces)


def attend_back_kernel(
    offs, middle_grad, qkv, before, after, seg_q, seg_k, cosine, sine, p0, p1, p2, p3,
    query_grad, own_grad, rim_before, rim_after, extended, mixed_grad, extended_grad,
):
    tokens, features = middle_grad.shape
    extend(qkv, before, after, extended)
    placed = lax.dot_general(
        middle_grad[...], joined((p0, p1, p2, p3)), NT, preferred_element_type=F32
    ).astype(BF16)
    for k in range(features // LANES):
        lanes = pl.ds(pl.multiple_of(offs[k] * LANES, LANES), LANES)
        mixed_grad[:, lanes] = placed[:, k * LANES : (k + 1) * LANES]
    scale = 1.0 / math.sqrt(HEAD_DIM)
    span = BLOCK + 2 * HALO
    row = lax.broadcasted_iota(jnp.int32, (span, BLOCK), 1)
    col = lax.broadcasted_iota(jnp.int32, (span, BLOCK), 0)
    near = (col >= row) & (col - row <= 2 * HALO)
    low = lax.broadcasted_iota(jnp.int32, (BLOCK, LANES), 1) < HEAD_DIM
    bias = []
    for block in range(tokens // BLOCK):
        base = block * BLOCK
        same = seg_q[:, base : base + BLOCK] == seg_k[base : base + span, :]
        bias.append(jnp.where(near & same, 0.0, NEG))

    def pair(index, carry):
        lanes = pl.ds(pl.multiple_of(index * LANES, LANES), LANES)
        value_lanes = pl.ds(pl.multiple_of(features + index * LANES, LANES), LANES)
        key_sums = []
        value_sums = []
        for block in range(tokens // BLOCK):
            base = block * BLOCK
            here = slice(base, base + BLOCK)
            queries = qkv[here, lanes]
            grads = mixed_grad[here, lanes]
            keys = extended[base : base + span, lanes]
            values = extended[base : base + span, value_lanes]
            key_sum = None
            value_sum = None
            query_parts = []
            for keep in (low, ~low):
                chosen = jnp.where(keep, queries, jnp.zeros_like(queries))
                chosen_grad = jnp.where(keep, grads, jnp.zeros_like(grads))
                raw = lax.dot_general(keys, chosen, NT, preferred_element_type=F32)
                scores = raw * scale + bias[block]
                expo = jnp.exp(scores - jnp.max(scores, axis=0, keepdims=True))
                probs = expo * (1.0 / jnp.sum(expo, axis=0, keepdims=True))
                prob_grad = lax.dot_general(values, chosen_grad, NT, preferred_element_type=F32)
                delta = jnp.sum(prob_grad * probs, axis=0, keepdims=True)
                score_grad = (probs * (prob_grad - delta) * scale).astype(BF16)
                query_parts.append(
                    lax.dot_general(score_grad, keys, TN, preferred_element_type=F32)
                )
                to_keys = jnp.dot(score_grad, chosen, preferred_element_type=F32)
                to_values = jnp.dot(
                    probs.astype(BF16), chosen_grad, preferred_element_type=F32
                )
                key_sum = to_keys if key_sum is None else key_sum + to_keys
                value_sum = to_values if value_sum is None else value_sum + to_values
            joint = jnp.where(low, query_parts[0], query_parts[1])
            query_grad[here, lanes] = turn_chunk(
                joint, cosine[here, :], sine[here, :], -1
            ).astype(BF16)
            key_sums.append(key_sum)
            value_sums.append(value_sum)
        for sums, place in ((key_sums, lanes), (value_sums, value_lanes)):
            over = 2 * HALO
            extended_grad[:BLOCK, place] = sums[0][:BLOCK]
            extended_grad[BLOCK : BLOCK + over, place] = sums[0][BLOCK:] + sums[1][:over]
            extended_grad[BLOCK + over :, place] = sums[1][over:]
        return carry

    lax.fori_loop(0, features // LANES, pair, 0)
    rim_before[...] = extended_grad[:HALO, :].astype(BF16)
    own_grad[...] = extended_grad[HALO : HALO + tokens, :]
    rim_after[...] = extended_grad[HALO + tokens :, :].astype(BF16)


def run_attend_back(offs, middle_grad, qkv, before, after, seg_q, seg_k, cosine, sine, pieces):
    tokens, features = middle_grad.shape
    rim = struct((HALO, 2 * features), BF16)
    return call(
        attend_back_kernel,
        (struct((tokens, features), BF16), struct((tokens, 2 * features), F32), rim, rim),
        [
            pltpu.VMEM((tokens + 2 * HALO, 2 * features), BF16),
            pltpu.VMEM((tokens, features), BF16),
            pltpu.VMEM((tokens + 2 * HALO, 2 * features), F32),
        ],
        grid=(1,),
        in_specs=[pl.BlockSpec(memory_space=pltpu.SMEM)]
        + [
            whole_spec(v.shape)
            for v in (middle_grad, qkv, before, after, seg_q, seg_k, cosine, sine)
        ]
        + proj_specs(pieces[0].shape[0], features),
        out_specs=(
            whole_spec((tokens, features)),
            whole_spec((tokens, 2 * features)),
            whole_spec((HALO, 2 * features)),
            whole_spec((HALO, 2 * features)),
        ),
    )(offs, middle_grad, qkv, before, after, seg_q, seg_k, cosine, sine, *pieces)


def qkv_back_kernel(
    offs, query_grad, own_grad, arrived_first, arrived_last, cosine, sine, x, gain, middle_grad,
    p0, p1, p2, p3, right, upstream, upstream_b, gain_grad, sums, ordered,
):
    step = pl.program_id(0)
    tokens, features = x.shape
    for part in range(3):

        @pl.when(step == part)
        def _():
            if part == 0:
                joint = query_grad[...]
            else:
                chunks = []
                for k in range(features // LANES):
                    at = (part - 1) * features + k * LANES
                    there = slice(at, at + LANES)
                    rows = [
                        own_grad[:HALO, there] + arrived_first[:, there].astype(F32),
                        own_grad[HALO : tokens - HALO, there],
                        own_grad[tokens - HALO :, there] + arrived_last[:, there].astype(F32),
                    ]
                    grads = jnp.concatenate(rows, axis=0)
                    if part == 1:
                        grads = turn_chunk(grads, cosine[...], sine[...], -1)
                    chunks.append(grads.astype(BF16))
                joint = jnp.concatenate(chunks, axis=1)
            store(right, part * features, joint)
            product = lax.dot_general(
                joint, joined((p0, p1, p2, p3)), NT, preferred_element_type=F32
            )
            sums[...] = product if part == 0 else sums[...] + product

    @pl.when(step == 2)
    def _():
        from_pieces(offs, sums, ordered)
        pulled, gains = norm_pull(x[...], gain[...], ordered[...])
        result = middle_grad[...] + pulled
        upstream[...] = result
        upstream_b[...] = result.astype(BF16)
        gain_grad[...] = gains


def run_qkv_back(
    offs, query_grad, own_grad, arrived_first, arrived_last, cosine, sine, x, gain, middle_grad, pieces
):
    tokens, features = x.shape
    whole = (query_grad, own_grad, arrived_first, arrived_last, cosine, sine, x, gain, middle_grad)
    outs = (
        struct((tokens, 3 * features), BF16),
        struct((tokens, features), F32),
        struct((tokens, features), BF16),
        struct((1, features), F32),
    )
    return call(
        qkv_back_kernel,
        outs,
        [pltpu.VMEM((tokens, features), F32), pltpu.VMEM((tokens, features), F32)],
        grid=(3,),
        in_specs=[pl.BlockSpec(memory_space=pltpu.SMEM)]
        + [whole_spec(v.shape) for v in whole]
        + piece_specs(pieces[0].shape[0], features),
        out_specs=tuple(whole_spec(out.shape) for out in outs),
    )(offs, *whole, *pieces)


def pick_kernel(which, *refs):
    pickers, lefts, (mine, theirs) = refs[:2], refs[2:-2], refs[-2:]
    half = pickers[0].shape[0] // 2
    for k, (picker, left) in enumerate(which):
        rows = lax.dot_general(
            pickers[picker][...], lefts[left][...], NT, preferred_element_type=F32
        ).astype(BF16)
        mine[k * half : (k + 1) * half, :] = rows[:half]
        theirs[k * half : (k + 1) * half, :] = rows[half:]


def run_pick(pickers, lefts, which):
    rows = len(which) * pickers[0].shape[0] // 2
    out = struct((rows, lefts[0].shape[0]), BF16)
    return call(functools.partial(pick_kernel, which), (out, out), smem=0)(*pickers, *lefts)


def exchange_kernel(plan, *refs):
    segments, stages = plan
    refs = list(refs)
    take = lambda count: [refs.pop(0) for _ in range(count)]
    adding, ending, far_ending, finishing = stages
    if segments:
        rights, rights_far = take(2), take(2)
        lefts = [take(2) for _ in segments]
    kept = take(2) if adding else None
    last = take(2) if ending else None
    come = take(2) if adding or ending else None
    near_pair = take(2) if far_ending else None
    far_pair = take(2) if finishing else None
    keep = take(2) if segments else None
    stay = take(2) if adding else None
    send = take(2) if segments or adding else None
    near_out = take(2) if ending else None
    far_out = take(2) if far_ending else None
    result = take(1)[0] if finishing else None

    def added(pair, rows, columns):
        return pair[0][rows, columns].astype(F32) + pair[1][rows, columns].astype(F32)

    def body(step):
        everything = slice(None)
        top = 0
        if segments:
            half, tile = keep[0].shape
            for (path, start, stop), (left, left_far) in zip(segments, lefts):
                low, high = max(start - step * tile, 0), min(stop - step * tile, tile)
                if low >= high:
                    continue
                columns = slice(low, high)
                total = jnp.dot(
                    jnp.concatenate([left[...], left_far[...]], axis=1),
                    jnp.concatenate(
                        [rights[path][:, columns], rights_far[path][:, columns]], axis=0
                    ),
                    preferred_element_type=F32,
                ).astype(BF16)
                keep[path][:, columns] = total[:half]
                send[path][:half, columns] = total[half:]
            top = half
        came = 0
        if adding:
            rows, tile = kept[0].shape
            half = rows // 2
            for path in range(2):
                total = kept[path][...].astype(F32) + come[path][:rows, :].astype(F32)
                stay[path][...] = total[:half].astype(BF16)
                send[1 - path][top : top + half, :] = total[half:].astype(BF16)
            came = rows
        if ending:
            rows, tile = last[0].shape
            half = rows // 2
            for path in range(2):
                at = (path * TILES + step) * tile
                total = last[path][...].astype(F32) + come[1 - path][
                    came : came + rows, :
                ].astype(F32)
                near_out[0][:, at : at + tile] = total[:half].astype(BF16)
                near_out[1][:, at : at + tile] = total[half:].astype(BF16)
        if step == 0 and far_ending:
            half = near_pair[0].shape[0] // 2
            far_out[0][...] = added(near_pair, slice(0, half), everything).astype(BF16)
            far_out[1][...] = added(near_pair, slice(half, 2 * half), everything).astype(BF16)
        if step == 0 and finishing:
            result[...] = added(far_pair, everything, everything).astype(result.dtype)

    for step in range(TILES):
        pl.when(pl.program_id(0) == step)(functools.partial(body, step))


class Exchange:
    def __init__(self, flow, rows, width, bits):
        self.flow = flow
        self.rows = rows
        self.width = width
        self.near, self.far = bits[:2]
        self.dtype = F32 if len(bits) == 2 else BF16
        self.kept = self.last = self.come = self.near_pair = self.far_pair = None

    def busy(self):
        return any((self.kept, self.last, self.near_pair, self.far_pair))

    def step(self, rights=None, segments=()):
        flow, rows, width = self.flow, self.rows, self.width
        tile = width // TILES
        args, specs, outs, out_specs = [], [], [], []

        def tiled(shape):
            return pl.BlockSpec((shape[0], tile), lambda j: (0, j))

        def give(pair, spec):
            if pair:
                args.extend(pair)
                specs.extend(spec(value.shape) for value in pair)

        def want(height, columns, spec, count=2, dtype=BF16):
            outs.extend([struct((height, columns), dtype)] * count)
            out_specs.extend([spec((height, columns))] * count)

        for right in rights or ():
            args += [right, right]
            block = (right.shape[0], tile)
            specs += [pl.BlockSpec(block, lambda j: (0, j))]
            specs += [pl.BlockSpec(block, lambda j: (0, TILES + j))]
        for _, _, _, left, place in segments:
            args += left
            specs += [pl.BlockSpec((rows, left[0].shape[1]), lambda j, at=place: (at, 0))] * 2
        give(self.kept, tiled)
        give(self.last, tiled)
        give(self.come if self.kept or self.last else None, tiled)
        give(self.near_pair, whole_spec)
        give(self.far_pair, whole_spec)
        height = 0
        if segments:
            want(rows // 2, width, tiled)
            height += rows // 2
        if self.kept:
            want(rows // 4, width, tiled)
            height += rows // 4
        if height:
            want(height, width, tiled)
        if self.last:
            want(rows // 8, 2 * width, whole_spec)
        if self.near_pair:
            want(rows // 16, 2 * width, whole_spec)
        if self.far_pair:
            want(rows // 16, 2 * width, whole_spec, 1, self.dtype)
        stages = tuple(map(bool, (self.kept, self.last, self.near_pair, self.far_pair)))
        plan = (
            tuple((path, start - path * width, stop - path * width) for path, start, stop, _, _ in segments),
            stages,
        )
        args[0] = flow.tie(args[0])
        results = list(
            call(
                functools.partial(exchange_kernel, plan),
                tuple(outs),
                grid=(TILES,),
                in_specs=specs,
                out_specs=tuple(out_specs),
            )(*args)
        )

        def got(wanted):
            return [results.pop(0), results.pop(0)] if wanted else None

        keep, stay, send = got(segments), got(self.kept), got(height)
        near, far = got(self.last), got(self.near_pair)
        result = results.pop(0) if self.far_pair else None
        self.kept, self.last = keep, stay
        self.come = send and [flow.swap(value, 1 + path) for path, value in enumerate(send)]
        self.near_pair = near and [near[0], flow.swap(near[1], self.near)]
        self.far_pair = far and [far[0], flow.swap(far[1], self.far)]
        return result


class Ending:
    def __init__(self, flow, value, bits, deliver):
        self.flow = flow
        self.bits = list(bits)
        self.deliver = deliver
        self.keep = value
        self.come = None

    def step(self):
        if self.come is not None:
            self.keep = self.keep.astype(F32) + self.flow.tie(self.come).astype(F32)
        if not self.bits:
            self.deliver(self.keep)
            return False
        half = self.keep.shape[0] // 2
        send = self.keep[half:].astype(BF16)
        self.keep = self.keep[:half].astype(BF16)
        self.come = self.flow.swap(send, self.bits.pop(0))
        return True


def rope_tables(position):
    inverse = jnp.power(THETA, -jnp.arange(0, HEAD_DIM, 2, dtype=F32) / HEAD_DIM)
    angles = position[:, None] * inverse[None, :]
    cosine, sine = jnp.cos(angles), jnp.sin(angles)
    return (
        jnp.concatenate([cosine, cosine, cosine, cosine], axis=-1),
        jnp.concatenate([-sine, sine, -sine, sine], axis=-1),
    )


def layout(positions, lengths, total):
    count = lengths.shape[0]
    blocks = (lengths + BLOCK - 1) // BLOCK
    first = (jnp.cumsum(blocks) - blocks) * BLOCK
    owner = jnp.sum((positions[:, None] >= first[None, :]).astype(jnp.int32), axis=1) - 1
    table = owner[:, None] == jnp.arange(count, dtype=jnp.int32)[None, :]
    start = jnp.sum(jnp.where(table, first[None, :], 0), axis=1)
    span = jnp.sum(jnp.where(table, lengths[None, :], 0), axis=1)
    local = positions - start
    inside = (positions >= 0) & (positions < total)
    valid = inside & (local < span)
    segment = jnp.where(inside, jnp.where(valid, owner, owner + count), -1)
    return (segment, local, valid)


def body(
    tokens,
    cotangent,
    lengths,
    block_perm,
    attn_gain,
    qkv_weight,
    proj_weight,
    mlp_gain,
    wide_weight,
    narrow_weight,
):
    flow = Phases()
    seq_index = lax.axis_index("seq")
    seq_count = lax.axis_size("seq")
    levels = seq_count.bit_length() - 1
    tok_dev = tokens.shape[1]
    features = tokens.shape[2]
    block_rows = tok_dev // BLK_DEV
    order_map = block_perm[0]
    target = order_map[0::BLK_DEV] // BLK_DEV
    source = jnp.arange(seq_count, dtype=jnp.int32)

    def holder(bit_level):
        low_mask = (1 << bit_level) - 1
        place = jnp.bitwise_or(
            jnp.bitwise_and(target, low_mask), jnp.bitwise_and(source, ~low_mask)
        )
        return jnp.sum(jnp.where(place == seq_index, source, 0))

    home_index = holder(levels)
    slot_of = lax.dynamic_slice_in_dim(order_map, home_index * BLK_DEV, BLK_DEV) % BLK_DEV
    crossed = slot_of[0] == 1

    def crossing(rows):
        turned = jnp.concatenate([rows[block_rows:], rows[:block_rows]], axis=0)
        return jnp.where(crossed, turned, rows)

    def crossed_over(bit_level, given):
        payload = holder(bit_level + 1 if given else bit_level)
        if not given:
            payload = jnp.sum(jnp.where(source == payload, target, 0))
        flips = jnp.right_shift(jnp.bitwise_xor(seq_index, payload), bit_level)
        return jnp.bitwise_and(flips, 1) == 1

    class Route:
        def __init__(self, rows, given, last=levels):
            self.rows = rows
            self.given = given
            self.levels = list(range(last))
            if given:
                self.levels.reverse()
            self.arrived = None

        def step(self):
            if self.arrived is not None:
                self.rows = jnp.where(
                    crossed_over(self.level, self.given), flow.tie(self.arrived), self.rows
                )
                self.arrived = None
            if self.levels:
                self.level = self.levels.pop(0)
                self.arrived = flow.swap(self.rows, 2 + self.level)
                return True
            return False

        def finish(self):
            while self.step():
                flow.next()
            return self.rows

    total = seq_count * tok_dev
    own_place = seq_index * tok_dev + jnp.arange(tok_dev, dtype=jnp.int32)
    key_place = seq_index * tok_dev - HALO + jnp.arange(tok_dev + 2 * HALO, dtype=jnp.int32)
    seg_query, local_query, valid_query = layout(own_place, lengths[0], total)
    seg_key, _, _ = layout(key_place, lengths[0], total)
    cosine, sine = rope_tables(local_query.astype(F32))
    seg_q_col, seg_q_row = seg_query[:, None], seg_query[None, :]
    seg_k_col, seg_k_row = seg_key[:, None], seg_key[None, :]
    offs = piece_order()
    bits_x, bits_y = stage_bits(True), stage_bits(False)
    picker_x, picker_y = row_picker(features, bits_x), row_picker(features, bits_y)

    gains = jnp.concatenate([attn_gain, mlp_gain], axis=0)
    gains = lax.all_gather(gains, "fsdp", axis=1, tiled=True).astype(F32)
    gains_a = [gains[layer : layer + 1] for layer in range(LAYERS)]
    gains_m = [gains[LAYERS + layer : LAYERS + layer + 1] for layer in range(LAYERS)]

    side = (seq_index % 2).astype(jnp.int32).reshape(1)
    arrays = (proj_weight, wide_weight, narrow_weight)
    items = []
    for layer in range(LAYERS):
        packs = run_pack(side, (qkv_weight,), layer) + run_pack(side, arrays, layer)
        items += [Weights(flow, *pack) for pack in packs]
    per_layer = len(items) // LAYERS
    tok_route, cot_route = Route(tokens[0], False), Route(cotangent[0], False, levels - 1)

    first_use = 3
    owns = {0: (0, 1), 1: (2,), 2: (3,), 4: (4, 5), 5: (6,), 6: (7,)}
    phase = 0

    def transfers():
        if phase < len(items):
            items[phase].over_x()
        if 0 <= phase - 1 < len(items):
            items[phase - 1].over_y()
        if 0 <= phase - 2 < len(items):
            items[phase - 2].over_core()
        for place in owns.get(phase, ()):
            items[place].own()

    flow.keep(gains)
    while phase < first_use or tok_route.levels:
        transfers()
        tok_route.step()
        if phase < 2:
            cot_route.step()
        if phase == 0:
            flow.keep(*(item.shard for item in items[1:]))
        phase += 1
        flow.next()
    tok_route.step()
    residual = crossing(tok_route.rows).astype(F32)
    cot_halves = []
    kept = []
    for layer in range(LAYERS):
        base = layer * per_layer
        transfers()
        qkv, normed, edge_first, edge_last = run_qkv(
            offs, flow.tie(residual), gains_a[layer], cosine, sine, items[base].pieces
        )
        flow.keep(normed)
        before = flow.shift(edge_last, True)
        after = flow.shift(edge_first, False)
        phase += 1
        flow.next()
        transfers()
        if layer and kept[-1][-1] is None:
            kept[-1][-1] = (mine, flow.swap(theirs, 0))
        start = residual
        mixed, middle, second = run_attend(
            offs, flow.tie(qkv), before, after, seg_q_col, seg_k_row, residual, gains_m[layer],
            items[base + 1].pieces,
        )
        residual = middle
        hidden = []
        for chunk in range(CHUNKS):
            if chunk:
                phase += 1
                flow.next()
                transfers()
                if layer == 0:
                    if not cot_halves:
                        cot_rows = cot_route.finish()
                        for half in (cot_rows[:block_rows], cot_rows[block_rows:]):
                            cot_halves.append(Route(half, False))
                            cot_halves[-1].levels = [levels - 1]
                    cot_halves[chunk - 1].step()
            residual, gated, slope, gate = run_mlp(
                offs, second, flow.tie(residual), items[base + 1 + chunk].pieces, chunk
            )
            flow.keep(residual, gated)
            hidden.append((gated, slope, gate))
            if chunk == 1:
                lefts = (normed, mixed, second)
                which = ((0, 0), (1, 0), (1, 1), (0, 2), (1, 2))
                mine, theirs = run_pick((picker_x, picker_y), lefts, which)
                flow.keep(theirs)
        picks = None
        if layer == LAYERS - 1:
            flow.next()
            picks = (mine, flow.swap(theirs, 0))
        kept.append([start, qkv, before, after, middle, hidden, picks])
        phase += 1
        flow.next()

    packed_cot = crossing(jnp.concatenate([half.finish() for half in cot_halves], axis=0))
    upstream_b = packed_cot * valid_query[:, None].astype(BF16)
    upstream = upstream_b.astype(F32)

    def both_halves(rows):
        rows = crossing(rows)
        return [Route(rows[:block_rows], True), Route(rows[block_rows:], True)]

    out_routes = both_halves(residual.astype(BF16))

    late = bits_x[2:]
    exchange = Exchange(flow, features // 2, 3 * features // 2, late)
    endings = []
    sums = {}
    count = 0
    width = 3 * features // 2

    def settle(done):
        nonlocal count
        if done is None:
            return
        deliver = functools.partial(sums.__setitem__, count)
        count += 1
        if len(late) > 2:
            endings.append(Ending(flow, done, late[2:], deliver))
        else:
            deliver(done)

    def step_endings():
        for item in list(endings):
            if not item.step():
                endings.remove(item)

    def group(right, parts):
        segments = []
        at = 0
        for columns, lefts in parts:
            for path in range(2):
                low = max(at, path * width)
                high = min(at + columns, (path + 1) * width)
                if low < high:
                    segments.append((path, low, high, lefts[path][:2], lefts[path][2]))
            at += columns
        return list(right), tuple(segments)

    terms = [None] * LAYERS
    made, ready = None, None

    def backward_phase():
        nonlocal made, ready
        flow.next()
        moving = bool(made or ready or exchange.busy())
        if ready or exchange.busy():
            settle(exchange.step(*(group(*ready) if ready else ())))
        ready = None
        if made:
            right, parts = made
            ready = ((right, flow.swap(right, 0)), parts)
        made = None
        step_endings()
        return moving

    for layer in reversed(range(LAYERS)):
        start, qkv, before, after, middle, hidden, picks = kept[layer]
        base = layer * per_layer
        normed_x, normed_y, mixed_y, second_x, second_y = (picks + (row,) for row in range(5))
        carried = None
        upstream_left = None
        for chunk in reversed(range(CHUNKS)):
            if layer < LAYERS - 1 or chunk < CHUNKS - 1:
                backward_phase()
            pieces = items[base + 1 + chunk].pieces
            if upstream_left is None:
                mine, theirs = run_pick(
                    (picker_x, picker_y), (flow.tie(upstream_b),), ((0, 0), (1, 0))
                )
                flow.keep(theirs)
                upstream_left = []
            elif not upstream_left:
                far = flow.swap(theirs, 0)
                upstream_left += [(mine, far, path) for path in range(2)]
            if layer == LAYERS - 1 and chunk:
                out_routes[CHUNKS - 1 - chunk].step()
            args = (offs, flow.tie(upstream_b), hidden[chunk], carried)
            columns = WIDTHS[chunk]
            parts = [
                (columns, upstream_left),
                (2 * columns, (second_x, second_y)),
            ]
            if chunk:
                carried, right = run_mlp_back(*args, pieces, chunk)
                flow.keep(carried)
            else:
                middle_grad, middle_grad_b, mlp_term, right = run_mlp_back_last(
                    *args, upstream, middle, gains_m[layer], pieces, chunk
                )
                parts.append((2 * width - 3 * columns, (None, mixed_y)))
                query_grad, own_grad, rim_before, rim_after = run_attend_back(
                    offs, middle_grad_b, qkv, before, after, seg_q_row, seg_k_col, cosine, sine, pieces
                )
                flow.keep(query_grad, own_grad)
                arrived_first = flow.shift(rim_after, True)
                arrived_last = flow.shift(rim_before, False)
            flow.keep(right)
            made = (right, parts)
        backward_phase()
        right, upstream, upstream_b, attn_term = run_qkv_back(
            offs, flow.tie(query_grad), own_grad, arrived_first, arrived_last, cosine, sine, start,
            gains_a[layer], middle_grad, items[base].pieces,
        )
        if layer:
            for route in out_routes:
                route.step()
        flow.keep(upstream_b, right)
        made = (right, [(2 * width, (normed_x, normed_y))])
        terms[layer] = (attn_term, mlp_term)
    backward_phase()
    grad_routes = both_halves(flow.tie(upstream_b))
    grad_routes[0].step()
    vectors = [terms[layer][0] for layer in range(LAYERS)]
    vectors += [terms[layer][1] for layer in range(LAYERS)]
    gain_sums = lax.dot_general(
        flow.tie(jnp.concatenate(vectors, axis=0)), picker_x.astype(F32), NT, precision=lax.Precision.HIGHEST
    )
    gain_bits = [0] + list(bits_x)
    while backward_phase() or endings or gain_bits:
        for route in grad_routes:
            route.step()
        if not grad_routes[0].levels:
            for route in out_routes:
                route.step()
        for bit in gain_bits[: 1 if len(gain_bits) > 2 else 2]:
            half = gain_sums.shape[1] // 2
            gain_sums = gain_sums[:, :half] + flow.swap(gain_sums[:, half:], bit)
        gain_bits = gain_bits[1 if len(gain_bits) > 2 else 2 :]
    block_out, token_grad = (
        jnp.concatenate([route.finish() for route in routes], axis=0)
        for routes in (out_routes, grad_routes)
    )

    def pieces_of(layer):
        at = per_layer * (LAYERS - 1 - layer)
        parts = {chunk: sums[at + CHUNKS - 1 - chunk] for chunk in range(CHUNKS)}
        return parts, sums[at + CHUNKS]

    def hidden_sum(parts, role):
        columns = [
            parts[chunk][:, role * WIDTHS[chunk] : (role + 1) * WIDTHS[chunk]]
            for chunk in range(CHUNKS)
        ]
        return jnp.concatenate(columns, axis=1)[:, :FF]

    wide, narrow, proj, qkv_sum = [], [], [], []
    for layer in range(LAYERS):
        parts, attend = pieces_of(layer)
        narrow.append(hidden_sum(parts, 0))
        wide.append(jnp.concatenate([hidden_sum(parts, 1), hidden_sum(parts, 2)], axis=1))
        proj.append(parts[0][:, 3 * WIDTHS[0] : 3 * WIDTHS[0] + features])
        qkv_sum.append(attend)
    return (
        block_out[None],
        token_grad[None],
        gain_sums[:LAYERS],
        jnp.stack(qkv_sum),
        jnp.stack(proj),
        gain_sums[LAYERS:],
        jnp.stack(wide),
        jnp.stack(narrow),
    )


def solution(mesh):
    in_specs = (
        P("fsdp", "seq", None),
        P("fsdp", "seq", None),
        P("fsdp", None),
        P("fsdp", None),
        P(None, "fsdp"),
        P(None, "fsdp", None),
        P(None, "fsdp", None),
        P(None, "fsdp"),
        P(None, "fsdp", None),
        P(None, "fsdp", None),
    )
    out_specs = (
        P("fsdp", "seq", None),
        P("fsdp", "seq", None),
        P(None, ("seq", "fsdp")),
        P(None, ("seq", "fsdp"), None),
        P(None, ("seq", "fsdp"), None),
        P(None, ("seq", "fsdp")),
        P(None, ("seq", "fsdp"), None),
        P(None, ("seq", "fsdp"), None),
    )
    return jax.shard_map(body, mesh=mesh, in_specs=in_specs, out_specs=out_specs, check_vma=False)
```

```python
import functools
import math

import jax
import jax.numpy as jnp
from jax import lax
from jax.experimental import pallas as pl
from jax.experimental.pallas import tpu as pltpu
from jax.sharding import PartitionSpec as P

HEADS = 16
HEAD_DIM = 64
FF = 2624
WINDOW = 128
BLOCK = 128
BLK_DEV = 2
LAYERS = 2

NEG = -1e30
EPS = 1e-05
THETA = 10000.0

AXES = ("seq", "fsdp")
LANES = 128
HALO = WINDOW // 2
SPLIT = (5, 8, 8)
FF_PAD = sum(SPLIT) * LANES
WIDTHS = tuple(blocks * LANES for blocks in SPLIT)
STARTS = tuple(sum(WIDTHS[:k]) for k in range(len(WIDTHS)))
CHUNKS = len(SPLIT)
TILES = 3
F32 = jnp.float32
BF16 = jnp.bfloat16
VMEM_LIMIT = 20 * 1024 * 1024
NT = (((1,), (1,)), ((), ()))
TN = (((0,), (0,)), ((), ()))


class Phases:
    def __init__(self):
        self.gate = ()
        self.made = []

    def next(self):
        self.gate = tuple(self.made)
        self.made = []

    def tie(self, value):
        return lax.optimization_barrier((value,) + self.gate)[0] if self.gate else value

    def keep(self, *values):
        self.made += values

    def route(self, value, axes, pairs):
        result = lax.ppermute(self.tie(value), axes, pairs)
        self.made.append(result)
        return result

    def swap(self, value, bit):
        count = lax.axis_size("seq") * lax.axis_size("fsdp")
        return self.route(value, AXES, [(i, i ^ (1 << bit)) for i in range(count)])

    def shift(self, value, up):
        pairs = [(i, i + 1) for i in range(lax.axis_size("seq") - 1)]
        if not up:
            pairs = [(b, a) for a, b in pairs]
        return self.route(value, "seq", pairs)


def flat_index():
    return lax.axis_index("seq") * lax.axis_size("fsdp") + lax.axis_index("fsdp")


class Weights:
    def __init__(self, flow, shard, sent):
        self.flow = flow
        self.shard = shard
        self.sent = sent

    def own(self):
        self.own_core = self.flow.swap(self.shard, 0)

    def over_x(self):
        self.far_x = self.flow.swap(self.sent, 1)

    def over_y(self):
        self.far_y = self.flow.swap(self.far_x, 2)

    def over_core(self):
        far = jnp.concatenate([self.far_x, self.flow.tie(self.far_y)], axis=0)
        self.pieces = (self.shard, far, self.own_core, self.flow.swap(far, 0))


def piece_order():
    quarter = lax.axis_index("fsdp")
    side = lax.axis_index("seq") % 2
    one = 1 - side
    order = []
    for core in (quarter, quarter ^ 1):
        order += [core * 2, core * 2 + 1, (core ^ 2) * 2 + side, (core ^ 2) * 2 + one]
    return jnp.stack(order).astype(jnp.int32)


def stage_bits(first_x):
    levels = lax.axis_size("seq").bit_length() - 1
    rest = [2 + level for level in range(1, levels)]
    return ([1, 2] if first_x else [2, 1]) + rest


def row_order(features, bits):
    order = [0] + bits
    per_device = features >> len(order)
    rows = jnp.arange(features, dtype=jnp.int32)
    place = rows // per_device
    owner = flat_index()
    for step, bit in enumerate(order):
        taken = (place >> (len(order) - 1 - step)) & 1
        owner = owner ^ (taken << bit)
    return owner * per_device + rows % per_device


def row_picker(features, bits):
    order = row_order(features, bits)
    grid = jnp.arange(features, dtype=jnp.int32)
    return (order[:, None] == grid[None, :]).astype(BF16)


def call(kernel, outs, scratch=(), smem=1, grid=None, in_specs=None, out_specs=None, limit=VMEM_LIMIT):
    params = dict(
        compiler_params=pltpu.CompilerParams(vmem_limit_bytes=limit),
        out_shape=outs,
        scratch_shapes=list(scratch),
        cost_estimate=pl.CostEstimate(
            flops=0, bytes_accessed=0, transcendentals=0
        ),
    )
    if grid is not None:
        params["grid"] = grid

    def run(*args):
        specs = in_specs
        if specs is None:
            specs = [pl.BlockSpec(memory_space=pltpu.SMEM)] * smem
            specs += [pl.BlockSpec(memory_space=pltpu.VMEM)] * (len(args) - smem)
        results = out_specs
        if results is None:
            results = jax.tree.map(lambda _: pl.BlockSpec(memory_space=pltpu.VMEM), outs)
        return pl.pallas_call(kernel, in_specs=specs, out_specs=results, **params)(*args)

    return run


def struct(shape, dtype):
    return jax.ShapeDtypeStruct(shape, dtype)


def to_pieces(offs, source, target):
    for k in range(source.shape[1] // LANES):
        start = pl.multiple_of(offs[k] * LANES, LANES)
        target[:, k * LANES : (k + 1) * LANES] = source[:, pl.ds(start, LANES)]


def from_pieces(offs, source, target):
    for k in range(source.shape[1] // LANES):
        start = pl.multiple_of(offs[k] * LANES, LANES)
        target[:, pl.ds(start, LANES)] = source[:, k * LANES : (k + 1) * LANES]


def joined(pieces, columns=slice(None)):
    return jnp.concatenate([piece[:, columns] for piece in pieces], axis=0)


def statistics(values):
    average = jnp.mean(values, axis=-1, keepdims=True)
    centred = values - average
    spread = jnp.mean(centred * centred, axis=-1, keepdims=True)
    rho = lax.rsqrt(spread + EPS)
    return centred, rho


def norm_pull(values, gain, grad):
    centred, rho = statistics(values)
    unit = centred * rho
    scaled = grad * gain
    mean_a = jnp.mean(scaled, axis=-1, keepdims=True)
    mean_b = jnp.mean(scaled * unit, axis=-1, keepdims=True)
    return rho * (scaled - mean_a - unit * mean_b), jnp.sum(grad * unit, axis=0, keepdims=True)


def turn_chunk(values, cosine, sine, sign):
    lane = lax.broadcasted_iota(jnp.int32, values.shape, 1)
    ahead = pltpu.roll(values, LANES - HEAD_DIM // 2, 1)
    behind = pltpu.roll(values, HEAD_DIM // 2, 1)
    turned = jnp.where(lane % HEAD_DIM < HEAD_DIM // 2, ahead, behind)
    if sign > 0:
        return values * cosine + turned * sine
    return values * cosine - turned * sine


def pack_one_kernel(side, first, own, sent):
    half = first.shape[1] // 2
    own[...] = first[0]
    sent[...] = first[0, pl.ds(pl.multiple_of(side[0] * half, half), half), :]


def pack_kernel(side, second, wide, narrow, *outs):
    half = wide.shape[1] // 2
    features = second.shape[2]
    outs[0][:, :features] = second[0]
    for chunk in range(CHUNKS):
        own = outs[2 * chunk]
        at = features if chunk == 0 else 0
        width = WIDTHS[chunk]
        start, stop = STARTS[chunk], min(STARTS[chunk] + width, FF)
        for array, base in ((narrow, 0), (wide, 0), (wide, FF)):
            if stop - start < width:
                own[:, at + width - LANES : at + width] = jnp.zeros((2 * half, LANES), BF16)
            own[:, at : at + stop - start] = array[0, :, base + start : base + stop]
            at += width
    for k in range(0, len(outs), 2):
        outs[k + 1][...] = outs[k][pl.ds(pl.multiple_of(side[0] * half, half), half), :]


def run_pack(side, arrays, layer):
    rows = arrays[0].shape[1]
    one = len(arrays) == 1
    features = arrays[0].shape[2]
    columns = [features + 3 * WIDTHS[0]] + [3 * width for width in WIDTHS[1:]]
    if one:
        columns = [features]
    outs = tuple(struct((height, width), BF16) for width in columns for height in (rows, rows // 2))
    flat = call(
        pack_one_kernel if one else pack_kernel,
        outs,
        grid=(1,),
        in_specs=[pl.BlockSpec(memory_space=pltpu.SMEM)]
        + [pl.BlockSpec((1,) + v.shape[1:], lambda j: (layer, 0, 0)) for v in arrays],
        out_specs=tuple(whole_spec(out.shape) for out in outs),
    )(side, *arrays)
    return [flat[k : k + 2] for k in range(0, len(flat), 2)]


def qkv_kernel(offs, x, gain, cosine, sine, p0, p1, p2, p3, out, normed, first, last, placed):
    step = pl.program_id(0)
    tokens = x.shape[0]

    @pl.when(step == 0)
    def _():
        centred, rho = statistics(x[...])
        normed[...] = (centred * rho * gain[...]).astype(BF16)
        to_pieces(offs, normed, placed)

    product = jnp.dot(
        placed[...], joined((p0, p1, p2, p3)), preferred_element_type=F32
    )

    @pl.when(step < 2)
    def _():
        for k in range(product.shape[1] // LANES):
            part = slice(k * LANES, (k + 1) * LANES)
            out[:, part] = turn_chunk(product[:, part], cosine[...], sine[...], 1).astype(BF16)

    @pl.when(step == 2)
    def _():
        out[...] = product.astype(BF16)

    first[...] = out[:HALO, :]
    last[...] = out[tokens - HALO :, :]


def piece_specs(rows, columns):
    return [pl.BlockSpec((rows, columns), lambda j: (0, j))] * 4


def proj_specs(rows, columns):
    return [pl.BlockSpec((rows, columns), lambda j: (0, 0))] * 4


def whole_spec(shape):
    return pl.BlockSpec(shape, lambda j: tuple(0 for _ in shape))


def run_qkv(offs, x, gain, cosine, sine, pieces):
    tokens, features = x.shape
    return call(
        qkv_kernel,
        (
            struct((tokens, 3 * features), BF16),
            struct((tokens, features), BF16),
            struct((HALO, 2 * features), BF16),
            struct((HALO, 2 * features), BF16),
        ),
        [pltpu.VMEM((tokens, features), BF16)],
        grid=(3,),
        in_specs=[pl.BlockSpec(memory_space=pltpu.SMEM)]
        + [whole_spec(v.shape) for v in (x, gain, cosine, sine)]
        + piece_specs(pieces[0].shape[0], features),
        out_specs=(
            pl.BlockSpec((tokens, features), lambda j: (0, j)),
            whole_spec((tokens, features)),
            pl.BlockSpec((HALO, features), lambda j: (0, jnp.maximum(j - 1, 0))),
            pl.BlockSpec((HALO, features), lambda j: (0, jnp.maximum(j - 1, 0))),
        ),
    )(offs, x, gain, cosine, sine, *pieces)


def stacked(rows, low):
    zero = jnp.zeros_like(rows)
    return jnp.concatenate([jnp.where(low, rows, zero), jnp.where(low, zero, rows)], axis=0)


def extend(qkv, before, after, extended):
    tokens, features = qkv.shape[0], qkv.shape[1] // 3
    extended[:HALO, :] = before[...]
    extended[HALO : HALO + tokens, :] = qkv[:, features:]
    extended[HALO + tokens :, :] = after[...]


def attend_kernel(
    offs, qkv, before, after, seg_q, seg_k, x, gain,
    p0, p1, p2, p3, mixed, middle, second, extended, placed,
):
    tokens, features = x.shape
    extend(qkv, before, after, extended)
    scale = jnp.asarray(1.0 / math.sqrt(HEAD_DIM), BF16)
    span = BLOCK + 2 * HALO
    row = lax.broadcasted_iota(jnp.int32, (BLOCK, span), 0)
    col = lax.broadcasted_iota(jnp.int32, (BLOCK, span), 1)
    near = (col >= row) & (col - row <= 2 * HALO)
    low = lax.broadcasted_iota(jnp.int32, (BLOCK, LANES), 1) < HEAD_DIM
    bias = []
    for block in range(tokens // BLOCK):
        base = block * BLOCK
        same = seg_q[base : base + BLOCK, :] == seg_k[:, base : base + span]
        one = jnp.where(near & same, 0.0, NEG)
        bias.append(jnp.concatenate([one, one], axis=0))

    def pair(index, carry):
        lanes = pl.ds(pl.multiple_of(index * LANES, LANES), LANES)
        value_lanes = pl.ds(pl.multiple_of(features + index * LANES, LANES), LANES)
        for block in range(tokens // BLOCK):
            base = block * BLOCK
            queries = qkv[base : base + BLOCK, lanes]
            keys = extended[base : base + span, lanes]
            values = extended[base : base + span, value_lanes]
            scores = (
                lax.dot_general(stacked(queries * scale, low), keys, NT, preferred_element_type=F32)
                + bias[block]
            )
            expo = jnp.exp(scores - jnp.max(scores, axis=-1, keepdims=True))
            probs = expo * (1.0 / jnp.sum(expo, axis=-1, keepdims=True))
            both = jnp.dot(probs.astype(BF16), values, preferred_element_type=F32)
            mixed[base : base + BLOCK, lanes] = jnp.where(low, both[:BLOCK], both[BLOCK:]).astype(BF16)
        return carry

    lax.fori_loop(0, features // LANES, pair, 0)
    to_pieces(offs, mixed, placed)
    total = x[...] + jnp.dot(
        placed[...], joined((p0, p1, p2, p3)), preferred_element_type=F32
    )
    middle[...] = total
    centred, rho = statistics(total)
    second[...] = (centred * rho * gain[...]).astype(BF16)


def run_attend(offs, qkv, before, after, seg_q, seg_k, x, gain, pieces):
    tokens, features = x.shape
    return call(
        attend_kernel,
        (
            struct((tokens, features), BF16),
            struct((tokens, features), F32),
            struct((tokens, features), BF16),
        ),
        [
            pltpu.VMEM((tokens + 2 * HALO, 2 * features), BF16),
            pltpu.VMEM((tokens, features), BF16),
        ],
        grid=(1,),
        in_specs=[pl.BlockSpec(memory_space=pltpu.SMEM)]
        + [whole_spec(v.shape) for v in (qkv, before, after, seg_q, seg_k, x, gain)]
        + proj_specs(pieces[0].shape[0], features),
        out_specs=(whole_spec((tokens, features)),) * 3,
    )(offs, qkv, before, after, seg_q, seg_k, x, gain, *pieces)


def chunk_parts(pieces, base, width):
    return [
        joined(pieces, slice(base + k * width, base + (k + 1) * width)) for k in range(3)
    ]


def mlp_kernel(
    base, width, offs, second, carried, p0, p1, p2, p3, total, gated, slope, gate, placed, part
):
    output, first, other = chunk_parts((p0, p1, p2, p3), base, width)
    to_pieces(offs, second, placed)
    source = placed[...]
    hidden = jnp.dot(source, first, preferred_element_type=F32)
    factor = jnp.dot(source, other, preferred_element_type=F32)
    normal = 0.5 * (1.0 + lax.erf(hidden * math.sqrt(0.5)))
    density = jnp.exp(-0.5 * hidden * hidden) * (1.0 / math.sqrt(2.0 * math.pi))
    active = hidden * normal
    product = (active * factor).astype(BF16)
    gated[...] = product
    slope[...] = ((normal + hidden * density) * factor).astype(BF16)
    gate[...] = active.astype(BF16)
    part[...] = lax.dot_general(product, output, NT, preferred_element_type=F32)
    for k in range(part.shape[1] // LANES):
        lanes = pl.ds(pl.multiple_of(offs[k] * LANES, LANES), LANES)
        total[:, lanes] = carried[:, lanes] + part[:, k * LANES : (k + 1) * LANES]


def run_mlp(offs, second, carried, pieces, chunk):
    tokens, features = second.shape
    width = WIDTHS[chunk]
    base = pieces[0].shape[1] - 3 * width
    hidden = struct((tokens, width), BF16)
    return call(
        functools.partial(mlp_kernel, base, width),
        (struct((tokens, features), F32), hidden, hidden, hidden),
        [pltpu.VMEM((tokens, features), BF16), pltpu.VMEM((tokens, features), F32)],
    )(offs, second, carried, *pieces)


def mlp_pull(base, width, offs, upstream, gated, slope, gate, pieces, right, placed):
    output, first, other = chunk_parts(pieces, base, width)
    to_pieces(offs, upstream, placed)
    gated_grad = jnp.dot(placed[...], output, preferred_element_type=F32)
    input_grad = (slope[...].astype(F32) * gated_grad).astype(BF16)
    gate_grad = (gate[...].astype(F32) * gated_grad).astype(BF16)
    store(right, 0, gated[...])
    store(right, width, input_grad)
    store(right, 2 * width, gate_grad)
    return lax.dot_general(input_grad, first, NT, preferred_element_type=F32) + lax.dot_general(
        gate_grad, other, NT, preferred_element_type=F32
    )


def store(target, at, value):
    target[:, at : at + value.shape[1]] = value


def mlp_back_kernel(
    base, width, first, offs, upstream, gated, slope, gate, carried, p0, p1, p2, p3,
    total, right, placed,
):
    part = mlp_pull(
        base, width, offs, upstream, gated, slope, gate, (p0, p1, p2, p3), right, placed
    )
    total[...] = part if first else carried[...] + part


def mlp_back_last_kernel(
    base, width, offs, upstream, gated, slope, gate, carried, residual_grad, middle, gain,
    p0, p1, p2, p3, middle_grad, middle_grad_b, gain_grad, right, placed, sums, ordered,
):
    part = mlp_pull(
        base, width, offs, upstream, gated, slope, gate, (p0, p1, p2, p3), right, placed
    )
    sums[...] = carried[...] + part
    from_pieces(offs, sums, ordered)
    pulled, gains = norm_pull(middle[...], gain[...], ordered[...])
    result = residual_grad[...] + pulled
    middle_grad[...] = result
    middle_grad_b[...] = result.astype(BF16)
    gain_grad[...] = gains
    at = 3 * width
    store(right, at, result.astype(BF16))
    at += result.shape[1]
    rest = right.shape[1] - at
    if rest:
        store(right, at, jnp.zeros((result.shape[0], rest), BF16))


def run_mlp_back(offs, upstream, hidden, carried, pieces, chunk):
    tokens, features = upstream.shape
    width = WIDTHS[chunk]
    base = pieces[0].shape[1] - 3 * width
    right = struct((tokens, 3 * features), BF16)
    first = carried is None
    if first:
        carried = jnp.zeros((8, LANES), F32)
    return call(
        functools.partial(mlp_back_kernel, base, width, first),
        (struct((tokens, features), F32), right),
        [pltpu.VMEM((tokens, features), BF16)],
    )(offs, upstream, *hidden, carried, *pieces)


def run_mlp_back_last(offs, upstream, hidden, carried, residual_grad, middle, gain, pieces, chunk):
    tokens, features = upstream.shape
    width = WIDTHS[chunk]
    base = pieces[0].shape[1] - 3 * width
    right = struct((tokens, 3 * features), BF16)
    return call(
        functools.partial(mlp_back_last_kernel, base, width),
        (
            struct((tokens, features), F32),
            struct((tokens, features), BF16),
            struct((1, features), F32),
            right,
        ),
        [
            pltpu.VMEM((tokens, features), BF16),
            pltpu.VMEM((tokens, features), F32),
            pltpu.VMEM((tokens, features), F32),
        ],
    )(offs, upstream, *hidden, carried, residual_grad, middle, gain, *pieces)


def attend_back_kernel(
    offs, middle_grad, qkv, before, after, seg_q, seg_k, cosine, sine, p0, p1, p2, p3,
    query_grad, own_grad, rim_before, rim_after, extended, mixed_grad, extended_grad,
):
    tokens, features = middle_grad.shape
    extend(qkv, before, after, extended)
    placed = lax.dot_general(
        middle_grad[...], joined((p0, p1, p2, p3)), NT, preferred_element_type=F32
    ).astype(BF16)
    for k in range(features // LANES):
        lanes = pl.ds(pl.multiple_of(offs[k] * LANES, LANES), LANES)
        mixed_grad[:, lanes] = placed[:, k * LANES : (k + 1) * LANES]
    scale = jnp.asarray(1.0 / math.sqrt(HEAD_DIM), BF16)
    span = BLOCK + 2 * HALO
    row = lax.broadcasted_iota(jnp.int32, (span, BLOCK), 1)
    col = lax.broadcasted_iota(jnp.int32, (span, BLOCK), 0)
    near = (col >= row) & (col - row <= 2 * HALO)
    low = lax.broadcasted_iota(jnp.int32, (BLOCK, LANES), 1) < HEAD_DIM
    bias = []
    for block in range(tokens // BLOCK):
        base = block * BLOCK
        same = seg_q[:, base : base + BLOCK] == seg_k[base : base + span, :]
        one = jnp.where(near & same, 0.0, NEG)
        bias.append(jnp.concatenate([one, one], axis=1))

    def pair(index, carry):
        lanes = pl.ds(pl.multiple_of(index * LANES, LANES), LANES)
        value_lanes = pl.ds(pl.multiple_of(features + index * LANES, LANES), LANES)
        key_sums = []
        value_sums = []
        for block in range(tokens // BLOCK):
            base = block * BLOCK
            here = slice(base, base + BLOCK)
            queries = qkv[here, lanes]
            grads = mixed_grad[here, lanes]
            keys = extended[base : base + span, lanes]
            values = extended[base : base + span, value_lanes]
            chosen = stacked(queries * scale, low)
            chosen_grad = stacked(grads, low)
            scores = (
                lax.dot_general(keys, chosen, NT, preferred_element_type=F32) + bias[block]
            )
            expo = jnp.exp(scores - jnp.max(scores, axis=0, keepdims=True))
            probs = expo * (1.0 / jnp.sum(expo, axis=0, keepdims=True))
            prob_grad = lax.dot_general(values, chosen_grad, NT, preferred_element_type=F32)
            delta = jnp.sum(prob_grad * probs, axis=0, keepdims=True)
            score_grad = (probs * (prob_grad - delta)).astype(BF16)
            both = lax.dot_general(score_grad, keys, TN, preferred_element_type=F32)
            key_sum = jnp.dot(score_grad, chosen, preferred_element_type=F32)
            value_sum = jnp.dot(probs.astype(BF16), chosen_grad, preferred_element_type=F32)
            joint = jnp.where(low, both[:BLOCK], both[BLOCK:]) * (1.0 / math.sqrt(HEAD_DIM))
            query_grad[here, lanes] = turn_chunk(
                joint, cosine[here, :], sine[here, :], -1
            ).astype(BF16)
            key_sums.append(key_sum)
            value_sums.append(value_sum)
        for sums, place in ((key_sums, lanes), (value_sums, value_lanes)):
            over = 2 * HALO
            extended_grad[:BLOCK, place] = sums[0][:BLOCK]
            extended_grad[BLOCK : BLOCK + over, place] = sums[0][BLOCK:] + sums[1][:over]
            extended_grad[BLOCK + over :, place] = sums[1][over:]
        return carry

    lax.fori_loop(0, features // LANES, pair, 0)
    rim_before[...] = extended_grad[:HALO, :].astype(BF16)
    own_grad[...] = extended_grad[HALO : HALO + tokens, :]
    rim_after[...] = extended_grad[HALO + tokens :, :].astype(BF16)


def run_attend_back(offs, middle_grad, qkv, before, after, seg_q, seg_k, cosine, sine, pieces):
    tokens, features = middle_grad.shape
    rim = struct((HALO, 2 * features), BF16)
    return call(
        attend_back_kernel,
        (struct((tokens, features), BF16), struct((tokens, 2 * features), F32), rim, rim),
        [
            pltpu.VMEM((tokens + 2 * HALO, 2 * features), BF16),
            pltpu.VMEM((tokens, features), BF16),
            pltpu.VMEM((tokens + 2 * HALO, 2 * features), F32),
        ],
        grid=(1,),
        in_specs=[pl.BlockSpec(memory_space=pltpu.SMEM)]
        + [
            whole_spec(v.shape)
            for v in (middle_grad, qkv, before, after, seg_q, seg_k, cosine, sine)
        ]
        + proj_specs(pieces[0].shape[0], features),
        out_specs=(
            whole_spec((tokens, features)),
            whole_spec((tokens, 2 * features)),
            whole_spec((HALO, 2 * features)),
            whole_spec((HALO, 2 * features)),
        ),
    )(offs, middle_grad, qkv, before, after, seg_q, seg_k, cosine, sine, *pieces)


def qkv_back_kernel(
    offs, query_grad, own_grad, arrived_first, arrived_last, cosine, sine, x, gain, middle_grad,
    p0, p1, p2, p3, right, upstream, upstream_b, gain_grad, sums, ordered,
):
    step = pl.program_id(0)
    tokens, features = x.shape
    for part in range(3):

        @pl.when(step == part)
        def _():
            if part == 0:
                joint = query_grad[...]
            else:
                chunks = []
                for k in range(features // LANES):
                    at = (part - 1) * features + k * LANES
                    there = slice(at, at + LANES)
                    rows = [
                        own_grad[:HALO, there] + arrived_first[:, there].astype(F32),
                        own_grad[HALO : tokens - HALO, there],
                        own_grad[tokens - HALO :, there] + arrived_last[:, there].astype(F32),
                    ]
                    grads = jnp.concatenate(rows, axis=0)
                    if part == 1:
                        grads = turn_chunk(grads, cosine[...], sine[...], -1)
                    chunks.append(grads.astype(BF16))
                joint = jnp.concatenate(chunks, axis=1)
            store(right, part * features, joint)
            product = lax.dot_general(
                joint, joined((p0, p1, p2, p3)), NT, preferred_element_type=F32
            )
            sums[...] = product if part == 0 else sums[...] + product

    @pl.when(step == 2)
    def _():
        from_pieces(offs, sums, ordered)
        pulled, gains = norm_pull(x[...], gain[...], ordered[...])
        result = middle_grad[...] + pulled
        upstream[...] = result
        upstream_b[...] = result.astype(BF16)
        gain_grad[...] = gains


def run_qkv_back(
    offs, query_grad, own_grad, arrived_first, arrived_last, cosine, sine, x, gain, middle_grad, pieces
):
    tokens, features = x.shape
    whole = (query_grad, own_grad, arrived_first, arrived_last, cosine, sine, x, gain, middle_grad)
    outs = (
        struct((tokens, 3 * features), BF16),
        struct((tokens, features), F32),
        struct((tokens, features), BF16),
        struct((1, features), F32),
    )
    return call(
        qkv_back_kernel,
        outs,
        [pltpu.VMEM((tokens, features), F32), pltpu.VMEM((tokens, features), F32)],
        grid=(3,),
        in_specs=[pl.BlockSpec(memory_space=pltpu.SMEM)]
        + [whole_spec(v.shape) for v in whole]
        + piece_specs(pieces[0].shape[0], features),
        out_specs=tuple(whole_spec(out.shape) for out in outs),
    )(offs, *whole, *pieces)


def pick_kernel(which, *refs):
    pickers, lefts, (mine, theirs) = refs[:2], refs[2:-2], refs[-2:]
    half = pickers[0].shape[0] // 2
    for k, (picker, left) in enumerate(which):
        rows = lax.dot_general(
            pickers[picker][...], lefts[left][...], NT, preferred_element_type=F32
        ).astype(BF16)
        mine[k * half : (k + 1) * half, :] = rows[:half]
        theirs[k * half : (k + 1) * half, :] = rows[half:]


def run_pick(pickers, lefts, which):
    rows = len(which) * pickers[0].shape[0] // 2
    out = struct((rows, lefts[0].shape[0]), BF16)
    return call(functools.partial(pick_kernel, which), (out, out), smem=0)(*pickers, *lefts)


def exchange_kernel(plan, *refs):
    segments, stages = plan
    refs = list(refs)
    take = lambda count: [refs.pop(0) for _ in range(count)]
    adding, ending, far_ending, finishing = stages
    if segments:
        rights, rights_far = take(2), take(2)
        lefts = [take(2) for _ in segments]
    kept = take(2) if adding else None
    last = take(2) if ending else None
    come = take(2) if adding or ending else None
    near_pair = take(2) if far_ending else None
    far_pair = take(2) if finishing else None
    keep = take(2) if segments else None
    stay = take(2) if adding else None
    send = take(2) if segments or adding else None
    near_out = take(2) if ending else None
    far_out = take(2) if far_ending else None
    result = take(1)[0] if finishing else None

    def added(pair, rows, columns):
        return pair[0][rows, columns].astype(F32) + pair[1][rows, columns].astype(F32)

    def body(step):
        everything = slice(None)
        top = 0
        if segments:
            half, tile = keep[0].shape
            for (path, start, stop), (left, left_far) in zip(segments, lefts):
                low, high = max(start - step * tile, 0), min(stop - step * tile, tile)
                if low >= high:
                    continue
                columns = slice(low, high)
                total = jnp.dot(
                    jnp.concatenate([left[...], left_far[...]], axis=1),
                    jnp.concatenate(
                        [rights[path][:, columns], rights_far[path][:, columns]], axis=0
                    ),
                    preferred_element_type=F32,
                ).astype(BF16)
                keep[path][:, columns] = total[:half]
                send[path][:half, columns] = total[half:]
            top = half
        came = 0
        if adding:
            rows, tile = kept[0].shape
            half = rows // 2
            for path in range(2):
                total = kept[path][...].astype(F32) + come[path][:rows, :].astype(F32)
                stay[path][...] = total[:half].astype(BF16)
                send[1 - path][top : top + half, :] = total[half:].astype(BF16)
            came = rows
        if ending:
            rows, tile = last[0].shape
            half = rows // 2
            for path in range(2):
                at = (path * TILES + step) * tile
                total = last[path][...].astype(F32) + come[1 - path][
                    came : came + rows, :
                ].astype(F32)
                near_out[0][:, at : at + tile] = total[:half].astype(BF16)
                near_out[1][:, at : at + tile] = total[half:].astype(BF16)
        if step == 0 and far_ending:
            half = near_pair[0].shape[0] // 2
            far_out[0][...] = added(near_pair, slice(0, half), everything).astype(BF16)
            far_out[1][...] = added(near_pair, slice(half, 2 * half), everything).astype(BF16)
        if step == 0 and finishing:
            result[...] = added(far_pair, everything, everything).astype(result.dtype)

    for step in range(TILES):
        pl.when(pl.program_id(0) == step)(functools.partial(body, step))


class Exchange:
    def __init__(self, flow, rows, width, bits):
        self.flow = flow
        self.rows = rows
        self.width = width
        self.near, self.far = bits[:2]
        self.dtype = F32 if len(bits) == 2 else BF16
        self.kept = self.last = self.come = self.near_pair = self.far_pair = None

    def busy(self):
        return any((self.kept, self.last, self.near_pair, self.far_pair))

    def step(self, rights=None, segments=()):
        flow, rows, width = self.flow, self.rows, self.width
        tile = width // TILES
        args, specs, outs, out_specs = [], [], [], []

        def tiled(shape):
            return pl.BlockSpec((shape[0], tile), lambda j: (0, j))

        def give(pair, spec):
            if pair:
                args.extend(pair)
                specs.extend(spec(value.shape) for value in pair)

        def want(height, columns, spec, count=2, dtype=BF16):
            outs.extend([struct((height, columns), dtype)] * count)
            out_specs.extend([spec((height, columns))] * count)

        for right in rights or ():
            args += [right, right]
            block = (right.shape[0], tile)
            specs += [pl.BlockSpec(block, lambda j: (0, j))]
            specs += [pl.BlockSpec(block, lambda j: (0, TILES + j))]
        for _, _, _, left, place in segments:
            args += left
            specs += [pl.BlockSpec((rows, left[0].shape[1]), lambda j, at=place: (at, 0))] * 2
        give(self.kept, tiled)
        give(self.last, tiled)
        give(self.come if self.kept or self.last else None, tiled)
        give(self.near_pair, whole_spec)
        give(self.far_pair, whole_spec)
        height = 0
        if segments:
            want(rows // 2, width, tiled)
            height += rows // 2
        if self.kept:
            want(rows // 4, width, tiled)
            height += rows // 4
        if height:
            want(height, width, tiled)
        if self.last:
            want(rows // 8, 2 * width, whole_spec)
        if self.near_pair:
            want(rows // 16, 2 * width, whole_spec)
        if self.far_pair:
            want(rows // 16, 2 * width, whole_spec, 1, self.dtype)
        stages = tuple(map(bool, (self.kept, self.last, self.near_pair, self.far_pair)))
        plan = (
            tuple((path, start - path * width, stop - path * width) for path, start, stop, _, _ in segments),
            stages,
        )
        args[0] = flow.tie(args[0])
        results = list(
            call(
                functools.partial(exchange_kernel, plan),
                tuple(outs),
                grid=(TILES,),
                in_specs=specs,
                out_specs=tuple(out_specs),
            )(*args)
        )

        def got(wanted):
            return [results.pop(0), results.pop(0)] if wanted else None

        keep, stay, send = got(segments), got(self.kept), got(height)
        near, far = got(self.last), got(self.near_pair)
        result = results.pop(0) if self.far_pair else None
        self.kept, self.last = keep, stay
        self.come = send and [flow.swap(value, 1 + path) for path, value in enumerate(send)]
        self.near_pair = near and [near[0], flow.swap(near[1], self.near)]
        self.far_pair = far and [far[0], flow.swap(far[1], self.far)]
        return result


class Ending:
    def __init__(self, flow, value, bits, deliver):
        self.flow = flow
        self.bits = list(bits)
        self.deliver = deliver
        self.keep = value
        self.come = None

    def step(self):
        if self.come is not None:
            self.keep = self.keep.astype(F32) + self.flow.tie(self.come).astype(F32)
        if not self.bits:
            self.deliver(self.keep)
            return False
        half = self.keep.shape[0] // 2
        send = self.keep[half:].astype(BF16)
        self.keep = self.keep[:half].astype(BF16)
        self.come = self.flow.swap(send, self.bits.pop(0))
        return True


def rope_tables(position):
    inverse = jnp.power(THETA, -jnp.arange(0, HEAD_DIM, 2, dtype=F32) / HEAD_DIM)
    angles = position[:, None] * inverse[None, :]
    cosine, sine = jnp.cos(angles), jnp.sin(angles)
    return (
        jnp.concatenate([cosine, cosine, cosine, cosine], axis=-1),
        jnp.concatenate([-sine, sine, -sine, sine], axis=-1),
    )


def layout(positions, lengths, total):
    count = lengths.shape[0]
    blocks = (lengths + BLOCK - 1) // BLOCK
    first = (jnp.cumsum(blocks) - blocks) * BLOCK
    owner = jnp.sum((positions[:, None] >= first[None, :]).astype(jnp.int32), axis=1) - 1
    table = owner[:, None] == jnp.arange(count, dtype=jnp.int32)[None, :]
    start = jnp.sum(jnp.where(table, first[None, :], 0), axis=1)
    span = jnp.sum(jnp.where(table, lengths[None, :], 0), axis=1)
    local = positions - start
    inside = (positions >= 0) & (positions < total)
    valid = inside & (local < span)
    segment = jnp.where(inside, jnp.where(valid, owner, owner + count), -1)
    return (segment, local, valid)


def body(
    tokens,
    cotangent,
    lengths,
    block_perm,
    attn_gain,
    qkv_weight,
    proj_weight,
    mlp_gain,
    wide_weight,
    narrow_weight,
):
    flow = Phases()
    seq_index = lax.axis_index("seq")
    seq_count = lax.axis_size("seq")
    levels = seq_count.bit_length() - 1
    tok_dev = tokens.shape[1]
    features = tokens.shape[2]
    block_rows = tok_dev // BLK_DEV
    order_map = block_perm[0]
    target = order_map[0::BLK_DEV] // BLK_DEV
    source = jnp.arange(seq_count, dtype=jnp.int32)

    def holder(bit_level):
        low_mask = (1 << bit_level) - 1
        place = jnp.bitwise_or(
            jnp.bitwise_and(target, low_mask), jnp.bitwise_and(source, ~low_mask)
        )
        return jnp.sum(jnp.where(place == seq_index, source, 0))

    home_index = holder(levels)
    slot_of = lax.dynamic_slice_in_dim(order_map, home_index * BLK_DEV, BLK_DEV) % BLK_DEV
    crossed = slot_of[0] == 1

    def crossing(rows):
        turned = jnp.concatenate([rows[block_rows:], rows[:block_rows]], axis=0)
        return jnp.where(crossed, turned, rows)

    def crossed_over(bit_level, given):
        payload = holder(bit_level + 1 if given else bit_level)
        if not given:
            payload = jnp.sum(jnp.where(source == payload, target, 0))
        flips = jnp.right_shift(jnp.bitwise_xor(seq_index, payload), bit_level)
        return jnp.bitwise_and(flips, 1) == 1

    class Route:
        def __init__(self, rows, given, last=levels):
            self.rows = rows
            self.given = given
            self.levels = list(range(last))
            if given:
                self.levels.reverse()
            self.arrived = None

        def step(self):
            if self.arrived is not None:
                self.rows = jnp.where(
                    crossed_over(self.level, self.given), flow.tie(self.arrived), self.rows
                )
                self.arrived = None
            if self.levels:
                self.level = self.levels.pop(0)
                self.arrived = flow.swap(self.rows, 2 + self.level)
                return True
            return False

        def finish(self):
            while self.step():
                flow.next()
            return self.rows

    total = seq_count * tok_dev
    own_place = seq_index * tok_dev + jnp.arange(tok_dev, dtype=jnp.int32)
    key_place = seq_index * tok_dev - HALO + jnp.arange(tok_dev + 2 * HALO, dtype=jnp.int32)
    seg_query, local_query, valid_query = layout(own_place, lengths[0], total)
    seg_key, _, _ = layout(key_place, lengths[0], total)
    cosine, sine = rope_tables(local_query.astype(F32))
    seg_q_col, seg_q_row = seg_query[:, None], seg_query[None, :]
    seg_k_col, seg_k_row = seg_key[:, None], seg_key[None, :]
    offs = piece_order()
    bits_x, bits_y = stage_bits(True), stage_bits(False)
    picker_x, picker_y = row_picker(features, bits_x), row_picker(features, bits_y)

    gains = jnp.concatenate([attn_gain, mlp_gain], axis=0)
    gains = lax.all_gather(gains, "fsdp", axis=1, tiled=True).astype(F32)
    gains_a = [gains[layer : layer + 1] for layer in range(LAYERS)]
    gains_m = [gains[LAYERS + layer : LAYERS + layer + 1] for layer in range(LAYERS)]

    side = (seq_index % 2).astype(jnp.int32).reshape(1)
    arrays = (proj_weight, wide_weight, narrow_weight)
    items = []
    for layer in range(LAYERS):
        packs = run_pack(side, (qkv_weight,), layer) + run_pack(side, arrays, layer)
        items += [Weights(flow, *pack) for pack in packs]
    per_layer = len(items) // LAYERS
    tok_route, cot_route = Route(tokens[0], False), Route(cotangent[0], False, levels - 1)

    first_use = 3
    owns = {0: (0,), 1: (1, 3), 2: (2,), 4: (4,), 5: (5,), 6: (6,), 8: (7,)}
    phase = 0

    def transfers():
        if phase < len(items):
            items[phase].over_x()
        if 0 <= phase - 1 < len(items):
            items[phase - 1].over_y()
        if 0 <= phase - 2 < len(items):
            items[phase - 2].over_core()
        for place in owns.get(phase, ()):
            items[place].own()

    flow.keep(gains)
    while phase < first_use or tok_route.levels:
        transfers()
        tok_route.step()
        if phase == 0:
            cot_route.step()
            flow.keep(*(item.shard for item in items[1:]))
        phase += 1
        flow.next()
    tok_route.step()
    residual = crossing(tok_route.rows).astype(F32)
    cot_halves = []
    kept = []
    for layer in range(LAYERS):
        base = layer * per_layer
        transfers()
        qkv, normed, edge_first, edge_last = run_qkv(
            offs, flow.tie(residual), gains_a[layer], cosine, sine, items[base].pieces
        )
        flow.keep(normed)
        before = flow.shift(edge_last, True)
        after = flow.shift(edge_first, False)
        phase += 1
        flow.next()
        transfers()
        if layer == 0:
            cot_route.step()
        if layer and kept[-1][-1] is None:
            kept[-1][-1] = (mine, flow.swap(theirs, 0))
        start = residual
        mixed, middle, second = run_attend(
            offs, flow.tie(qkv), before, after, seg_q_col, seg_k_row, residual, gains_m[layer],
            items[base + 1].pieces,
        )
        residual = middle
        hidden = []
        for chunk in range(CHUNKS):
            if chunk:
                phase += 1
                flow.next()
                transfers()
                if layer == 0:
                    if not cot_halves:
                        cot_rows = cot_route.finish()
                        for half in (cot_rows[:block_rows], cot_rows[block_rows:]):
                            cot_halves.append(Route(half, False))
                            cot_halves[-1].levels = [levels - 1]
                    cot_halves[chunk - 1].step()
            residual, gated, slope, gate = run_mlp(
                offs, second, flow.tie(residual), items[base + 1 + chunk].pieces, chunk
            )
            flow.keep(residual, gated)
            hidden.append((gated, slope, gate))
            if chunk == 1:
                lefts = (normed, mixed, second)
                which = ((0, 0), (1, 0), (1, 1), (0, 2), (1, 2))
                mine, theirs = run_pick((picker_x, picker_y), lefts, which)
                flow.keep(theirs)
        picks = None
        if layer == LAYERS - 1:
            flow.next()
            picks = (mine, flow.swap(theirs, 0))
        kept.append([start, qkv, before, after, middle, hidden, picks])
        phase += 1
        flow.next()

    packed_cot = crossing(jnp.concatenate([half.finish() for half in cot_halves], axis=0))
    upstream_b = packed_cot * valid_query[:, None].astype(BF16)
    upstream = upstream_b.astype(F32)

    def both_halves(rows):
        rows = crossing(rows)
        return [Route(rows[:block_rows], True), Route(rows[block_rows:], True)]

    out_routes = both_halves(residual.astype(BF16))

    late = bits_x[2:]
    exchange = Exchange(flow, features // 2, 3 * features // 2, late)
    endings = []
    sums = {}
    count = 0
    width = 3 * features // 2

    def settle(done):
        nonlocal count
        if done is None:
            return
        deliver = functools.partial(sums.__setitem__, count)
        count += 1
        if len(late) > 2:
            endings.append(Ending(flow, done, late[2:], deliver))
        else:
            deliver(done)

    def step_endings():
        for item in list(endings):
            if not item.step():
                endings.remove(item)

    def group(right, parts):
        segments = []
        at = 0
        for columns, lefts in parts:
            for path in range(2):
                low = max(at, path * width)
                high = min(at + columns, (path + 1) * width)
                if low < high:
                    segments.append((path, low, high, lefts[path][:2], lefts[path][2]))
            at += columns
        return list(right), tuple(segments)

    terms = [None] * LAYERS
    made, ready = None, None

    def backward_phase():
        nonlocal made, ready
        flow.next()
        moving = bool(made or ready or exchange.busy())
        if ready or exchange.busy():
            settle(exchange.step(*(group(*ready) if ready else ())))
        ready = None
        if made:
            right, parts = made
            ready = ((right, flow.swap(right, 0)), parts)
        made = None
        step_endings()
        return moving

    for layer in reversed(range(LAYERS)):
        start, qkv, before, after, middle, hidden, picks = kept[layer]
        base = layer * per_layer
        normed_x, normed_y, mixed_y, second_x, second_y = (picks + (row,) for row in range(5))
        carried = None
        upstream_left = None
        for chunk in reversed(range(CHUNKS)):
            if layer < LAYERS - 1 or chunk < CHUNKS - 1:
                backward_phase()
            pieces = items[base + 1 + chunk].pieces
            if upstream_left is None:
                mine, theirs = run_pick(
                    (picker_x, picker_y), (flow.tie(upstream_b),), ((0, 0), (1, 0))
                )
                flow.keep(theirs)
                upstream_left = []
            elif not upstream_left:
                far = flow.swap(theirs, 0)
                upstream_left += [(mine, far, path) for path in range(2)]
            if layer == LAYERS - 1 and chunk:
                out_routes[CHUNKS - 1 - chunk].step()
            args = (offs, flow.tie(upstream_b), hidden[chunk], carried)
            columns = WIDTHS[chunk]
            parts = [
                (columns, upstream_left),
                (2 * columns, (second_x, second_y)),
            ]
            if chunk:
                carried, right = run_mlp_back(*args, pieces, chunk)
                flow.keep(carried)
            else:
                middle_grad, middle_grad_b, mlp_term, right = run_mlp_back_last(
                    *args, upstream, middle, gains_m[layer], pieces, chunk
                )
                parts.append((2 * width - 3 * columns, (None, mixed_y)))
                query_grad, own_grad, rim_before, rim_after = run_attend_back(
                    offs, middle_grad_b, qkv, before, after, seg_q_row, seg_k_col, cosine, sine, pieces
                )
                flow.keep(query_grad, own_grad)
                arrived_first = flow.shift(rim_after, True)
                arrived_last = flow.shift(rim_before, False)
            flow.keep(right)
            made = (right, parts)
        backward_phase()
        right, upstream, upstream_b, attn_term = run_qkv_back(
            offs, flow.tie(query_grad), own_grad, arrived_first, arrived_last, cosine, sine, start,
            gains_a[layer], middle_grad, items[base].pieces,
        )
        if layer:
            for route in out_routes:
                route.step()
        flow.keep(upstream_b, right)
        made = (right, [(2 * width, (normed_x, normed_y))])
        terms[layer] = (attn_term, mlp_term)
    backward_phase()
    grad_routes = both_halves(flow.tie(upstream_b))
    grad_routes[0].step()
    vectors = [terms[layer][0] for layer in range(LAYERS)]
    vectors += [terms[layer][1] for layer in range(LAYERS)]
    gain_sums = lax.dot_general(
        flow.tie(jnp.concatenate(vectors, axis=0)), picker_x.astype(F32), NT, precision=lax.Precision.HIGHEST
    )
    gain_bits = [0] + list(bits_x)
    while backward_phase() or endings or gain_bits:
        for route in grad_routes:
            route.step()
        if not grad_routes[0].levels:
            for route in out_routes:
                route.step()
        for bit in gain_bits[: 1 if len(gain_bits) > 2 else 2]:
            half = gain_sums.shape[1] // 2
            gain_sums = gain_sums[:, :half] + flow.swap(gain_sums[:, half:], bit)
        gain_bits = gain_bits[1 if len(gain_bits) > 2 else 2 :]
    block_out, token_grad = (
        jnp.concatenate([route.finish() for route in routes], axis=0)
        for routes in (out_routes, grad_routes)
    )

    def pieces_of(layer):
        at = per_layer * (LAYERS - 1 - layer)
        parts = {chunk: sums[at + CHUNKS - 1 - chunk] for chunk in range(CHUNKS)}
        return parts, sums[at + CHUNKS]

    def hidden_sum(parts, role):
        columns = [
            parts[chunk][:, role * WIDTHS[chunk] : (role + 1) * WIDTHS[chunk]]
            for chunk in range(CHUNKS)
        ]
        return jnp.concatenate(columns, axis=1)[:, :FF]

    wide, narrow, proj, qkv_sum = [], [], [], []
    for layer in range(LAYERS):
        parts, attend = pieces_of(layer)
        narrow.append(hidden_sum(parts, 0))
        wide.append(jnp.concatenate([hidden_sum(parts, 1), hidden_sum(parts, 2)], axis=1))
        proj.append(parts[0][:, 3 * WIDTHS[0] : 3 * WIDTHS[0] + features])
        qkv_sum.append(attend)
    return (
        block_out[None],
        token_grad[None],
        gain_sums[:LAYERS],
        jnp.stack(qkv_sum),
        jnp.stack(proj),
        gain_sums[LAYERS:],
        jnp.stack(wide),
        jnp.stack(narrow),
    )


def solution(mesh):
    in_specs = (
        P("fsdp", "seq", None),
        P("fsdp", "seq", None),
        P("fsdp", None),
        P("fsdp", None),
        P(None, "fsdp"),
        P(None, "fsdp", None),
        P(None, "fsdp", None),
        P(None, "fsdp"),
        P(None, "fsdp", None),
        P(None, "fsdp", None),
    )
    out_specs = (
        P("fsdp", "seq", None),
        P("fsdp", "seq", None),
        P(None, ("seq", "fsdp")),
        P(None, ("seq", "fsdp"), None),
        P(None, ("seq", "fsdp"), None),
        P(None, ("seq", "fsdp")),
        P(None, ("seq", "fsdp"), None),
        P(None, ("seq", "fsdp"), None),
    )
    return jax.shard_map(body, mesh=mesh, in_specs=in_specs, out_specs=out_specs, check_vma=False)
```

```python
import functools
import math

import jax
import jax.numpy as jnp
from jax import lax
from jax.experimental import pallas as pl
from jax.experimental.pallas import tpu as pltpu
from jax.sharding import PartitionSpec as P

HEADS = 16
HEAD_DIM = 64
FF = 2624
WINDOW = 128
BLOCK = 128
BLK_DEV = 2
LAYERS = 2

NEG = -1e30
EPS = 1e-05
THETA = 10000.0

AXES = ("seq", "fsdp")
LANES = 128
HALO = WINDOW // 2
SPLIT = (5, 8, 8)
FF_PAD = sum(SPLIT) * LANES
WIDTHS = tuple(blocks * LANES for blocks in SPLIT)
STARTS = tuple(sum(WIDTHS[:k]) for k in range(len(WIDTHS)))
CHUNKS = len(SPLIT)
TILES = 3
F32 = jnp.float32
BF16 = jnp.bfloat16
VMEM_LIMIT = 20 * 1024 * 1024
NT = (((1,), (1,)), ((), ()))
TN = (((0,), (0,)), ((), ()))


class Phases:
    def __init__(self):
        self.gate = ()
        self.made = []

    def next(self):
        self.gate = tuple(self.made)
        self.made = []

    def tie(self, value):
        return lax.optimization_barrier((value,) + self.gate)[0] if self.gate else value

    def keep(self, *values):
        self.made += values

    def route(self, value, axes, pairs):
        result = lax.ppermute(self.tie(value), axes, pairs)
        self.made.append(result)
        return result

    def swap(self, value, bit):
        count = lax.axis_size("seq") * lax.axis_size("fsdp")
        return self.route(value, AXES, [(i, i ^ (1 << bit)) for i in range(count)])

    def shift(self, value, up):
        pairs = [(i, i + 1) for i in range(lax.axis_size("seq") - 1)]
        if not up:
            pairs = [(b, a) for a, b in pairs]
        return self.route(value, "seq", pairs)


def flat_index():
    return lax.axis_index("seq") * lax.axis_size("fsdp") + lax.axis_index("fsdp")


class Weights:
    def __init__(self, flow, shard, sent):
        self.flow = flow
        self.shard = shard
        self.sent = sent

    def own(self):
        self.own_core = self.flow.swap(self.shard, 0)

    def over_x(self):
        self.far_x = self.flow.swap(self.sent, 1)

    def over_y(self):
        self.far_y = self.flow.swap(self.far_x, 2)

    def over_core(self):
        far = jnp.concatenate([self.far_x, self.flow.tie(self.far_y)], axis=0)
        self.pieces = (self.shard, far, self.own_core, self.flow.swap(far, 0))


def piece_order():
    quarter = lax.axis_index("fsdp")
    side = lax.axis_index("seq") % 2
    one = 1 - side
    order = []
    for core in (quarter, quarter ^ 1):
        order += [core * 2, core * 2 + 1, (core ^ 2) * 2 + side, (core ^ 2) * 2 + one]
    return jnp.stack(order).astype(jnp.int32)


def stage_bits(first_x):
    levels = lax.axis_size("seq").bit_length() - 1
    rest = [2 + level for level in range(1, levels)]
    return ([1, 2] if first_x else [2, 1]) + rest


def row_order(features, bits):
    order = [0] + bits
    per_device = features >> len(order)
    rows = jnp.arange(features, dtype=jnp.int32)
    place = rows // per_device
    owner = flat_index()
    for step, bit in enumerate(order):
        taken = (place >> (len(order) - 1 - step)) & 1
        owner = owner ^ (taken << bit)
    return owner * per_device + rows % per_device


def row_picker(features, bits):
    order = row_order(features, bits)
    grid = jnp.arange(features, dtype=jnp.int32)
    return (order[:, None] == grid[None, :]).astype(BF16)


def call(kernel, outs, scratch=(), smem=1, grid=None, in_specs=None, out_specs=None, limit=VMEM_LIMIT):
    params = dict(
        compiler_params=pltpu.CompilerParams(vmem_limit_bytes=limit),
        out_shape=outs,
        scratch_shapes=list(scratch),
        cost_estimate=pl.CostEstimate(
            flops=0, bytes_accessed=0, transcendentals=0
        ),
    )
    if grid is not None:
        params["grid"] = grid

    def run(*args):
        specs = in_specs
        if specs is None:
            specs = [pl.BlockSpec(memory_space=pltpu.SMEM)] * smem
            specs += [pl.BlockSpec(memory_space=pltpu.VMEM)] * (len(args) - smem)
        results = out_specs
        if results is None:
            results = jax.tree.map(lambda _: pl.BlockSpec(memory_space=pltpu.VMEM), outs)
        return pl.pallas_call(kernel, in_specs=specs, out_specs=results, **params)(*args)

    return run


def struct(shape, dtype):
    return jax.ShapeDtypeStruct(shape, dtype)


def to_pieces(offs, source, target):
    for k in range(source.shape[1] // LANES):
        start = pl.multiple_of(offs[k] * LANES, LANES)
        target[:, k * LANES : (k + 1) * LANES] = source[:, pl.ds(start, LANES)]


def from_pieces(offs, source, target):
    for k in range(source.shape[1] // LANES):
        start = pl.multiple_of(offs[k] * LANES, LANES)
        target[:, pl.ds(start, LANES)] = source[:, k * LANES : (k + 1) * LANES]


def joined(pieces, columns=slice(None)):
    return jnp.concatenate([piece[:, columns] for piece in pieces], axis=0)


def statistics(values):
    average = jnp.mean(values, axis=-1, keepdims=True)
    centred = values - average
    spread = jnp.mean(centred * centred, axis=-1, keepdims=True)
    rho = lax.rsqrt(spread + EPS)
    return centred, rho


def norm_pull(values, gain, grad):
    centred, rho = statistics(values)
    unit = centred * rho
    scaled = grad * gain
    mean_a = jnp.mean(scaled, axis=-1, keepdims=True)
    mean_b = jnp.mean(scaled * unit, axis=-1, keepdims=True)
    return rho * (scaled - mean_a - unit * mean_b), jnp.sum(grad * unit, axis=0, keepdims=True)


def turn_chunk(values, cosine, sine, sign):
    lane = lax.broadcasted_iota(jnp.int32, values.shape, 1)
    ahead = pltpu.roll(values, LANES - HEAD_DIM // 2, 1)
    behind = pltpu.roll(values, HEAD_DIM // 2, 1)
    turned = jnp.where(lane % HEAD_DIM < HEAD_DIM // 2, ahead, behind)
    if sign > 0:
        return values * cosine + turned * sine
    return values * cosine - turned * sine


def pack_one_kernel(side, first, own, sent):
    half = first.shape[1] // 2
    own[...] = first[0]
    sent[...] = first[0, pl.ds(pl.multiple_of(side[0] * half, half), half), :]


def pack_kernel(side, second, wide, narrow, *outs):
    half = wide.shape[1] // 2
    features = second.shape[2]
    outs[0][:, :features] = second[0]
    for chunk in range(CHUNKS):
        own = outs[2 * chunk]
        at = features if chunk == 0 else 0
        width = WIDTHS[chunk]
        start, stop = STARTS[chunk], min(STARTS[chunk] + width, FF)
        for array, base in ((narrow, 0), (wide, 0), (wide, FF)):
            if stop - start < width:
                own[:, at + width - LANES : at + width] = jnp.zeros((2 * half, LANES), BF16)
            own[:, at : at + stop - start] = array[0, :, base + start : base + stop]
            at += width
    for k in range(0, len(outs), 2):
        outs[k + 1][...] = outs[k][pl.ds(pl.multiple_of(side[0] * half, half), half), :]


def run_pack(side, arrays, layer):
    rows = arrays[0].shape[1]
    one = len(arrays) == 1
    features = arrays[0].shape[2]
    columns = [features + 3 * WIDTHS[0]] + [3 * width for width in WIDTHS[1:]]
    if one:
        columns = [features]
    outs = tuple(struct((height, width), BF16) for width in columns for height in (rows, rows // 2))
    flat = call(
        pack_one_kernel if one else pack_kernel,
        outs,
        grid=(1,),
        in_specs=[pl.BlockSpec(memory_space=pltpu.SMEM)]
        + [pl.BlockSpec((1,) + v.shape[1:], lambda j: (layer, 0, 0)) for v in arrays],
        out_specs=tuple(whole_spec(out.shape) for out in outs),
    )(side, *arrays)
    return [flat[k : k + 2] for k in range(0, len(flat), 2)]


def qkv_kernel(offs, x, gain, cosine, sine, p0, p1, p2, p3, out, normed, first, last, placed):
    step = pl.program_id(0)
    tokens = x.shape[0]

    @pl.when(step == 0)
    def _():
        centred, rho = statistics(x[...])
        normed[...] = (centred * rho * gain[...]).astype(BF16)
        to_pieces(offs, normed, placed)

    product = jnp.dot(
        placed[...], joined((p0, p1, p2, p3)), preferred_element_type=F32
    )

    @pl.when(step < 2)
    def _():
        for k in range(product.shape[1] // LANES):
            part = slice(k * LANES, (k + 1) * LANES)
            out[:, part] = turn_chunk(product[:, part], cosine[...], sine[...], 1).astype(BF16)

    @pl.when(step == 2)
    def _():
        out[...] = product.astype(BF16)

    first[...] = out[:HALO, :]
    last[...] = out[tokens - HALO :, :]


def piece_specs(rows, columns):
    return [pl.BlockSpec((rows, columns), lambda j: (0, j))] * 4


def proj_specs(rows, columns):
    return [pl.BlockSpec((rows, columns), lambda j: (0, 0))] * 4


def whole_spec(shape):
    return pl.BlockSpec(shape, lambda j: tuple(0 for _ in shape))


def run_qkv(offs, x, gain, cosine, sine, pieces):
    tokens, features = x.shape
    return call(
        qkv_kernel,
        (
            struct((tokens, 3 * features), BF16),
            struct((tokens, features), BF16),
            struct((HALO, 2 * features), BF16),
            struct((HALO, 2 * features), BF16),
        ),
        [pltpu.VMEM((tokens, features), BF16)],
        grid=(3,),
        in_specs=[pl.BlockSpec(memory_space=pltpu.SMEM)]
        + [whole_spec(v.shape) for v in (x, gain, cosine, sine)]
        + piece_specs(pieces[0].shape[0], features),
        out_specs=(
            pl.BlockSpec((tokens, features), lambda j: (0, j)),
            whole_spec((tokens, features)),
            pl.BlockSpec((HALO, features), lambda j: (0, jnp.maximum(j - 1, 0))),
            pl.BlockSpec((HALO, features), lambda j: (0, jnp.maximum(j - 1, 0))),
        ),
    )(offs, x, gain, cosine, sine, *pieces)


def stacked(rows, low):
    zero = jnp.zeros_like(rows)
    return jnp.concatenate([jnp.where(low, rows, zero), jnp.where(low, zero, rows)], axis=0)


def extend(qkv, before, after, extended):
    tokens, features = qkv.shape[0], qkv.shape[1] // 3
    extended[:HALO, :] = before[...]
    extended[HALO : HALO + tokens, :] = qkv[:, features:]
    extended[HALO + tokens :, :] = after[...]


def attend_kernel(
    offs, qkv, before, after, seg_q, seg_k, x, gain,
    p0, p1, p2, p3, mixed, middle, second, extended, placed,
):
    tokens, features = x.shape
    extend(qkv, before, after, extended)
    scale = jnp.asarray(1.0 / math.sqrt(HEAD_DIM), BF16)
    span = BLOCK + 2 * HALO
    row = lax.broadcasted_iota(jnp.int32, (BLOCK, span), 0)
    col = lax.broadcasted_iota(jnp.int32, (BLOCK, span), 1)
    near = (col >= row) & (col - row <= 2 * HALO)
    low = lax.broadcasted_iota(jnp.int32, (BLOCK, LANES), 1) < HEAD_DIM
    bias = []
    for block in range(tokens // BLOCK):
        base = block * BLOCK
        same = seg_q[base : base + BLOCK, :] == seg_k[:, base : base + span]
        one = jnp.where(near & same, 0.0, NEG)
        bias.append(jnp.concatenate([one, one], axis=0))

    def pair(index, carry):
        lanes = pl.ds(pl.multiple_of(index * LANES, LANES), LANES)
        value_lanes = pl.ds(pl.multiple_of(features + index * LANES, LANES), LANES)
        for block in range(tokens // BLOCK):
            base = block * BLOCK
            queries = qkv[base : base + BLOCK, lanes]
            keys = extended[base : base + span, lanes]
            values = extended[base : base + span, value_lanes]
            scores = (
                lax.dot_general(stacked(queries * scale, low), keys, NT, preferred_element_type=F32)
                + bias[block]
            )
            expo = jnp.exp(scores - jnp.max(scores, axis=-1, keepdims=True))
            probs = expo * (1.0 / jnp.sum(expo, axis=-1, keepdims=True))
            both = jnp.dot(probs.astype(BF16), values, preferred_element_type=F32)
            mixed[base : base + BLOCK, lanes] = jnp.where(low, both[:BLOCK], both[BLOCK:]).astype(BF16)
        return carry

    lax.fori_loop(0, features // LANES, pair, 0)
    to_pieces(offs, mixed, placed)
    total = x[...] + jnp.dot(
        placed[...], joined((p0, p1, p2, p3)), preferred_element_type=F32
    )
    middle[...] = total
    centred, rho = statistics(total)
    second[...] = (centred * rho * gain[...]).astype(BF16)


def run_attend(offs, qkv, before, after, seg_q, seg_k, x, gain, pieces):
    tokens, features = x.shape
    return call(
        attend_kernel,
        (
            struct((tokens, features), BF16),
            struct((tokens, features), F32),
            struct((tokens, features), BF16),
        ),
        [
            pltpu.VMEM((tokens + 2 * HALO, 2 * features), BF16),
            pltpu.VMEM((tokens, features), BF16),
        ],
        grid=(1,),
        in_specs=[pl.BlockSpec(memory_space=pltpu.SMEM)]
        + [whole_spec(v.shape) for v in (qkv, before, after, seg_q, seg_k, x, gain)]
        + proj_specs(pieces[0].shape[0], features),
        out_specs=(whole_spec((tokens, features)),) * 3,
    )(offs, qkv, before, after, seg_q, seg_k, x, gain, *pieces)


def chunk_parts(pieces, base, width):
    return [
        joined(pieces, slice(base + k * width, base + (k + 1) * width)) for k in range(3)
    ]


def mlp_kernel(
    base, width, offs, second, carried, p0, p1, p2, p3, total, gated, slope, gate, placed, part
):
    output, first, other = chunk_parts((p0, p1, p2, p3), base, width)
    to_pieces(offs, second, placed)
    source = placed[...]
    hidden = jnp.dot(source, first, preferred_element_type=F32)
    factor = jnp.dot(source, other, preferred_element_type=F32)
    normal = 0.5 * (1.0 + lax.erf(hidden * math.sqrt(0.5)))
    density = jnp.exp(-0.5 * hidden * hidden) * (1.0 / math.sqrt(2.0 * math.pi))
    active = hidden * normal
    product = (active * factor).astype(BF16)
    gated[...] = product
    slope[...] = ((normal + hidden * density) * factor).astype(BF16)
    gate[...] = active.astype(BF16)
    part[...] = lax.dot_general(product, output, NT, preferred_element_type=F32)
    for k in range(part.shape[1] // LANES):
        lanes = pl.ds(pl.multiple_of(offs[k] * LANES, LANES), LANES)
        total[:, lanes] = carried[:, lanes] + part[:, k * LANES : (k + 1) * LANES]


def run_mlp(offs, second, carried, pieces, chunk):
    tokens, features = second.shape
    width = WIDTHS[chunk]
    base = pieces[0].shape[1] - 3 * width
    hidden = struct((tokens, width), BF16)
    return call(
        functools.partial(mlp_kernel, base, width),
        (struct((tokens, features), F32), hidden, hidden, hidden),
        [pltpu.VMEM((tokens, features), BF16), pltpu.VMEM((tokens, features), F32)],
    )(offs, second, carried, *pieces)


def mlp_pull(base, width, offs, upstream, gated, slope, gate, pieces, right, placed):
    output, first, other = chunk_parts(pieces, base, width)
    to_pieces(offs, upstream, placed)
    gated_grad = jnp.dot(placed[...], output, preferred_element_type=F32)
    input_grad = (slope[...].astype(F32) * gated_grad).astype(BF16)
    gate_grad = (gate[...].astype(F32) * gated_grad).astype(BF16)
    store(right, 0, gated[...])
    store(right, width, input_grad)
    store(right, 2 * width, gate_grad)
    return lax.dot_general(input_grad, first, NT, preferred_element_type=F32) + lax.dot_general(
        gate_grad, other, NT, preferred_element_type=F32
    )


def store(target, at, value):
    target[:, at : at + value.shape[1]] = value


def mlp_back_kernel(
    base, width, first, offs, upstream, gated, slope, gate, carried, p0, p1, p2, p3,
    total, right, placed,
):
    part = mlp_pull(
        base, width, offs, upstream, gated, slope, gate, (p0, p1, p2, p3), right, placed
    )
    total[...] = part if first else carried[...] + part


def mlp_back_last_kernel(
    base, width, offs, upstream, gated, slope, gate, carried, residual_grad, middle, gain,
    p0, p1, p2, p3, middle_grad, middle_grad_b, gain_grad, right, placed, sums, ordered,
):
    part = mlp_pull(
        base, width, offs, upstream, gated, slope, gate, (p0, p1, p2, p3), right, placed
    )
    sums[...] = carried[...] + part
    from_pieces(offs, sums, ordered)
    pulled, gains = norm_pull(middle[...], gain[...], ordered[...])
    result = residual_grad[...] + pulled
    middle_grad[...] = result
    middle_grad_b[...] = result.astype(BF16)
    gain_grad[...] = gains
    at = 3 * width
    store(right, at, result.astype(BF16))
    at += result.shape[1]
    rest = right.shape[1] - at
    if rest:
        store(right, at, jnp.zeros((result.shape[0], rest), BF16))


def run_mlp_back(offs, upstream, hidden, carried, pieces, chunk):
    tokens, features = upstream.shape
    width = WIDTHS[chunk]
    base = pieces[0].shape[1] - 3 * width
    right = struct((tokens, 3 * features), BF16)
    first = carried is None
    if first:
        carried = jnp.zeros((8, LANES), F32)
    return call(
        functools.partial(mlp_back_kernel, base, width, first),
        (struct((tokens, features), F32), right),
        [pltpu.VMEM((tokens, features), BF16)],
    )(offs, upstream, *hidden, carried, *pieces)


def run_mlp_back_last(offs, upstream, hidden, carried, residual_grad, middle, gain, pieces, chunk):
    tokens, features = upstream.shape
    width = WIDTHS[chunk]
    base = pieces[0].shape[1] - 3 * width
    right = struct((tokens, 3 * features), BF16)
    return call(
        functools.partial(mlp_back_last_kernel, base, width),
        (
            struct((tokens, features), F32),
            struct((tokens, features), BF16),
            struct((1, features), F32),
            right,
        ),
        [
            pltpu.VMEM((tokens, features), BF16),
            pltpu.VMEM((tokens, features), F32),
            pltpu.VMEM((tokens, features), F32),
        ],
    )(offs, upstream, *hidden, carried, residual_grad, middle, gain, *pieces)


def attend_back_kernel(
    offs, middle_grad, qkv, before, after, seg_q, seg_k, cosine, sine, p0, p1, p2, p3,
    query_grad, own_grad, rim_before, rim_after, extended, mixed_grad, extended_grad,
):
    tokens, features = middle_grad.shape
    extend(qkv, before, after, extended)
    placed = lax.dot_general(
        middle_grad[...], joined((p0, p1, p2, p3)), NT, preferred_element_type=F32
    ).astype(BF16)
    for k in range(features // LANES):
        lanes = pl.ds(pl.multiple_of(offs[k] * LANES, LANES), LANES)
        mixed_grad[:, lanes] = placed[:, k * LANES : (k + 1) * LANES]
    scale = jnp.asarray(1.0 / math.sqrt(HEAD_DIM), BF16)
    span = BLOCK + 2 * HALO
    row = lax.broadcasted_iota(jnp.int32, (span, BLOCK), 1)
    col = lax.broadcasted_iota(jnp.int32, (span, BLOCK), 0)
    near = (col >= row) & (col - row <= 2 * HALO)
    low = lax.broadcasted_iota(jnp.int32, (BLOCK, LANES), 1) < HEAD_DIM
    bias = []
    for block in range(tokens // BLOCK):
        base = block * BLOCK
        same = seg_q[:, base : base + BLOCK] == seg_k[base : base + span, :]
        one = jnp.where(near & same, 0.0, NEG)
        bias.append(jnp.concatenate([one, one], axis=1))

    def pair(index, carry):
        lanes = pl.ds(pl.multiple_of(index * LANES, LANES), LANES)
        value_lanes = pl.ds(pl.multiple_of(features + index * LANES, LANES), LANES)
        key_sums = []
        value_sums = []
        for block in range(tokens // BLOCK):
            base = block * BLOCK
            here = slice(base, base + BLOCK)
            queries = qkv[here, lanes]
            grads = mixed_grad[here, lanes]
            keys = extended[base : base + span, lanes]
            values = extended[base : base + span, value_lanes]
            chosen = stacked(queries * scale, low)
            chosen_grad = stacked(grads, low)
            scores = (
                lax.dot_general(keys, chosen, NT, preferred_element_type=F32) + bias[block]
            )
            expo = jnp.exp(scores - jnp.max(scores, axis=0, keepdims=True))
            probs = expo * (1.0 / jnp.sum(expo, axis=0, keepdims=True))
            prob_grad = lax.dot_general(values, chosen_grad, NT, preferred_element_type=F32)
            delta = jnp.sum(prob_grad * probs, axis=0, keepdims=True)
            score_grad = (probs * (prob_grad - delta)).astype(BF16)
            both = lax.dot_general(score_grad, keys, TN, preferred_element_type=F32)
            key_sum = jnp.dot(score_grad, chosen, preferred_element_type=F32)
            value_sum = jnp.dot(probs.astype(BF16), chosen_grad, preferred_element_type=F32)
            joint = jnp.where(low, both[:BLOCK], both[BLOCK:]) * (1.0 / math.sqrt(HEAD_DIM))
            query_grad[here, lanes] = turn_chunk(
                joint, cosine[here, :], sine[here, :], -1
            ).astype(BF16)
            key_sums.append(key_sum)
            value_sums.append(value_sum)
        for sums, place in ((key_sums, lanes), (value_sums, value_lanes)):
            over = 2 * HALO
            extended_grad[:BLOCK, place] = sums[0][:BLOCK]
            extended_grad[BLOCK : BLOCK + over, place] = sums[0][BLOCK:] + sums[1][:over]
            extended_grad[BLOCK + over :, place] = sums[1][over:]
        return carry

    lax.fori_loop(0, features // LANES, pair, 0)
    rim_before[...] = extended_grad[:HALO, :].astype(BF16)
    own_grad[...] = extended_grad[HALO : HALO + tokens, :]
    rim_after[...] = extended_grad[HALO + tokens :, :].astype(BF16)


def run_attend_back(offs, middle_grad, qkv, before, after, seg_q, seg_k, cosine, sine, pieces):
    tokens, features = middle_grad.shape
    rim = struct((HALO, 2 * features), BF16)
    return call(
        attend_back_kernel,
        (struct((tokens, features), BF16), struct((tokens, 2 * features), F32), rim, rim),
        [
            pltpu.VMEM((tokens + 2 * HALO, 2 * features), BF16),
            pltpu.VMEM((tokens, features), BF16),
            pltpu.VMEM((tokens + 2 * HALO, 2 * features), F32),
        ],
        grid=(1,),
        in_specs=[pl.BlockSpec(memory_space=pltpu.SMEM)]
        + [
            whole_spec(v.shape)
            for v in (middle_grad, qkv, before, after, seg_q, seg_k, cosine, sine)
        ]
        + proj_specs(pieces[0].shape[0], features),
        out_specs=(
            whole_spec((tokens, features)),
            whole_spec((tokens, 2 * features)),
            whole_spec((HALO, 2 * features)),
            whole_spec((HALO, 2 * features)),
        ),
    )(offs, middle_grad, qkv, before, after, seg_q, seg_k, cosine, sine, *pieces)


def qkv_back_kernel(
    offs, query_grad, own_grad, arrived_first, arrived_last, cosine, sine, x, gain, middle_grad,
    p0, p1, p2, p3, right, upstream, upstream_b, gain_grad, sums, ordered,
):
    step = pl.program_id(0)
    tokens, features = x.shape
    for part in range(3):

        @pl.when(step == part)
        def _():
            if part == 0:
                joint = query_grad[...]
            else:
                chunks = []
                for k in range(features // LANES):
                    at = (part - 1) * features + k * LANES
                    there = slice(at, at + LANES)
                    rows = [
                        own_grad[:HALO, there] + arrived_first[:, there].astype(F32),
                        own_grad[HALO : tokens - HALO, there],
                        own_grad[tokens - HALO :, there] + arrived_last[:, there].astype(F32),
                    ]
                    grads = jnp.concatenate(rows, axis=0)
                    if part == 1:
                        grads = turn_chunk(grads, cosine[...], sine[...], -1)
                    chunks.append(grads.astype(BF16))
                joint = jnp.concatenate(chunks, axis=1)
            store(right, part * features, joint)
            product = lax.dot_general(
                joint, joined((p0, p1, p2, p3)), NT, preferred_element_type=F32
            )
            sums[...] = product if part == 0 else sums[...] + product

    @pl.when(step == 2)
    def _():
        from_pieces(offs, sums, ordered)
        pulled, gains = norm_pull(x[...], gain[...], ordered[...])
        result = middle_grad[...] + pulled
        upstream[...] = result
        upstream_b[...] = result.astype(BF16)
        gain_grad[...] = gains


def run_qkv_back(
    offs, query_grad, own_grad, arrived_first, arrived_last, cosine, sine, x, gain, middle_grad, pieces
):
    tokens, features = x.shape
    whole = (query_grad, own_grad, arrived_first, arrived_last, cosine, sine, x, gain, middle_grad)
    outs = (
        struct((tokens, 3 * features), BF16),
        struct((tokens, features), F32),
        struct((tokens, features), BF16),
        struct((1, features), F32),
    )
    return call(
        qkv_back_kernel,
        outs,
        [pltpu.VMEM((tokens, features), F32), pltpu.VMEM((tokens, features), F32)],
        grid=(3,),
        in_specs=[pl.BlockSpec(memory_space=pltpu.SMEM)]
        + [whole_spec(v.shape) for v in whole]
        + piece_specs(pieces[0].shape[0], features),
        out_specs=tuple(whole_spec(out.shape) for out in outs),
    )(offs, *whole, *pieces)


def pick_kernel(which, *refs):
    pickers, lefts, (mine, theirs) = refs[:2], refs[2:-2], refs[-2:]
    half = pickers[0].shape[0] // 2
    for k, (picker, left) in enumerate(which):
        rows = lax.dot_general(
            pickers[picker][...], lefts[left][...], NT, preferred_element_type=F32
        ).astype(BF16)
        mine[k * half : (k + 1) * half, :] = rows[:half]
        theirs[k * half : (k + 1) * half, :] = rows[half:]


def run_pick(pickers, lefts, which):
    rows = len(which) * pickers[0].shape[0] // 2
    out = struct((rows, lefts[0].shape[0]), BF16)
    return call(functools.partial(pick_kernel, which), (out, out), smem=0)(*pickers, *lefts)


def exchange_kernel(plan, *refs):
    segments, stages = plan
    refs = list(refs)
    take = lambda count: [refs.pop(0) for _ in range(count)]
    adding, ending, far_ending, finishing = stages
    if segments:
        rights, rights_far = take(2), take(2)
        lefts = [take(2) for _ in segments]
    kept = take(2) if adding else None
    last = take(2) if ending else None
    come = take(2) if adding or ending else None
    near_pair = take(2) if far_ending else None
    far_pair = take(2) if finishing else None
    keep = take(2) if segments else None
    stay = take(2) if adding else None
    send = take(2) if segments or adding else None
    near_out = take(2) if ending else None
    far_out = take(2) if far_ending else None
    result = take(1)[0] if finishing else None

    def added(pair, rows, columns):
        return pair[0][rows, columns].astype(F32) + pair[1][rows, columns].astype(F32)

    def body(step):
        everything = slice(None)
        top = 0
        if segments:
            half, tile = keep[0].shape
            for (path, start, stop), (left, left_far) in zip(segments, lefts):
                low, high = max(start - step * tile, 0), min(stop - step * tile, tile)
                if low >= high:
                    continue
                columns = slice(low, high)
                total = jnp.dot(
                    jnp.concatenate([left[...], left_far[...]], axis=1),
                    jnp.concatenate(
                        [rights[path][:, columns], rights_far[path][:, columns]], axis=0
                    ),
                    preferred_element_type=F32,
                ).astype(BF16)
                keep[path][:, columns] = total[:half]
                send[path][:half, columns] = total[half:]
            top = half
        came = 0
        if adding:
            rows, tile = kept[0].shape
            half = rows // 2
            for path in range(2):
                total = kept[path][...].astype(F32) + come[path][:rows, :].astype(F32)
                stay[path][...] = total[:half].astype(BF16)
                send[1 - path][top : top + half, :] = total[half:].astype(BF16)
            came = rows
        if ending:
            rows, tile = last[0].shape
            half = rows // 2
            for path in range(2):
                at = (path * TILES + step) * tile
                total = last[path][...].astype(F32) + come[1 - path][
                    came : came + rows, :
                ].astype(F32)
                near_out[0][:, at : at + tile] = total[:half].astype(BF16)
                near_out[1][:, at : at + tile] = total[half:].astype(BF16)
        if step == 0 and far_ending:
            half = near_pair[0].shape[0] // 2
            far_out[0][...] = added(near_pair, slice(0, half), everything).astype(BF16)
            far_out[1][...] = added(near_pair, slice(half, 2 * half), everything).astype(BF16)
        if step == 0 and finishing:
            result[...] = added(far_pair, everything, everything).astype(result.dtype)

    for step in range(TILES):
        pl.when(pl.program_id(0) == step)(functools.partial(body, step))


class Exchange:
    def __init__(self, flow, rows, width, bits):
        self.flow = flow
        self.rows = rows
        self.width = width
        self.near, self.far = bits[:2]
        self.dtype = F32 if len(bits) == 2 else BF16
        self.kept = self.last = self.come = self.near_pair = self.far_pair = None

    def busy(self):
        return any((self.kept, self.last, self.near_pair, self.far_pair))

    def step(self, rights=None, segments=(), after=()):
        flow, rows, width = self.flow, self.rows, self.width
        tile = width // TILES
        args, specs, outs, out_specs = [], [], [], []

        def tiled(shape):
            return pl.BlockSpec((shape[0], tile), lambda j: (0, j))

        def give(pair, spec):
            if pair:
                args.extend(pair)
                specs.extend(spec(value.shape) for value in pair)

        def want(height, columns, spec, count=2, dtype=BF16):
            outs.extend([struct((height, columns), dtype)] * count)
            out_specs.extend([spec((height, columns))] * count)

        for right in rights or ():
            args += [right, right]
            block = (right.shape[0], tile)
            specs += [pl.BlockSpec(block, lambda j: (0, j))]
            specs += [pl.BlockSpec(block, lambda j: (0, TILES + j))]
        for _, _, _, left, place in segments:
            args += left
            specs += [pl.BlockSpec((rows, left[0].shape[1]), lambda j, at=place: (at, 0))] * 2
        give(self.kept, tiled)
        give(self.last, tiled)
        give(self.come if self.kept or self.last else None, tiled)
        give(self.near_pair, whole_spec)
        give(self.far_pair, whole_spec)
        height = 0
        if segments:
            want(rows // 2, width, tiled)
            height += rows // 2
        if self.kept:
            want(rows // 4, width, tiled)
            height += rows // 4
        if height:
            want(height, width, tiled)
        if self.last:
            want(rows // 8, 2 * width, whole_spec)
        if self.near_pair:
            want(rows // 16, 2 * width, whole_spec)
        if self.far_pair:
            want(rows // 16, 2 * width, whole_spec, 1, self.dtype)
        stages = tuple(map(bool, (self.kept, self.last, self.near_pair, self.far_pair)))
        plan = (
            tuple((path, start - path * width, stop - path * width) for path, start, stop, _, _ in segments),
            stages,
        )
        args[0] = flow.tie(args[0])
        results = list(
            call(
                functools.partial(exchange_kernel, plan),
                tuple(outs),
                grid=(TILES,),
                in_specs=specs,
                out_specs=tuple(out_specs),
            )(*args)
        )

        def got(wanted):
            return [results.pop(0), results.pop(0)] if wanted else None

        keep, stay, send = got(segments), got(self.kept), got(height)
        near, far = got(self.last), got(self.near_pair)
        result = results.pop(0) if self.far_pair else None
        self.kept, self.last = keep, stay
        self.come = send and [flow.swap(value, 1 + path) for path, value in enumerate(send)]
        if near:
            near[1] = lax.optimization_barrier((near[1],) + after)[0]
        self.near_pair = near and [near[0], flow.swap(near[1], self.near)]
        self.far_pair = far and [far[0], flow.swap(far[1], self.far)]
        return result


class Ending:
    def __init__(self, flow, value, bits, deliver):
        self.flow = flow
        self.bits = list(bits)
        self.deliver = deliver
        self.keep = value
        self.come = None

    def step(self):
        if self.come is not None:
            self.keep = self.keep.astype(F32) + self.flow.tie(self.come).astype(F32)
        if not self.bits:
            self.deliver(self.keep)
            return False
        half = self.keep.shape[0] // 2
        send = self.keep[half:].astype(BF16)
        self.keep = self.keep[:half].astype(BF16)
        self.come = self.flow.swap(send, self.bits.pop(0))
        return True


def rope_tables(position):
    inverse = jnp.power(THETA, -jnp.arange(0, HEAD_DIM, 2, dtype=F32) / HEAD_DIM)
    angles = position[:, None] * inverse[None, :]
    cosine, sine = jnp.cos(angles), jnp.sin(angles)
    return (
        jnp.concatenate([cosine, cosine, cosine, cosine], axis=-1),
        jnp.concatenate([-sine, sine, -sine, sine], axis=-1),
    )


def layout(positions, lengths, total):
    count = lengths.shape[0]
    blocks = (lengths + BLOCK - 1) // BLOCK
    first = (jnp.cumsum(blocks) - blocks) * BLOCK
    owner = jnp.sum((positions[:, None] >= first[None, :]).astype(jnp.int32), axis=1) - 1
    table = owner[:, None] == jnp.arange(count, dtype=jnp.int32)[None, :]
    start = jnp.sum(jnp.where(table, first[None, :], 0), axis=1)
    span = jnp.sum(jnp.where(table, lengths[None, :], 0), axis=1)
    local = positions - start
    inside = (positions >= 0) & (positions < total)
    valid = inside & (local < span)
    segment = jnp.where(inside, jnp.where(valid, owner, owner + count), -1)
    return (segment, local, valid)


def body(
    tokens,
    cotangent,
    lengths,
    block_perm,
    attn_gain,
    qkv_weight,
    proj_weight,
    mlp_gain,
    wide_weight,
    narrow_weight,
):
    flow = Phases()
    seq_index = lax.axis_index("seq")
    seq_count = lax.axis_size("seq")
    levels = seq_count.bit_length() - 1
    tok_dev = tokens.shape[1]
    features = tokens.shape[2]
    block_rows = tok_dev // BLK_DEV
    order_map = block_perm[0]
    target = order_map[0::BLK_DEV] // BLK_DEV
    source = jnp.arange(seq_count, dtype=jnp.int32)

    def holder(bit_level):
        low_mask = (1 << bit_level) - 1
        place = jnp.bitwise_or(
            jnp.bitwise_and(target, low_mask), jnp.bitwise_and(source, ~low_mask)
        )
        return jnp.sum(jnp.where(place == seq_index, source, 0))

    home_index = holder(levels)
    slot_of = lax.dynamic_slice_in_dim(order_map, home_index * BLK_DEV, BLK_DEV) % BLK_DEV
    crossed = slot_of[0] == 1

    def crossing(rows):
        turned = jnp.concatenate([rows[block_rows:], rows[:block_rows]], axis=0)
        return jnp.where(crossed, turned, rows)

    def crossed_over(bit_level, given):
        payload = holder(bit_level + 1 if given else bit_level)
        if not given:
            payload = jnp.sum(jnp.where(source == payload, target, 0))
        flips = jnp.right_shift(jnp.bitwise_xor(seq_index, payload), bit_level)
        return jnp.bitwise_and(flips, 1) == 1

    class Route:
        def __init__(self, rows, given, last=levels):
            self.rows = rows
            self.given = given
            self.levels = list(range(last))
            if given:
                self.levels.reverse()
            self.arrived = None

        def step(self):
            if self.arrived is not None:
                self.rows = jnp.where(
                    crossed_over(self.level, self.given), flow.tie(self.arrived), self.rows
                )
                self.arrived = None
            if self.levels:
                self.level = self.levels.pop(0)
                self.arrived = flow.swap(self.rows, 2 + self.level)
                return True
            return False

        def finish(self):
            while self.step():
                flow.next()
            return self.rows

    total = seq_count * tok_dev
    own_place = seq_index * tok_dev + jnp.arange(tok_dev, dtype=jnp.int32)
    key_place = seq_index * tok_dev - HALO + jnp.arange(tok_dev + 2 * HALO, dtype=jnp.int32)
    seg_query, local_query, valid_query = layout(own_place, lengths[0], total)
    seg_key, _, _ = layout(key_place, lengths[0], total)
    cosine, sine = rope_tables(local_query.astype(F32))
    seg_q_col, seg_q_row = seg_query[:, None], seg_query[None, :]
    seg_k_col, seg_k_row = seg_key[:, None], seg_key[None, :]
    offs = piece_order()
    bits_x, bits_y = stage_bits(True), stage_bits(False)
    picker_x, picker_y = row_picker(features, bits_x), row_picker(features, bits_y)

    gains = jnp.concatenate([attn_gain, mlp_gain], axis=0)
    gains = lax.all_gather(gains, "fsdp", axis=1, tiled=True).astype(F32)
    gains_a = [gains[layer : layer + 1] for layer in range(LAYERS)]
    gains_m = [gains[LAYERS + layer : LAYERS + layer + 1] for layer in range(LAYERS)]

    side = (seq_index % 2).astype(jnp.int32).reshape(1)
    arrays = (proj_weight, wide_weight, narrow_weight)
    items = []
    for layer in range(LAYERS):
        packs = run_pack(side, (qkv_weight,), layer) + run_pack(side, arrays, layer)
        items += [Weights(flow, *pack) for pack in packs]
    per_layer = len(items) // LAYERS
    tok_route, cot_route = Route(tokens[0], False), Route(cotangent[0], False, levels - 1)

    first_use = 3
    owns = {0: (0,), 1: (1, 3), 2: (2,), 4: (4,), 5: (5,), 6: (6,), 8: (7,)}
    phase = 0

    def transfers():
        if phase < len(items):
            items[phase].over_x()
        if 0 <= phase - 1 < len(items):
            items[phase - 1].over_y()
        if 0 <= phase - 2 < len(items):
            items[phase - 2].over_core()
        for place in owns.get(phase, ()):
            items[place].own()

    flow.keep(gains)
    while phase < first_use or tok_route.levels:
        transfers()
        tok_route.step()
        if phase == 0:
            cot_route.step()
            flow.keep(*(item.shard for item in items[1:]))
        phase += 1
        flow.next()
    tok_route.step()
    residual = crossing(tok_route.rows).astype(F32)
    cot_halves = []
    kept = []
    for layer in range(LAYERS):
        base = layer * per_layer
        transfers()
        qkv, normed, edge_first, edge_last = run_qkv(
            offs, flow.tie(residual), gains_a[layer], cosine, sine, items[base].pieces
        )
        flow.keep(normed)
        before = flow.shift(edge_last, True)
        after = flow.shift(edge_first, False)
        phase += 1
        flow.next()
        transfers()
        if layer == 0:
            cot_route.step()
        if layer and kept[-1][-1] is None:
            kept[-1][-1] = (mine, flow.swap(theirs, 0))
        start = residual
        mixed, middle, second = run_attend(
            offs, flow.tie(qkv), before, after, seg_q_col, seg_k_row, residual, gains_m[layer],
            items[base + 1].pieces,
        )
        residual = middle
        hidden = []
        for chunk in range(CHUNKS):
            if chunk:
                phase += 1
                flow.next()
                transfers()
                if layer == 0:
                    if not cot_halves:
                        cot_rows = cot_route.finish()
                        for half in (cot_rows[:block_rows], cot_rows[block_rows:]):
                            cot_halves.append(Route(half, False))
                            cot_halves[-1].levels = [levels - 1]
                    cot_halves[chunk - 1].step()
            residual, gated, slope, gate = run_mlp(
                offs, second, flow.tie(residual), items[base + 1 + chunk].pieces, chunk
            )
            flow.keep(residual, gated)
            hidden.append((gated, slope, gate))
            if chunk == 1:
                lefts = (normed, mixed, second)
                which = ((0, 0), (1, 0), (1, 1), (0, 2), (1, 2))
                mine, theirs = run_pick((picker_x, picker_y), lefts, which)
                flow.keep(theirs)
        picks = None
        if layer == LAYERS - 1:
            flow.next()
            picks = (mine, flow.swap(theirs, 0))
        kept.append([start, qkv, before, after, middle, hidden, picks])
        phase += 1
        flow.next()

    packed_cot = crossing(jnp.concatenate([half.finish() for half in cot_halves], axis=0))
    upstream_b = packed_cot * valid_query[:, None].astype(BF16)
    upstream = upstream_b.astype(F32)

    def both_halves(rows):
        rows = crossing(rows)
        return [Route(rows[:block_rows], True), Route(rows[block_rows:], True)]

    out_routes = both_halves(residual.astype(BF16))

    late = bits_x[2:]
    exchange = Exchange(flow, features // 2, 3 * features // 2, late)
    endings = []
    sums = {}
    count = 0
    width = 3 * features // 2

    def settle(done):
        nonlocal count
        if done is None:
            return
        deliver = functools.partial(sums.__setitem__, count)
        count += 1
        if len(late) > 2:
            endings.append(Ending(flow, done, late[2:], deliver))
        else:
            deliver(done)

    def step_endings():
        for item in list(endings):
            if not item.step():
                endings.remove(item)

    def group(right, parts):
        segments = []
        at = 0
        for columns, lefts in parts:
            for path in range(2):
                low = max(at, path * width)
                high = min(at + columns, (path + 1) * width)
                if low < high:
                    segments.append((path, low, high, lefts[path][:2], lefts[path][2]))
            at += columns
        return list(right), tuple(segments)

    terms = [None] * LAYERS
    made, ready = None, None

    def backward_phase():
        nonlocal made, ready
        flow.next()
        moving = bool(made or ready or exchange.busy())
        now, ready, after = ready, None, ()
        if made:
            right, parts = made
            after = (flow.swap(right, 0),)
            ready = ((right,) + after, parts)
        made = None
        if now or exchange.busy():
            settle(exchange.step(*(group(*now) if now else (None, ())), after))
        step_endings()
        return moving

    for layer in reversed(range(LAYERS)):
        start, qkv, before, after, middle, hidden, picks = kept[layer]
        base = layer * per_layer
        normed_x, normed_y, mixed_y, second_x, second_y = (picks + (row,) for row in range(5))
        carried = None
        upstream_left = None
        for chunk in reversed(range(CHUNKS)):
            if layer < LAYERS - 1 or chunk < CHUNKS - 1:
                backward_phase()
            pieces = items[base + 1 + chunk].pieces
            if upstream_left is None:
                mine, theirs = run_pick(
                    (picker_x, picker_y), (flow.tie(upstream_b),), ((0, 0), (1, 0))
                )
                flow.keep(theirs)
                upstream_left = []
            elif not upstream_left:
                far = flow.swap(theirs, 0)
                upstream_left += [(mine, far, path) for path in range(2)]
            if layer == LAYERS - 1 and chunk == CHUNKS - 1:
                out_routes[0].step()
            elif layer == LAYERS - 2 and chunk == CHUNKS - 1:
                for route in out_routes:
                    route.step()
            args = (offs, flow.tie(upstream_b), hidden[chunk], carried)
            columns = WIDTHS[chunk]
            parts = [
                (columns, upstream_left),
                (2 * columns, (second_x, second_y)),
            ]
            if chunk:
                carried, right = run_mlp_back(*args, pieces, chunk)
                flow.keep(carried)
            else:
                middle_grad, middle_grad_b, mlp_term, right = run_mlp_back_last(
                    *args, upstream, middle, gains_m[layer], pieces, chunk
                )
                parts.append((2 * width - 3 * columns, (None, mixed_y)))
                query_grad, own_grad, rim_before, rim_after = run_attend_back(
                    offs, middle_grad_b, qkv, before, after, seg_q_row, seg_k_col, cosine, sine, pieces
                )
                flow.keep(query_grad, own_grad)
                arrived_first = flow.shift(rim_after, True)
                arrived_last = flow.shift(rim_before, False)
            flow.keep(right)
            made = (right, parts)
        backward_phase()
        right, upstream, upstream_b, attn_term = run_qkv_back(
            offs, flow.tie(query_grad), own_grad, arrived_first, arrived_last, cosine, sine, start,
            gains_a[layer], middle_grad, items[base].pieces,
        )
        if layer:
            out_routes[1].step()
        flow.keep(upstream_b, right)
        made = (right, [(2 * width, (normed_x, normed_y))])
        terms[layer] = (attn_term, mlp_term)
    backward_phase()
    grad_routes = both_halves(flow.tie(upstream_b))
    grad_routes[0].step()
    vectors = [terms[layer][0] for layer in range(LAYERS)]
    vectors += [terms[layer][1] for layer in range(LAYERS)]
    gain_sums = lax.dot_general(
        flow.tie(jnp.concatenate(vectors, axis=0)), picker_x.astype(F32), NT, precision=lax.Precision.HIGHEST
    )
    gain_bits = [0] + list(bits_x)
    while backward_phase() or endings or gain_bits:
        for route in grad_routes:
            route.step()
        if not grad_routes[0].levels:
            for route in out_routes:
                route.step()
        for bit in gain_bits[: 1 if len(gain_bits) > 2 else 2]:
            half = gain_sums.shape[1] // 2
            gain_sums = gain_sums[:, :half] + flow.swap(gain_sums[:, half:], bit)
        gain_bits = gain_bits[1 if len(gain_bits) > 2 else 2 :]
    block_out, token_grad = (
        jnp.concatenate([route.finish() for route in routes], axis=0)
        for routes in (out_routes, grad_routes)
    )

    def pieces_of(layer):
        at = per_layer * (LAYERS - 1 - layer)
        parts = {chunk: sums[at + CHUNKS - 1 - chunk] for chunk in range(CHUNKS)}
        return parts, sums[at + CHUNKS]

    def hidden_sum(parts, role):
        columns = [
            parts[chunk][:, role * WIDTHS[chunk] : (role + 1) * WIDTHS[chunk]]
            for chunk in range(CHUNKS)
        ]
        return jnp.concatenate(columns, axis=1)[:, :FF]

    wide, narrow, proj, qkv_sum = [], [], [], []
    for layer in range(LAYERS):
        parts, attend = pieces_of(layer)
        narrow.append(hidden_sum(parts, 0))
        wide.append(jnp.concatenate([hidden_sum(parts, 1), hidden_sum(parts, 2)], axis=1))
        proj.append(parts[0][:, 3 * WIDTHS[0] : 3 * WIDTHS[0] + features])
        qkv_sum.append(attend)
    return (
        block_out[None],
        token_grad[None],
        gain_sums[:LAYERS],
        jnp.stack(qkv_sum),
        jnp.stack(proj),
        gain_sums[LAYERS:],
        jnp.stack(wide),
        jnp.stack(narrow),
    )


def solution(mesh):
    in_specs = (
        P("fsdp", "seq", None),
        P("fsdp", "seq", None),
        P("fsdp", None),
        P("fsdp", None),
        P(None, "fsdp"),
        P(None, "fsdp", None),
        P(None, "fsdp", None),
        P(None, "fsdp"),
        P(None, "fsdp", None),
        P(None, "fsdp", None),
    )
    out_specs = (
        P("fsdp", "seq", None),
        P("fsdp", "seq", None),
        P(None, ("seq", "fsdp")),
        P(None, ("seq", "fsdp"), None),
        P(None, ("seq", "fsdp"), None),
        P(None, ("seq", "fsdp")),
        P(None, ("seq", "fsdp"), None),
        P(None, ("seq", "fsdp"), None),
    )
    return jax.shard_map(body, mesh=mesh, in_specs=in_specs, out_specs=out_specs, check_vma=False)
```

```python
import functools
import math

import jax
import jax.numpy as jnp
from jax import lax
from jax.experimental import pallas as pl
from jax.experimental.pallas import tpu as pltpu
from jax.sharding import PartitionSpec as P

HEADS = 16
HEAD_DIM = 64
FF = 2624
WINDOW = 128
BLOCK = 128
BLK_DEV = 2
LAYERS = 2

NEG = -1e30
EPS = 1e-05
THETA = 10000.0

AXES = ("seq", "fsdp")
LANES = 128
HALO = WINDOW // 2
SPLIT = (5, 8, 8)
FF_PAD = sum(SPLIT) * LANES
WIDTHS = tuple(blocks * LANES for blocks in SPLIT)
STARTS = tuple(sum(WIDTHS[:k]) for k in range(len(WIDTHS)))
CHUNKS = len(SPLIT)
TILES = 3
F32 = jnp.float32
BF16 = jnp.bfloat16
VMEM_LIMIT = 20 * 1024 * 1024
NT = (((1,), (1,)), ((), ()))
TN = (((0,), (0,)), ((), ()))


class Phases:
    def __init__(self):
        self.gate = ()
        self.made = []

    def next(self):
        self.gate = tuple(self.made)
        self.made = []

    def tie(self, value):
        return lax.optimization_barrier((value,) + self.gate)[0] if self.gate else value

    def keep(self, *values):
        self.made += values

    def route(self, value, axes, pairs):
        result = lax.ppermute(self.tie(value), axes, pairs)
        self.made.append(result)
        return result

    def swap(self, value, bit):
        count = lax.axis_size("seq") * lax.axis_size("fsdp")
        return self.route(value, AXES, [(i, i ^ (1 << bit)) for i in range(count)])

    def shift(self, value, up):
        pairs = [(i, i + 1) for i in range(lax.axis_size("seq") - 1)]
        if not up:
            pairs = [(b, a) for a, b in pairs]
        return self.route(value, "seq", pairs)


def flat_index():
    return lax.axis_index("seq") * lax.axis_size("fsdp") + lax.axis_index("fsdp")


class Weights:
    def __init__(self, flow, shard, sent):
        self.flow = flow
        self.shard = shard
        self.sent = sent

    def own(self):
        self.own_core = self.flow.swap(self.shard, 0)

    def over_x(self):
        self.far_x = self.flow.swap(self.sent, 1)

    def over_y(self):
        self.far_y = self.flow.swap(self.far_x, 2)

    def over_core(self):
        far = jnp.concatenate([self.far_x, self.flow.tie(self.far_y)], axis=0)
        self.pieces = (self.shard, far, self.own_core, self.flow.swap(far, 0))


def piece_order():
    quarter = lax.axis_index("fsdp")
    side = lax.axis_index("seq") % 2
    one = 1 - side
    order = []
    for core in (quarter, quarter ^ 1):
        order += [core * 2, core * 2 + 1, (core ^ 2) * 2 + side, (core ^ 2) * 2 + one]
    return jnp.stack(order).astype(jnp.int32)


def stage_bits(first_x):
    levels = lax.axis_size("seq").bit_length() - 1
    rest = [2 + level for level in range(1, levels)]
    return ([1, 2] if first_x else [2, 1]) + rest


def row_order(features, bits):
    order = [0] + bits
    per_device = features >> len(order)
    rows = jnp.arange(features, dtype=jnp.int32)
    place = rows // per_device
    owner = flat_index()
    for step, bit in enumerate(order):
        taken = (place >> (len(order) - 1 - step)) & 1
        owner = owner ^ (taken << bit)
    return owner * per_device + rows % per_device


def row_picker(features, bits):
    order = row_order(features, bits)
    grid = jnp.arange(features, dtype=jnp.int32)
    return (order[:, None] == grid[None, :]).astype(BF16)


def call(kernel, outs, scratch=(), smem=1, grid=None, in_specs=None, out_specs=None, limit=VMEM_LIMIT):
    params = dict(
        compiler_params=pltpu.CompilerParams(vmem_limit_bytes=limit),
        out_shape=outs,
        scratch_shapes=list(scratch),
        cost_estimate=pl.CostEstimate(
            flops=0, bytes_accessed=0, transcendentals=0
        ),
    )
    if grid is not None:
        params["grid"] = grid

    def run(*args):
        specs = in_specs
        if specs is None:
            specs = [pl.BlockSpec(memory_space=pltpu.SMEM)] * smem
            specs += [pl.BlockSpec(memory_space=pltpu.VMEM)] * (len(args) - smem)
        results = out_specs
        if results is None:
            results = jax.tree.map(lambda _: pl.BlockSpec(memory_space=pltpu.VMEM), outs)
        return pl.pallas_call(kernel, in_specs=specs, out_specs=results, **params)(*args)

    return run


def struct(shape, dtype):
    return jax.ShapeDtypeStruct(shape, dtype)


def to_pieces(offs, source, target):
    for k in range(source.shape[1] // LANES):
        start = pl.multiple_of(offs[k] * LANES, LANES)
        target[:, k * LANES : (k + 1) * LANES] = source[:, pl.ds(start, LANES)]


def from_pieces(offs, source, target):
    for k in range(source.shape[1] // LANES):
        start = pl.multiple_of(offs[k] * LANES, LANES)
        target[:, pl.ds(start, LANES)] = source[:, k * LANES : (k + 1) * LANES]


def joined(pieces, columns=slice(None)):
    return jnp.concatenate([piece[:, columns] for piece in pieces], axis=0)


def statistics(values):
    average = jnp.mean(values, axis=-1, keepdims=True)
    centred = values - average
    spread = jnp.mean(centred * centred, axis=-1, keepdims=True)
    rho = lax.rsqrt(spread + EPS)
    return centred, rho


def norm_pull(values, gain, grad):
    centred, rho = statistics(values)
    unit = centred * rho
    scaled = grad * gain
    mean_a = jnp.mean(scaled, axis=-1, keepdims=True)
    mean_b = jnp.mean(scaled * unit, axis=-1, keepdims=True)
    return rho * (scaled - mean_a - unit * mean_b), jnp.sum(grad * unit, axis=0, keepdims=True)


def turn_chunk(values, cosine, sine, sign):
    lane = lax.broadcasted_iota(jnp.int32, values.shape, 1)
    ahead = pltpu.roll(values, LANES - HEAD_DIM // 2, 1)
    behind = pltpu.roll(values, HEAD_DIM // 2, 1)
    turned = jnp.where(lane % HEAD_DIM < HEAD_DIM // 2, ahead, behind)
    if sign > 0:
        return values * cosine + turned * sine
    return values * cosine - turned * sine


def pack_one_kernel(side, first, own, sent):
    half = first.shape[1] // 2
    own[...] = first[0]
    sent[...] = first[0, pl.ds(pl.multiple_of(side[0] * half, half), half), :]


def pack_kernel(side, second, wide, narrow, *outs):
    half = wide.shape[1] // 2
    features = second.shape[2]
    outs[0][:, :features] = second[0]
    for chunk in range(CHUNKS):
        own = outs[2 * chunk]
        at = features if chunk == 0 else 0
        width = WIDTHS[chunk]
        start, stop = STARTS[chunk], min(STARTS[chunk] + width, FF)
        for array, base in ((narrow, 0), (wide, 0), (wide, FF)):
            if stop - start < width:
                own[:, at + width - LANES : at + width] = jnp.zeros((2 * half, LANES), BF16)
            own[:, at : at + stop - start] = array[0, :, base + start : base + stop]
            at += width
    for k in range(0, len(outs), 2):
        outs[k + 1][...] = outs[k][pl.ds(pl.multiple_of(side[0] * half, half), half), :]


def run_pack(side, arrays, layer):
    rows = arrays[0].shape[1]
    one = len(arrays) == 1
    features = arrays[0].shape[2]
    columns = [features + 3 * WIDTHS[0]] + [3 * width for width in WIDTHS[1:]]
    if one:
        columns = [features]
    outs = tuple(struct((height, width), BF16) for width in columns for height in (rows, rows // 2))
    flat = call(
        pack_one_kernel if one else pack_kernel,
        outs,
        grid=(1,),
        in_specs=[pl.BlockSpec(memory_space=pltpu.SMEM)]
        + [pl.BlockSpec((1,) + v.shape[1:], lambda j: (layer, 0, 0)) for v in arrays],
        out_specs=tuple(whole_spec(out.shape) for out in outs),
    )(side, *arrays)
    return [flat[k : k + 2] for k in range(0, len(flat), 2)]


def qkv_kernel(offs, x, gain, cosine, sine, p0, p1, p2, p3, out, normed, first, last, placed):
    step = pl.program_id(0)
    tokens = x.shape[0]

    @pl.when(step == 0)
    def _():
        centred, rho = statistics(x[...])
        normed[...] = (centred * rho * gain[...]).astype(BF16)
        to_pieces(offs, normed, placed)

    product = jnp.dot(
        placed[...], joined((p0, p1, p2, p3)), preferred_element_type=F32
    )

    @pl.when(step < 2)
    def _():
        for k in range(product.shape[1] // LANES):
            part = slice(k * LANES, (k + 1) * LANES)
            out[:, part] = turn_chunk(product[:, part], cosine[...], sine[...], 1).astype(BF16)

    @pl.when(step == 2)
    def _():
        out[...] = product.astype(BF16)

    first[...] = out[:HALO, :]
    last[...] = out[tokens - HALO :, :]


def piece_specs(rows, columns):
    return [pl.BlockSpec((rows, columns), lambda j: (0, j))] * 4


def proj_specs(rows, columns):
    return [pl.BlockSpec((rows, columns), lambda j: (0, 0))] * 4


def whole_spec(shape):
    return pl.BlockSpec(shape, lambda j: tuple(0 for _ in shape))


def run_qkv(offs, x, gain, cosine, sine, pieces):
    tokens, features = x.shape
    return call(
        qkv_kernel,
        (
            struct((tokens, 3 * features), BF16),
            struct((tokens, features), BF16),
            struct((HALO, 2 * features), BF16),
            struct((HALO, 2 * features), BF16),
        ),
        [pltpu.VMEM((tokens, features), BF16)],
        grid=(3,),
        in_specs=[pl.BlockSpec(memory_space=pltpu.SMEM)]
        + [whole_spec(v.shape) for v in (x, gain, cosine, sine)]
        + piece_specs(pieces[0].shape[0], features),
        out_specs=(
            pl.BlockSpec((tokens, features), lambda j: (0, j)),
            whole_spec((tokens, features)),
            pl.BlockSpec((HALO, features), lambda j: (0, jnp.maximum(j - 1, 0))),
            pl.BlockSpec((HALO, features), lambda j: (0, jnp.maximum(j - 1, 0))),
        ),
    )(offs, x, gain, cosine, sine, *pieces)


def stacked(rows, low):
    zero = jnp.zeros_like(rows)
    return jnp.concatenate([jnp.where(low, rows, zero), jnp.where(low, zero, rows)], axis=0)


def extend(qkv, before, after, extended):
    tokens, features = qkv.shape[0], qkv.shape[1] // 3
    extended[:HALO, :] = before[...]
    extended[HALO : HALO + tokens, :] = qkv[:, features:]
    extended[HALO + tokens :, :] = after[...]


def attend_kernel(
    offs, qkv, before, after, seg_q, seg_k, x, gain,
    p0, p1, p2, p3, mixed, middle, second, extended, placed,
):
    tokens, features = x.shape
    extend(qkv, before, after, extended)
    scale = jnp.asarray(1.0 / math.sqrt(HEAD_DIM), BF16)
    span = BLOCK + 2 * HALO
    row = lax.broadcasted_iota(jnp.int32, (BLOCK, span), 0)
    col = lax.broadcasted_iota(jnp.int32, (BLOCK, span), 1)
    near = (col >= row) & (col - row <= 2 * HALO)
    low = lax.broadcasted_iota(jnp.int32, (BLOCK, LANES), 1) < HEAD_DIM
    bias = []
    for block in range(tokens // BLOCK):
        base = block * BLOCK
        same = seg_q[base : base + BLOCK, :] == seg_k[:, base : base + span]
        one = jnp.where(near & same, 0.0, NEG)
        bias.append(jnp.concatenate([one, one], axis=0))

    def pair(index, carry):
        lanes = pl.ds(pl.multiple_of(index * LANES, LANES), LANES)
        value_lanes = pl.ds(pl.multiple_of(features + index * LANES, LANES), LANES)
        for block in range(tokens // BLOCK):
            base = block * BLOCK
            queries = qkv[base : base + BLOCK, lanes]
            keys = extended[base : base + span, lanes]
            values = extended[base : base + span, value_lanes]
            scores = (
                lax.dot_general(stacked(queries * scale, low), keys, NT, preferred_element_type=F32)
                + bias[block]
            )
            expo = jnp.exp(scores - jnp.max(scores, axis=-1, keepdims=True))
            probs = expo * (1.0 / jnp.sum(expo, axis=-1, keepdims=True))
            both = jnp.dot(probs.astype(BF16), values, preferred_element_type=F32)
            mixed[base : base + BLOCK, lanes] = jnp.where(low, both[:BLOCK], both[BLOCK:]).astype(BF16)
        return carry

    lax.fori_loop(0, features // LANES, pair, 0)
    to_pieces(offs, mixed, placed)
    total = x[...] + jnp.dot(
        placed[...], joined((p0, p1, p2, p3)), preferred_element_type=F32
    )
    middle[...] = total
    centred, rho = statistics(total)
    second[...] = (centred * rho * gain[...]).astype(BF16)


def run_attend(offs, qkv, before, after, seg_q, seg_k, x, gain, pieces):
    tokens, features = x.shape
    return call(
        attend_kernel,
        (
            struct((tokens, features), BF16),
            struct((tokens, features), F32),
            struct((tokens, features), BF16),
        ),
        [
            pltpu.VMEM((tokens + 2 * HALO, 2 * features), BF16),
            pltpu.VMEM((tokens, features), BF16),
        ],
        grid=(1,),
        in_specs=[pl.BlockSpec(memory_space=pltpu.SMEM)]
        + [whole_spec(v.shape) for v in (qkv, before, after, seg_q, seg_k, x, gain)]
        + proj_specs(pieces[0].shape[0], features),
        out_specs=(whole_spec((tokens, features)),) * 3,
    )(offs, qkv, before, after, seg_q, seg_k, x, gain, *pieces)


def chunk_parts(pieces, base, width):
    return [
        joined(pieces, slice(base + k * width, base + (k + 1) * width)) for k in range(3)
    ]


def mlp_kernel(
    base, width, offs, second, carried, p0, p1, p2, p3, total, gated, slope, gate, placed, part
):
    output, first, other = chunk_parts((p0, p1, p2, p3), base, width)
    to_pieces(offs, second, placed)
    source = placed[...]
    hidden = jnp.dot(source, first, preferred_element_type=F32)
    factor = jnp.dot(source, other, preferred_element_type=F32)
    normal = 0.5 * (1.0 + lax.erf(hidden * math.sqrt(0.5)))
    density = jnp.exp(-0.5 * hidden * hidden) * (1.0 / math.sqrt(2.0 * math.pi))
    active = hidden * normal
    product = (active * factor).astype(BF16)
    gated[...] = product
    slope[...] = ((normal + hidden * density) * factor).astype(BF16)
    gate[...] = active.astype(BF16)
    part[...] = lax.dot_general(product, output, NT, preferred_element_type=F32)
    for k in range(part.shape[1] // LANES):
        lanes = pl.ds(pl.multiple_of(offs[k] * LANES, LANES), LANES)
        total[:, lanes] = carried[:, lanes] + part[:, k * LANES : (k + 1) * LANES]


def run_mlp(offs, second, carried, pieces, chunk):
    tokens, features = second.shape
    width = WIDTHS[chunk]
    base = pieces[0].shape[1] - 3 * width
    hidden = struct((tokens, width), BF16)
    return call(
        functools.partial(mlp_kernel, base, width),
        (struct((tokens, features), F32), hidden, hidden, hidden),
        [pltpu.VMEM((tokens, features), BF16), pltpu.VMEM((tokens, features), F32)],
    )(offs, second, carried, *pieces)


def mlp_pull(base, width, offs, upstream, gated, slope, gate, pieces, right, placed):
    output, first, other = chunk_parts(pieces, base, width)
    to_pieces(offs, upstream, placed)
    gated_grad = jnp.dot(placed[...], output, preferred_element_type=F32)
    input_grad = (slope[...].astype(F32) * gated_grad).astype(BF16)
    gate_grad = (gate[...].astype(F32) * gated_grad).astype(BF16)
    store(right, 0, gated[...])
    store(right, width, input_grad)
    store(right, 2 * width, gate_grad)
    return lax.dot_general(input_grad, first, NT, preferred_element_type=F32) + lax.dot_general(
        gate_grad, other, NT, preferred_element_type=F32
    )


def store(target, at, value):
    target[:, at : at + value.shape[1]] = value


def mlp_back_kernel(
    base, width, first, offs, upstream, gated, slope, gate, carried, p0, p1, p2, p3,
    total, right, placed,
):
    part = mlp_pull(
        base, width, offs, upstream, gated, slope, gate, (p0, p1, p2, p3), right, placed
    )
    total[...] = part if first else carried[...] + part


def mlp_back_last_kernel(
    base, width, offs, upstream, gated, slope, gate, carried, residual_grad, middle, gain,
    p0, p1, p2, p3, middle_grad, middle_grad_b, gain_grad, right, placed, sums, ordered,
):
    part = mlp_pull(
        base, width, offs, upstream, gated, slope, gate, (p0, p1, p2, p3), right, placed
    )
    sums[...] = carried[...] + part
    from_pieces(offs, sums, ordered)
    pulled, gains = norm_pull(middle[...], gain[...], ordered[...])
    result = residual_grad[...] + pulled
    middle_grad[...] = result
    middle_grad_b[...] = result.astype(BF16)
    gain_grad[...] = gains
    at = 3 * width
    store(right, at, result.astype(BF16))
    at += result.shape[1]
    rest = right.shape[1] - at
    if rest:
        store(right, at, jnp.zeros((result.shape[0], rest), BF16))


def run_mlp_back(offs, upstream, hidden, carried, pieces, chunk):
    tokens, features = upstream.shape
    width = WIDTHS[chunk]
    base = pieces[0].shape[1] - 3 * width
    right = struct((tokens, 3 * features), BF16)
    first = carried is None
    if first:
        carried = jnp.zeros((8, LANES), F32)
    return call(
        functools.partial(mlp_back_kernel, base, width, first),
        (struct((tokens, features), F32), right),
        [pltpu.VMEM((tokens, features), BF16)],
    )(offs, upstream, *hidden, carried, *pieces)


def run_mlp_back_last(offs, upstream, hidden, carried, residual_grad, middle, gain, pieces, chunk):
    tokens, features = upstream.shape
    width = WIDTHS[chunk]
    base = pieces[0].shape[1] - 3 * width
    right = struct((tokens, 3 * features), BF16)
    return call(
        functools.partial(mlp_back_last_kernel, base, width),
        (
            struct((tokens, features), F32),
            struct((tokens, features), BF16),
            struct((1, features), F32),
            right,
        ),
        [
            pltpu.VMEM((tokens, features), BF16),
            pltpu.VMEM((tokens, features), F32),
            pltpu.VMEM((tokens, features), F32),
        ],
    )(offs, upstream, *hidden, carried, residual_grad, middle, gain, *pieces)


def attend_back_kernel(
    offs, middle_grad, qkv, before, after, seg_q, seg_k, cosine, sine, p0, p1, p2, p3,
    query_grad, own_grad, rim_before, rim_after, extended, mixed_grad, extended_grad,
):
    tokens, features = middle_grad.shape
    extend(qkv, before, after, extended)
    placed = lax.dot_general(
        middle_grad[...], joined((p0, p1, p2, p3)), NT, preferred_element_type=F32
    ).astype(BF16)
    for k in range(features // LANES):
        lanes = pl.ds(pl.multiple_of(offs[k] * LANES, LANES), LANES)
        mixed_grad[:, lanes] = placed[:, k * LANES : (k + 1) * LANES]
    scale = jnp.asarray(1.0 / math.sqrt(HEAD_DIM), BF16)
    span = BLOCK + 2 * HALO
    row = lax.broadcasted_iota(jnp.int32, (span, BLOCK), 1)
    col = lax.broadcasted_iota(jnp.int32, (span, BLOCK), 0)
    near = (col >= row) & (col - row <= 2 * HALO)
    low = lax.broadcasted_iota(jnp.int32, (BLOCK, LANES), 1) < HEAD_DIM
    bias = []
    for block in range(tokens // BLOCK):
        base = block * BLOCK
        same = seg_q[:, base : base + BLOCK] == seg_k[base : base + span, :]
        one = jnp.where(near & same, 0.0, NEG)
        bias.append(jnp.concatenate([one, one], axis=1))

    def pair(index, carry):
        lanes = pl.ds(pl.multiple_of(index * LANES, LANES), LANES)
        value_lanes = pl.ds(pl.multiple_of(features + index * LANES, LANES), LANES)
        key_sums = []
        value_sums = []
        for block in range(tokens // BLOCK):
            base = block * BLOCK
            here = slice(base, base + BLOCK)
            queries = qkv[here, lanes]
            grads = mixed_grad[here, lanes]
            keys = extended[base : base + span, lanes]
            values = extended[base : base + span, value_lanes]
            chosen = stacked(queries * scale, low)
            chosen_grad = stacked(grads, low)
            scores = (
                lax.dot_general(keys, chosen, NT, preferred_element_type=F32) + bias[block]
            )
            expo = jnp.exp(scores - jnp.max(scores, axis=0, keepdims=True))
            probs = expo * (1.0 / jnp.sum(expo, axis=0, keepdims=True))
            prob_grad = lax.dot_general(values, chosen_grad, NT, preferred_element_type=F32)
            delta = jnp.sum(prob_grad * probs, axis=0, keepdims=True)
            score_grad = (probs * (prob_grad - delta)).astype(BF16)
            both = lax.dot_general(score_grad, keys, TN, preferred_element_type=F32)
            key_sum = jnp.dot(score_grad, chosen, preferred_element_type=F32)
            value_sum = jnp.dot(probs.astype(BF16), chosen_grad, preferred_element_type=F32)
            joint = jnp.where(low, both[:BLOCK], both[BLOCK:]) * (1.0 / math.sqrt(HEAD_DIM))
            query_grad[here, lanes] = turn_chunk(
                joint, cosine[here, :], sine[here, :], -1
            ).astype(BF16)
            key_sums.append(key_sum)
            value_sums.append(value_sum)
        for sums, place in ((key_sums, lanes), (value_sums, value_lanes)):
            over = 2 * HALO
            extended_grad[:BLOCK, place] = sums[0][:BLOCK]
            extended_grad[BLOCK : BLOCK + over, place] = sums[0][BLOCK:] + sums[1][:over]
            extended_grad[BLOCK + over :, place] = sums[1][over:]
        return carry

    lax.fori_loop(0, features // LANES, pair, 0)
    rim_before[...] = extended_grad[:HALO, :].astype(BF16)
    own_grad[...] = extended_grad[HALO : HALO + tokens, :]
    rim_after[...] = extended_grad[HALO + tokens :, :].astype(BF16)


def run_attend_back(offs, middle_grad, qkv, before, after, seg_q, seg_k, cosine, sine, pieces):
    tokens, features = middle_grad.shape
    rim = struct((HALO, 2 * features), BF16)
    return call(
        attend_back_kernel,
        (struct((tokens, features), BF16), struct((tokens, 2 * features), F32), rim, rim),
        [
            pltpu.VMEM((tokens + 2 * HALO, 2 * features), BF16),
            pltpu.VMEM((tokens, features), BF16),
            pltpu.VMEM((tokens + 2 * HALO, 2 * features), F32),
        ],
        grid=(1,),
        in_specs=[pl.BlockSpec(memory_space=pltpu.SMEM)]
        + [
            whole_spec(v.shape)
            for v in (middle_grad, qkv, before, after, seg_q, seg_k, cosine, sine)
        ]
        + proj_specs(pieces[0].shape[0], features),
        out_specs=(
            whole_spec((tokens, features)),
            whole_spec((tokens, 2 * features)),
            whole_spec((HALO, 2 * features)),
            whole_spec((HALO, 2 * features)),
        ),
    )(offs, middle_grad, qkv, before, after, seg_q, seg_k, cosine, sine, *pieces)


def qkv_back_kernel(
    offs, query_grad, own_grad, arrived_first, arrived_last, cosine, sine, x, gain, middle_grad,
    p0, p1, p2, p3, right, upstream, upstream_b, gain_grad, sums, ordered,
):
    step = pl.program_id(0)
    tokens, features = x.shape
    for part in range(3):

        @pl.when(step == part)
        def _():
            if part == 0:
                joint = query_grad[...]
            else:
                chunks = []
                for k in range(features // LANES):
                    at = (part - 1) * features + k * LANES
                    there = slice(at, at + LANES)
                    rows = [
                        own_grad[:HALO, there] + arrived_first[:, there].astype(F32),
                        own_grad[HALO : tokens - HALO, there],
                        own_grad[tokens - HALO :, there] + arrived_last[:, there].astype(F32),
                    ]
                    grads = jnp.concatenate(rows, axis=0)
                    if part == 1:
                        grads = turn_chunk(grads, cosine[...], sine[...], -1)
                    chunks.append(grads.astype(BF16))
                joint = jnp.concatenate(chunks, axis=1)
            store(right, part * features, joint)
            product = lax.dot_general(
                joint, joined((p0, p1, p2, p3)), NT, preferred_element_type=F32
            )
            sums[...] = product if part == 0 else sums[...] + product

    @pl.when(step == 2)
    def _():
        from_pieces(offs, sums, ordered)
        pulled, gains = norm_pull(x[...], gain[...], ordered[...])
        result = middle_grad[...] + pulled
        upstream[...] = result
        upstream_b[...] = result.astype(BF16)
        gain_grad[...] = gains


def run_qkv_back(
    offs, query_grad, own_grad, arrived_first, arrived_last, cosine, sine, x, gain, middle_grad, pieces
):
    tokens, features = x.shape
    whole = (query_grad, own_grad, arrived_first, arrived_last, cosine, sine, x, gain, middle_grad)
    outs = (
        struct((tokens, 3 * features), BF16),
        struct((tokens, features), F32),
        struct((tokens, features), BF16),
        struct((1, features), F32),
    )
    return call(
        qkv_back_kernel,
        outs,
        [pltpu.VMEM((tokens, features), F32), pltpu.VMEM((tokens, features), F32)],
        grid=(3,),
        in_specs=[pl.BlockSpec(memory_space=pltpu.SMEM)]
        + [whole_spec(v.shape) for v in whole]
        + piece_specs(pieces[0].shape[0], features),
        out_specs=tuple(whole_spec(out.shape) for out in outs),
    )(offs, *whole, *pieces)


def pick_kernel(which, *refs):
    pickers, lefts, (mine, theirs) = refs[:2], refs[2:-2], refs[-2:]
    half = pickers[0].shape[0] // 2
    for k, (picker, left) in enumerate(which):
        rows = lax.dot_general(
            pickers[picker][...], lefts[left][...], NT, preferred_element_type=F32
        ).astype(BF16)
        mine[k * half : (k + 1) * half, :] = rows[:half]
        theirs[k * half : (k + 1) * half, :] = rows[half:]


def run_pick(pickers, lefts, which):
    rows = len(which) * pickers[0].shape[0] // 2
    out = struct((rows, lefts[0].shape[0]), BF16)
    return call(functools.partial(pick_kernel, which), (out, out), smem=0)(*pickers, *lefts)


def exchange_kernel(plan, *refs):
    segments, stages = plan
    refs = list(refs)
    take = lambda count: [refs.pop(0) for _ in range(count)]
    adding, ending, far_ending, finishing = stages
    if segments:
        rights, rights_far = take(2), take(2)
        lefts = [take(2) for _ in segments]
    kept = take(2) if adding else None
    last = take(2) if ending else None
    come = take(2) if adding or ending else None
    near_pair = take(2) if far_ending else None
    far_pair = take(2) if finishing else None
    keep = take(2) if segments else None
    stay = take(2) if adding else None
    send = take(2) if segments or adding else None
    near_out = take(2) if ending else None
    far_out = take(2) if far_ending else None
    result = take(1)[0] if finishing else None

    def added(pair, rows, columns):
        return pair[0][rows, columns].astype(F32) + pair[1][rows, columns].astype(F32)

    def body(step):
        everything = slice(None)
        top = 0
        if segments:
            half, tile = keep[0].shape
            for (path, start, stop), (left, left_far) in zip(segments, lefts):
                low, high = max(start - step * tile, 0), min(stop - step * tile, tile)
                if low >= high:
                    continue
                columns = slice(low, high)
                total = jnp.dot(
                    jnp.concatenate([left[...], left_far[...]], axis=1),
                    jnp.concatenate(
                        [rights[path][:, columns], rights_far[path][:, columns]], axis=0
                    ),
                    preferred_element_type=F32,
                ).astype(BF16)
                keep[path][:, columns] = total[:half]
                send[path][:half, columns] = total[half:]
            top = half
        came = 0
        if adding:
            rows, tile = kept[0].shape
            half = rows // 2
            for path in range(2):
                total = kept[path][...].astype(F32) + come[path][:rows, :].astype(F32)
                stay[path][...] = total[:half].astype(BF16)
                send[1 - path][top : top + half, :] = total[half:].astype(BF16)
            came = rows
        if ending:
            rows, tile = last[0].shape
            half = rows // 2
            for path in range(2):
                at = (path * TILES + step) * tile
                total = last[path][...].astype(F32) + come[1 - path][
                    came : came + rows, :
                ].astype(F32)
                near_out[0][:, at : at + tile] = total[:half].astype(BF16)
                near_out[1][:, at : at + tile] = total[half:].astype(BF16)
        if step == 0 and far_ending:
            half = near_pair[0].shape[0] // 2
            far_out[0][...] = added(near_pair, slice(0, half), everything).astype(BF16)
            far_out[1][...] = added(near_pair, slice(half, 2 * half), everything).astype(BF16)
        if step == 0 and finishing:
            result[...] = added(far_pair, everything, everything).astype(result.dtype)

    for step in range(TILES):
        pl.when(pl.program_id(0) == step)(functools.partial(body, step))


class Exchange:
    def __init__(self, flow, rows, width, bits):
        self.flow = flow
        self.rows = rows
        self.width = width
        self.near, self.far = bits[:2]
        self.dtype = F32 if len(bits) == 2 else BF16
        self.kept = self.last = self.come = self.near_pair = self.far_pair = None

    def busy(self):
        return any((self.kept, self.last, self.near_pair, self.far_pair))

    def step(self, rights=None, segments=(), after=()):
        flow, rows, width = self.flow, self.rows, self.width
        tile = width // TILES
        args, specs, outs, out_specs = [], [], [], []

        def tiled(shape):
            return pl.BlockSpec((shape[0], tile), lambda j: (0, j))

        def give(pair, spec):
            if pair:
                args.extend(pair)
                specs.extend(spec(value.shape) for value in pair)

        def want(height, columns, spec, count=2, dtype=BF16):
            outs.extend([struct((height, columns), dtype)] * count)
            out_specs.extend([spec((height, columns))] * count)

        for right in rights or ():
            args += [right, right]
            block = (right.shape[0], tile)
            specs += [pl.BlockSpec(block, lambda j: (0, j))]
            specs += [pl.BlockSpec(block, lambda j: (0, TILES + j))]
        for _, _, _, left, place in segments:
            args += left
            specs += [pl.BlockSpec((rows, left[0].shape[1]), lambda j, at=place: (at, 0))] * 2
        give(self.kept, tiled)
        give(self.last, tiled)
        give(self.come if self.kept or self.last else None, tiled)
        give(self.near_pair, whole_spec)
        give(self.far_pair, whole_spec)
        height = 0
        if segments:
            want(rows // 2, width, tiled)
            height += rows // 2
        if self.kept:
            want(rows // 4, width, tiled)
            height += rows // 4
        if height:
            want(height, width, tiled)
        if self.last:
            want(rows // 8, 2 * width, whole_spec)
        if self.near_pair:
            want(rows // 16, 2 * width, whole_spec)
        if self.far_pair:
            want(rows // 16, 2 * width, whole_spec, 1, self.dtype)
        stages = tuple(map(bool, (self.kept, self.last, self.near_pair, self.far_pair)))
        plan = (
            tuple((path, start - path * width, stop - path * width) for path, start, stop, _, _ in segments),
            stages,
        )
        args[0] = flow.tie(args[0])
        results = list(
            call(
                functools.partial(exchange_kernel, plan),
                tuple(outs),
                grid=(TILES,),
                in_specs=specs,
                out_specs=tuple(out_specs),
            )(*args)
        )

        def got(wanted):
            return [results.pop(0), results.pop(0)] if wanted else None

        keep, stay, send = got(segments), got(self.kept), got(height)
        near, far = got(self.last), got(self.near_pair)
        result = results.pop(0) if self.far_pair else None
        self.kept, self.last = keep, stay
        self.come = send and [flow.swap(value, 1 + path) for path, value in enumerate(send)]
        if near:
            near[1] = lax.optimization_barrier((near[1],) + after)[0]
        self.near_pair = near and [near[0], flow.swap(near[1], self.near)]
        self.far_pair = far and [far[0], flow.swap(far[1], self.far)]
        return result


class Ending:
    def __init__(self, flow, value, bits, deliver):
        self.flow = flow
        self.bits = list(bits)
        self.deliver = deliver
        self.keep = value
        self.come = None

    def step(self):
        if self.come is not None:
            self.keep = self.keep.astype(F32) + self.flow.tie(self.come).astype(F32)
        if not self.bits:
            self.deliver(self.keep)
            return False
        half = self.keep.shape[0] // 2
        send = self.keep[half:].astype(BF16)
        self.keep = self.keep[:half].astype(BF16)
        self.come = self.flow.swap(send, self.bits.pop(0))
        return True


def rope_tables(position):
    inverse = jnp.power(THETA, -jnp.arange(0, HEAD_DIM, 2, dtype=F32) / HEAD_DIM)
    angles = position[:, None] * inverse[None, :]
    cosine, sine = jnp.cos(angles), jnp.sin(angles)
    return (
        jnp.concatenate([cosine, cosine, cosine, cosine], axis=-1),
        jnp.concatenate([-sine, sine, -sine, sine], axis=-1),
    )


def layout(positions, lengths, total):
    count = lengths.shape[0]
    blocks = (lengths + BLOCK - 1) // BLOCK
    first = (jnp.cumsum(blocks) - blocks) * BLOCK
    owner = jnp.sum((positions[:, None] >= first[None, :]).astype(jnp.int32), axis=1) - 1
    table = owner[:, None] == jnp.arange(count, dtype=jnp.int32)[None, :]
    start = jnp.sum(jnp.where(table, first[None, :], 0), axis=1)
    span = jnp.sum(jnp.where(table, lengths[None, :], 0), axis=1)
    local = positions - start
    inside = (positions >= 0) & (positions < total)
    valid = inside & (local < span)
    segment = jnp.where(inside, jnp.where(valid, owner, owner + count), -1)
    return (segment, local, valid)


def body(
    tokens,
    cotangent,
    lengths,
    block_perm,
    attn_gain,
    qkv_weight,
    proj_weight,
    mlp_gain,
    wide_weight,
    narrow_weight,
):
    flow = Phases()
    seq_index = lax.axis_index("seq")
    seq_count = lax.axis_size("seq")
    levels = seq_count.bit_length() - 1
    tok_dev = tokens.shape[1]
    features = tokens.shape[2]
    block_rows = tok_dev // BLK_DEV
    order_map = block_perm[0]
    target = order_map[0::BLK_DEV] // BLK_DEV
    source = jnp.arange(seq_count, dtype=jnp.int32)

    def holder(bit_level):
        low_mask = (1 << bit_level) - 1
        place = jnp.bitwise_or(
            jnp.bitwise_and(target, low_mask), jnp.bitwise_and(source, ~low_mask)
        )
        return jnp.sum(jnp.where(place == seq_index, source, 0))

    home_index = holder(levels)
    slot_of = lax.dynamic_slice_in_dim(order_map, home_index * BLK_DEV, BLK_DEV) % BLK_DEV
    crossed = slot_of[0] == 1

    def crossing(rows):
        turned = jnp.concatenate([rows[block_rows:], rows[:block_rows]], axis=0)
        return jnp.where(crossed, turned, rows)

    def crossed_over(bit_level, given):
        payload = holder(bit_level + 1 if given else bit_level)
        if not given:
            payload = jnp.sum(jnp.where(source == payload, target, 0))
        flips = jnp.right_shift(jnp.bitwise_xor(seq_index, payload), bit_level)
        return jnp.bitwise_and(flips, 1) == 1

    class Route:
        def __init__(self, rows, given, last=levels):
            self.rows = rows
            self.given = given
            self.levels = list(range(last))
            if given:
                self.levels.reverse()
            self.arrived = None

        def step(self):
            if self.arrived is not None:
                self.rows = jnp.where(
                    crossed_over(self.level, self.given), flow.tie(self.arrived), self.rows
                )
                self.arrived = None
            if self.levels:
                self.level = self.levels.pop(0)
                self.arrived = flow.swap(self.rows, 2 + self.level)
                return True
            return False

        def finish(self):
            while self.step():
                flow.next()
            return self.rows

    total = seq_count * tok_dev
    own_place = seq_index * tok_dev + jnp.arange(tok_dev, dtype=jnp.int32)
    key_place = seq_index * tok_dev - HALO + jnp.arange(tok_dev + 2 * HALO, dtype=jnp.int32)
    seg_query, local_query, valid_query = layout(own_place, lengths[0], total)
    seg_key, _, _ = layout(key_place, lengths[0], total)
    cosine, sine = rope_tables(local_query.astype(F32))
    seg_q_col, seg_q_row = seg_query[:, None], seg_query[None, :]
    seg_k_col, seg_k_row = seg_key[:, None], seg_key[None, :]
    offs = piece_order()
    bits_x, bits_y = stage_bits(True), stage_bits(False)
    picker_x, picker_y = row_picker(features, bits_x), row_picker(features, bits_y)

    gains = jnp.concatenate([attn_gain, mlp_gain], axis=0)
    gains = lax.all_gather(gains, "fsdp", axis=1, tiled=True).astype(F32)
    gains_a = [gains[layer : layer + 1] for layer in range(LAYERS)]
    gains_m = [gains[LAYERS + layer : LAYERS + layer + 1] for layer in range(LAYERS)]

    side = (seq_index % 2).astype(jnp.int32).reshape(1)
    arrays = (proj_weight, wide_weight, narrow_weight)
    items = []
    for layer in range(LAYERS):
        packs = run_pack(side, (qkv_weight,), layer) + run_pack(side, arrays, layer)
        items += [Weights(flow, *pack) for pack in packs]
    per_layer = len(items) // LAYERS
    tok_route, cot_route = Route(tokens[0], False), Route(cotangent[0], False, levels - 1)

    first_use = 3
    owns = {0: (0,), 1: (1, 3), 2: (2,), 4: (4,), 5: (5,), 6: (6,), 8: (7,)}
    phase = 0

    def transfers():
        if phase < len(items):
            items[phase].over_x()
        if 0 <= phase - 1 < len(items):
            items[phase - 1].over_y()
        if 0 <= phase - 2 < len(items):
            items[phase - 2].over_core()
        for place in owns.get(phase, ()):
            items[place].own()

    while phase < first_use or tok_route.levels:
        transfers()
        tok_route.step()
        if phase == 2:
            flow.keep(gains)
        if phase == 0:
            cot_route.step()
            flow.keep(*(item.shard for item in items[1:]))
        phase += 1
        flow.next()
    tok_route.step()
    residual = crossing(tok_route.rows).astype(F32)
    cot_halves = []
    kept = []
    for layer in range(LAYERS):
        base = layer * per_layer
        transfers()
        qkv, normed, edge_first, edge_last = run_qkv(
            offs, flow.tie(residual), gains_a[layer], cosine, sine, items[base].pieces
        )
        flow.keep(normed)
        before = flow.shift(edge_last, True)
        after = flow.shift(edge_first, False)
        phase += 1
        flow.next()
        transfers()
        if layer == 0:
            cot_route.step()
        if layer and kept[-1][-1] is None:
            kept[-1][-1] = (mine, flow.swap(theirs, 0))
        start = residual
        mixed, middle, second = run_attend(
            offs, flow.tie(qkv), before, after, seg_q_col, seg_k_row, residual, gains_m[layer],
            items[base + 1].pieces,
        )
        residual = middle
        hidden = []
        for chunk in range(CHUNKS):
            if chunk:
                phase += 1
                flow.next()
                transfers()
                if layer == 0:
                    if not cot_halves:
                        cot_rows = cot_route.finish()
                        for half in (cot_rows[:block_rows], cot_rows[block_rows:]):
                            cot_halves.append(Route(half, False))
                            cot_halves[-1].levels = [levels - 1]
                    cot_halves[chunk - 1].step()
            residual, gated, slope, gate = run_mlp(
                offs, second, flow.tie(residual), items[base + 1 + chunk].pieces, chunk
            )
            flow.keep(residual, gated)
            hidden.append((gated, slope, gate))
            if chunk == 1:
                lefts = (normed, mixed, second)
                which = ((0, 0), (1, 0), (1, 1), (0, 2), (1, 2))
                mine, theirs = run_pick((picker_x, picker_y), lefts, which)
                flow.keep(theirs)
        picks = None
        if layer == LAYERS - 1:
            flow.next()
            picks = (mine, flow.swap(theirs, 0))
        kept.append([start, qkv, before, after, middle, hidden, picks])
        phase += 1
        flow.next()

    packed_cot = crossing(jnp.concatenate([half.finish() for half in cot_halves], axis=0))
    upstream_b = packed_cot * valid_query[:, None].astype(BF16)
    upstream = upstream_b.astype(F32)

    def both_halves(rows):
        rows = crossing(rows)
        return [Route(rows[:block_rows], True), Route(rows[block_rows:], True)]

    out_routes = both_halves(residual.astype(BF16))

    late = bits_x[2:]
    exchange = Exchange(flow, features // 2, 3 * features // 2, late)
    endings = []
    sums = {}
    count = 0
    width = 3 * features // 2

    def settle(done):
        nonlocal count
        if done is None:
            return
        deliver = functools.partial(sums.__setitem__, count)
        count += 1
        if len(late) > 2:
            endings.append(Ending(flow, done, late[2:], deliver))
        else:
            deliver(done)

    def step_endings():
        for item in list(endings):
            if not item.step():
                endings.remove(item)

    def group(right, parts):
        segments = []
        at = 0
        for columns, lefts in parts:
            for path in range(2):
                low = max(at, path * width)
                high = min(at + columns, (path + 1) * width)
                if low < high:
                    segments.append((path, low, high, lefts[path][:2], lefts[path][2]))
            at += columns
        return list(right), tuple(segments)

    terms = [None] * LAYERS
    made, ready = None, None

    def backward_phase():
        nonlocal made, ready
        flow.next()
        moving = bool(made or ready or exchange.busy())
        now, ready, after = ready, None, ()
        if made:
            right, parts = made
            after = (flow.swap(right, 0),)
            ready = ((right,) + after, parts)
        made = None
        if now or exchange.busy():
            settle(exchange.step(*(group(*now) if now else (None, ())), after))
        step_endings()
        return moving

    for layer in reversed(range(LAYERS)):
        start, qkv, before, after, middle, hidden, picks = kept[layer]
        base = layer * per_layer
        normed_x, normed_y, mixed_y, second_x, second_y = (picks + (row,) for row in range(5))
        carried = None
        upstream_left = None
        for chunk in reversed(range(CHUNKS)):
            if layer < LAYERS - 1 or chunk < CHUNKS - 1:
                backward_phase()
            pieces = items[base + 1 + chunk].pieces
            if upstream_left is None:
                mine, theirs = run_pick(
                    (picker_x, picker_y), (flow.tie(upstream_b),), ((0, 0), (1, 0))
                )
                flow.keep(theirs)
                upstream_left = []
            elif not upstream_left:
                far = flow.swap(theirs, 0)
                upstream_left += [(mine, far, path) for path in range(2)]
            if layer == LAYERS - 1 and chunk == CHUNKS - 1:
                out_routes[0].step()
            elif layer == LAYERS - 2 and chunk == CHUNKS - 1:
                for route in out_routes:
                    route.step()
            args = (offs, flow.tie(upstream_b), hidden[chunk], carried)
            columns = WIDTHS[chunk]
            parts = [
                (columns, upstream_left),
                (2 * columns, (second_x, second_y)),
            ]
            if chunk:
                carried, right = run_mlp_back(*args, pieces, chunk)
                flow.keep(carried)
            else:
                middle_grad, middle_grad_b, mlp_term, right = run_mlp_back_last(
                    *args, upstream, middle, gains_m[layer], pieces, chunk
                )
                parts.append((2 * width - 3 * columns, (None, mixed_y)))
                query_grad, own_grad, rim_before, rim_after = run_attend_back(
                    offs, middle_grad_b, qkv, before, after, seg_q_row, seg_k_col, cosine, sine, pieces
                )
                flow.keep(query_grad, own_grad)
                arrived_first = flow.shift(rim_after, True)
                arrived_last = flow.shift(rim_before, False)
            flow.keep(right)
            made = (right, parts)
        backward_phase()
        right, upstream, upstream_b, attn_term = run_qkv_back(
            offs, flow.tie(query_grad), own_grad, arrived_first, arrived_last, cosine, sine, start,
            gains_a[layer], middle_grad, items[base].pieces,
        )
        if layer:
            out_routes[1].step()
        flow.keep(upstream_b, right)
        made = (right, [(2 * width, (normed_x, normed_y))])
        terms[layer] = (attn_term, mlp_term)
    backward_phase()
    grad_routes = both_halves(flow.tie(upstream_b))
    grad_routes[0].step()
    vectors = [terms[layer][0] for layer in range(LAYERS)]
    vectors += [terms[layer][1] for layer in range(LAYERS)]
    gain_sums = lax.dot_general(
        flow.tie(jnp.concatenate(vectors, axis=0)), picker_x.astype(F32), NT, precision=lax.Precision.HIGHEST
    )
    gain_bits = [0] + list(bits_x)
    while backward_phase() or endings or gain_bits:
        for route in grad_routes:
            route.step()
        if not grad_routes[0].levels:
            for route in out_routes:
                route.step()
        for bit in gain_bits[: 1 if len(gain_bits) > 2 else 2]:
            half = gain_sums.shape[1] // 2
            gain_sums = gain_sums[:, :half] + flow.swap(gain_sums[:, half:], bit)
        gain_bits = gain_bits[1 if len(gain_bits) > 2 else 2 :]
    block_out, token_grad = (
        jnp.concatenate([route.finish() for route in routes], axis=0)
        for routes in (out_routes, grad_routes)
    )

    def pieces_of(layer):
        at = per_layer * (LAYERS - 1 - layer)
        parts = {chunk: sums[at + CHUNKS - 1 - chunk] for chunk in range(CHUNKS)}
        return parts, sums[at + CHUNKS]

    def hidden_sum(parts, role):
        columns = [
            parts[chunk][:, role * WIDTHS[chunk] : (role + 1) * WIDTHS[chunk]]
            for chunk in range(CHUNKS)
        ]
        return jnp.concatenate(columns, axis=1)[:, :FF]

    wide, narrow, proj, qkv_sum = [], [], [], []
    for layer in range(LAYERS):
        parts, attend = pieces_of(layer)
        narrow.append(hidden_sum(parts, 0))
        wide.append(jnp.concatenate([hidden_sum(parts, 1), hidden_sum(parts, 2)], axis=1))
        proj.append(parts[0][:, 3 * WIDTHS[0] : 3 * WIDTHS[0] + features])
        qkv_sum.append(attend)
    return (
        block_out[None],
        token_grad[None],
        gain_sums[:LAYERS],
        jnp.stack(qkv_sum),
        jnp.stack(proj),
        gain_sums[LAYERS:],
        jnp.stack(wide),
        jnp.stack(narrow),
    )


def solution(mesh):
    in_specs = (
        P("fsdp", "seq", None),
        P("fsdp", "seq", None),
        P("fsdp", None),
        P("fsdp", None),
        P(None, "fsdp"),
        P(None, "fsdp", None),
        P(None, "fsdp", None),
        P(None, "fsdp"),
        P(None, "fsdp", None),
        P(None, "fsdp", None),
    )
    out_specs = (
        P("fsdp", "seq", None),
        P("fsdp", "seq", None),
        P(None, ("seq", "fsdp")),
        P(None, ("seq", "fsdp"), None),
        P(None, ("seq", "fsdp"), None),
        P(None, ("seq", "fsdp")),
        P(None, ("seq", "fsdp"), None),
        P(None, ("seq", "fsdp"), None),
    )
    return jax.shard_map(body, mesh=mesh, in_specs=in_specs, out_specs=out_specs, check_vma=False)
```
